128 devices in a mesh: pole: 4 (over x), row: 16 (over z, y), col: 2 (over core).
Axes of the slice: x: 4, y: 4, z: 4, core: 2. Of those that a mesh axis runs over, the one named last changes fastest.
Arguments:
- lower_factor: bfloat16 [4, 10, 2, 512, 512], P('pole', None, None, 'row', 'col'), may hold values from -0.125 to 0.125
- upper_factor: bfloat16 [4, 10, 2, 512, 512], P('pole', None, None, 'row', 'col'), may hold values from -0.125 to 0.125
- diag_inverse: bfloat16 [4, 7, 2, 512, 512], P('pole', None, None, 'row', 'col'), may hold values from -6 to 6
- residues: float32 [4, 2], P('pole'), may hold values from -4 to 4
- widths: int32 [7], replicated, may hold values from 192 to 512, as said below
- pattern: int32 [10], replicated, may hold values 0 or 1
Outputs:
- density: float32 [27, 512, 512], P(None, 'row', 'col')
The draws below stay inside these ranges and needn't reach their ends.
Inputs may be any that keep to these rules, and one draw needn't show every extreme that they name: `widths`: some supernode has exactly 512 columns.
All inputs are finite; a program needn't handle non-finite values.
Results may differ from the reference program's by a relative error of at most 0.014.
Values may be sent and summed in bfloat16 or wider, within the bound.
No kernel may reach another device: no remote copies, remote signals or barrier semaphores. Data moves between devices by JAX's collectives and lax.ppermute only.
A program may use at most 64 MiB of HBM per device.

```python
import jax
import jax.numpy as jnp
from jax import lax

B = 512
NS = 7
NL = 10
POLES = 4


def draw_widths(key, part):
    key = jax.random.fold_in(key, 5)
    value_key, pick_key = jax.random.split(key)
    values = jax.random.randint(value_key, (NS,), 3 * B // 8, B + 1)
    chosen = jax.random.randint(pick_key, (), 0, NS)
    return jnp.where(jnp.arange(NS) == chosen, B, values).astype(jnp.int32)


def with_ends(result, own_key, least, high):
    longest = result.shape.index(max(result.shape))
    spots = []
    for shift in (0, 1):
        where = [jax.random.randint(jax.random.fold_in(own_key, axis), (), 0, length) for axis, length in enumerate(result.shape)]
        where[longest] = (where[longest] + shift) % result.shape[longest]
        spots.append(tuple(where))
    return result.at[spots[0]].set(least).at[spots[1]].set(high)


def steps_of(rng, dims, cuts, least, largest):
    loudness, own = 1.0, jax.random.fold_in(rng, 6)
    for position, parts in cuts:
        draws = jnp.exp(jax.random.uniform(jax.random.fold_in(own, position), (parts,), jnp.float32, least / len(cuts), largest / len(cuts)))
        loudness = loudness * jnp.repeat(draws, dims[position] // parts).reshape([-1 if axis == position else 1 for axis in range(len(dims))])
    return loudness


def gaussian(own_key, shape, spread, most, shards=(), held_as=jnp.bfloat16):
    loudness = steps_of(own_key, shape, shards, -0.22, 0.18) if shards else 1.0
    drawn = jax.random.normal(own_key, shape, jnp.float32) * spread * loudness
    return jnp.minimum(jnp.maximum(drawn, -most), most).astype(held_as)


def setup_inputs(seed: int = 0) -> dict:
    seeds = jax.random.split(jax.random.key(seed), 7)
    lower_factor = gaussian(seeds[0], (POLES, NL, 2, B, B), (4 * B) ** -0.5, 0.125, ((0, 4), (3, 16), (4, 2)))
    upper_factor = gaussian(seeds[1], (POLES, NL, 2, B, B), (4 * B) ** -0.5, 0.125, ((0, 4), (3, 16), (4, 2)))
    diag_inverse = gaussian(seeds[2], (POLES, NS, 2, B, B), 1.0, 6.0, ((0, 4), (3, 16), (4, 2)))
    residues = gaussian(seeds[3], (POLES, 2), 1.0, 4.0, ((0, 4),), jnp.float32)
    widths = draw_widths(jax.random.fold_in(seeds[6], 71), 0)
    pattern = with_ends((jax.random.randint(seeds[5], (NL,), 0, 4) < 3).astype(jnp.int32), jax.random.fold_in(seeds[5], 1), 0, 1)
    return {"lower_factor": lower_factor, "upper_factor": upper_factor, "diag_inverse": diag_inverse, "residues": residues, "widths": widths, "pattern": pattern}


def ancestors(member):
    chain_list = []
    current = member
    while current > 0:
        current = (current - 1) // 2
        chain_list.append(current)
    return chain_list


def pair_table(count):
    table = {}
    for member in range(1, count):
        for above in ancestors(member):
            table[(member, above)] = len(table)
    return table


def complex_sum(lefts, rights):
    real_part = jnp.zeros((B, B), jnp.float32)
    imag_part = jnp.zeros((B, B), jnp.float32)
    for left, right in zip(lefts, rights):
        real_part = real_part + jnp.dot(left[0], right[0], preferred_element_type=jnp.float32) - jnp.dot(left[1], right[1], preferred_element_type=jnp.float32)
        imag_part = imag_part + jnp.dot(left[0], right[1], preferred_element_type=jnp.float32) + jnp.dot(left[1], right[0], preferred_element_type=jnp.float32)
    return jnp.stack([real_part, imag_part])


def invert_pole(lower, upper, dinv, keep, pattern):
    table = pair_table(NS)
    pattern_mask = pattern.astype(jnp.bfloat16)

    def lhat(member, above):
        index = table[(member, above)]
        return lower[index] * (pattern_mask[index] * keep[above][:, None] * keep[member][None, :])

    def uhat(member, above):
        index = table[(member, above)]
        return upper[index] * (pattern_mask[index] * keep[member][:, None] * keep[above][None, :])

    def dhat(member):
        return dinv[member] * (keep[member][:, None] * keep[member][None, :])

    blocks = {(0, 0): dhat(0)}
    for member in range(1, NS):
        chain_list = ancestors(member)
        lower_list = [lhat(member, above) for above in chain_list]
        upper_list = [uhat(member, above) for above in chain_list]
        for first in chain_list:
            blocks[(first, member)] = (-complex_sum([blocks[(first, second)] for second in chain_list], lower_list)).astype(jnp.bfloat16)
        for first in chain_list:
            blocks[(member, first)] = (-complex_sum(upper_list, [blocks[(second, first)] for second in chain_list])).astype(jnp.bfloat16)
        blocks[(member, member)] = (dhat(member).astype(jnp.float32) - complex_sum(upper_list, [blocks[(second, member)] for second in chain_list])).astype(jnp.bfloat16)
    ordered = [blocks[(member, member)] for member in range(NS)]
    ordered = ordered + [blocks[(pair[1], pair[0])] for pair in table]
    ordered = ordered + [blocks[(pair[0], pair[1])] for pair in table]
    return ordered


def reference(lower_factor, upper_factor, diag_inverse, residues, widths, pattern):
    keep = (jnp.arange(B).astype(jnp.int32)[None, :] < widths[:, None]).astype(jnp.bfloat16)

    def step(total, items):
        lower, upper, dinv, residue = items
        ordered = invert_pole(lower, upper, dinv, keep, pattern)
        term = jnp.stack([residue[0] * block[0].astype(jnp.float32) - residue[1] * block[1].astype(jnp.float32) for block in ordered])
        return total + term, None

    start_total = jnp.zeros((NS + 2 * NL, B, B), jnp.float32)
    total, unused = lax.scan(step, start_total, (lower_factor, upper_factor, diag_inverse, residues))
    return total
```

```python
import jax
import jax.numpy as jnp
from jax import lax
from jax.experimental import pallas as pl
from jax.experimental.pallas import tpu as pltpu
from jax.sharding import PartitionSpec as P

BF = jnp.bfloat16
F32 = jnp.float32
VMEM_LIMIT = 48 * 1024 * 1024


def ring_y(step):
    return [(z * 4 + y, z * 4 + (y + step) % 4) for z in range(4) for y in range(4)]


def ring_z(step):
    return [(z * 4 + y, ((z + step) % 4) * 4 + y) for z in range(4) for y in range(4)]


def ring_x(step):
    return [(x, (x + step) % 4) for x in range(4)]


SWAP = [(0, 1), (1, 0)]


def place():
    row = lax.axis_index("row")
    return lax.axis_index("pole"), lax.div(row, 4), lax.rem(row, 4), lax.axis_index("col")


def node_of(y):
    return 3 + 2 * lax.rem(y, 2) + lax.div(y, 2)


def vm():
    return pl.BlockSpec(memory_space=pltpu.VMEM)


def sm():
    return pl.BlockSpec(memory_space=pltpu.SMEM)


def hbm():
    return pl.BlockSpec(memory_space=pl.ANY)


def call(kernel, outs, in_specs, out_specs, scratch=(), flops=0, nbytes=0):
    return pl.pallas_call(
        kernel,
        out_shape=outs,
        in_specs=in_specs,
        out_specs=out_specs,
        scratch_shapes=list(scratch),
        compiler_params=pltpu.CompilerParams(vmem_limit_bytes=VMEM_LIMIT),
        cost_estimate=pl.CostEstimate(flops=flops, bytes_accessed=nbytes, transcendentals=0),
    )


def shape(*dims, dtype=BF):
    return jax.ShapeDtypeStruct(dims, dtype)


def pack_kernel(low, up, dia, widths, pattern, zbuf, y0, y1, y2, y3):
    x, z, y, c = place()
    rows = (32 * (4 * z + y)) + lax.broadcasted_iota(jnp.int32, (32, 256), 0)
    cols = (256 * c) + lax.broadcasted_iota(jnp.int32, (32, 256), 1)

    def masked(tile, row_node, col_node, on):
        keep = (rows < widths[row_node]) & (cols < widths[col_node]) & (on != 0)
        return jnp.where(keep[None], tile.astype(F32), 0.0).astype(BF)

    zbuf[0] = masked(dia[0], 0, 0, 1)
    for i in range(2):
        zbuf[1 + 2 * i] = masked(up[i], 1 + i, 0, pattern[i])
        zbuf[2 + 2 * i] = masked(low[i], 0, 1 + i, pattern[i])
    for d, out in enumerate((y0, y1, y2, y3)):
        k = node_of(lax.rem(y + d, 4))
        p = lax.div(k - 1, 2)
        at = 2 * (k - 3) + 2
        out[0] = masked(dia[p], p, p, 1)
        out[1] = masked(low[at], p, k, pattern[at])
        out[2] = masked(low[at + 1], 0, k, pattern[at + 1])
        out[3] = masked(up[at], k, p, pattern[at])
        out[4] = masked(up[at + 1], k, 0, pattern[at + 1])
        out[5] = masked(dia[k], k, k, 1)


def merge_z_kernel(b0, b1, b2, b3, own, other, sems):
    x, z, y, c = place()
    p = lax.rem(y, 2)
    copies = []
    for d, buf in enumerate((b0, b1, b2, b3)):
        at = lax.rem(z + 4 - d, 4)
        copies.append((buf.at[0], own.at[0, :, at]))
        copies.append((buf.at[0], other.at[0, :, at]))
        copies.append((buf.at[pl.ds(1 + 2 * p, 2)], own.at[pl.ds(1, 2), :, at]))
        copies.append((buf.at[pl.ds(3 - 2 * p, 2)], other.at[pl.ds(1, 2), :, at]))
    run_copies(copies, sems)


def run_copies(copies, sems):
    made = [pltpu.make_async_copy(s, t, sems.at[i]) for i, (s, t) in enumerate(copies)]
    for m in made:
        m.start()
    for m in made:
        m.wait()


def merge_y_kernel(b0, b1, b2, b3, zb, uk, dk, sems):
    x, z, y, c = place()
    copies = []
    for d, buf in enumerate((b0, b1, b2, b3)):
        at = lax.rem(y + 4 - d, 4)
        copies.append((buf.at[pl.ds(0, 3)], zb.at[:, :, at]))
        copies.append((buf.at[pl.ds(3, 2)], uk.at[:, :, at]))
        copies.append((buf.at[5], dk.at[:, at]))
    run_copies(copies, sems)


def left_of(pairs):
    real = [jnp.concatenate([r, -i], axis=1) for r, i in pairs]
    imag = [jnp.concatenate([i, r], axis=1) for r, i in pairs]
    return jnp.concatenate(real + imag, axis=0)


def dot(a, b):
    return jnp.dot(a, b, preferred_element_type=F32)


def pairs_of(res, count):
    half = 128 * count
    return [
        (res[128 * i : 128 * i + 128], res[half + 128 * i : half + 128 * i + 128])
        for i in range(count)
    ]


def first_kernel(
    o0, o1, o2, o3, s0, s1, s2, s3, z0, z1, z2, z3, uko, uks, res,
    edge, wide, dens, right, zright, ukf, sems,
):
    x, z, y, c = place()
    copies = []
    for d, (mine, swapped) in enumerate(((o0, s0), (o1, s1), (o2, s2), (o3, s3))):
        at = lax.rem(y + 4 - d, 4)
        copies.append((mine, right.at[c, :, :, :, at]))
        copies.append((swapped, right.at[1 - c, :, :, :, at]))
    for d, buf in enumerate((z0, z1, z2, z3)):
        at = lax.rem(z + 4 - d, 4)
        copies.append((buf.at[pl.ds(0, 1)], zright.at[:, :, at]))
    copies.append((uko, ukf.at[c]))
    copies.append((uks, ukf.at[1 - c]))
    run_copies(copies, sems)

    def operand(half, block):
        return right[half, block].reshape(1024, 256)

    def wide_rows(get):
        return tuple(jnp.concatenate([get(0, part), get(1, part)], axis=1) for part in range(2))

    ukp = wide_rows(lambda h, part: ukf[h, 0, part].reshape(128, 256))
    d0r = wide_rows(lambda h, part: right[h, 0, part, z].reshape(128, 256))
    upr = wide_rows(lambda h, part: right[h, 1, part, z].reshape(128, 256))
    ukp_left = left_of([ukp])
    halves = []
    for h in range(2):
        ((re, im),) = pairs_of(dot(ukp_left, operand(h, 1)), 1)
        halves.append(
            (
                (ukf[h, 1, 0].reshape(128, 256).astype(F32) - re).astype(BF),
                (ukf[h, 1, 1].reshape(128, 256).astype(F32) - im).astype(BF),
            )
        )
    v = tuple(jnp.concatenate([halves[0][i], halves[1][i]], axis=1) for i in range(2))
    left = left_of([v, upr])
    outs = []
    for h in range(2):
        got = pairs_of((-dot(left, operand(h, 0))).astype(BF), 2)
        outs.append(got)
    xk0 = tuple(jnp.concatenate([outs[0][0][i], outs[1][0][i]], axis=1) for i in range(2))
    xp0 = tuple(jnp.concatenate([outs[0][1][i], outs[1][1][i]], axis=1) for i in range(2))
    for i in range(2):
        wide[0, i] = xp0[i]
        wide[1, i] = d0r[i]
        wide[2, i] = xk0[i]
    kl, pl_, dl = pairs_of(dot(left_of([xk0, xp0, d0r]), right[c, 2].reshape(1024, 256)), 3)
    (kd,) = pairs_of(dot(ukp_left, zright[0].reshape(1024, 256)), 1)
    xkp = [-(kd[i] + kl[i]) for i in range(2)]
    xpp = [zright[0, i, z].reshape(128, 256).astype(F32) - pl_[i] for i in range(2)]
    x0p = [-dl[i] for i in range(2)]
    for i in range(2):
        edge[0, i] = xpp[i].astype(BF)
        edge[1, i] = x0p[i].astype(BF)
        edge[2, i] = xkp[i].astype(BF)
    wr, wi = res[0, 0], res[0, 1]

    def density(re, im):
        return wr * re.astype(F32) - wi * im.astype(F32)

    def half_of(block, part):
        return wide[block, part, :, pl.ds(pl.multiple_of(c * 256, 256), 256)]

    dens[0] = density(*xkp)
    dens[1] = density(half_of(2, 0), half_of(2, 1))
    a = density(*xpp)
    b = density(half_of(0, 0), half_of(0, 1))
    e = density(*x0p)
    f = density(half_of(1, 0), half_of(1, 1))
    dens[2] = jnp.where(y < 2, a, b)
    dens[3] = jnp.where(y < 2, f, e)


def second_kernel(
    edge_o, edge_s, wide, dens, z0, z1, z2, z3, dk, res,
    slot0, slot1, slot2, slot3, zright, slots, sems,
):
    x, z, y, c = place()
    copies = []
    for d, buf in enumerate((z0, z1, z2, z3)):
        at = lax.rem(z + 4 - d, 4)
        copies.append((buf.at[pl.ds(1, 2)], zright.at[:, :, at]))
    run_copies(copies, sems)

    first = c == 0

    def full(block):
        out = []
        for i in range(2):
            a, b = edge_o[block, i], edge_s[block, i]
            out.append(
                jnp.concatenate([jnp.where(first, a, b), jnp.where(first, b, a)], axis=1)
            )
        return tuple(out)

    left_p = left_of([full(0), full(1), full(2)])
    left_0 = left_of([(wide[i, 0], wide[i, 1]) for i in range(3)])
    total = dot(left_p, zright[0].reshape(1024, 256)) + dot(left_0, zright[1].reshape(1024, 256))
    pk, ok, kk = pairs_of(total, 3)
    wr, wi = res[0, 0], res[0, 1]
    parts = [
        wr * (dk[0].reshape(128, 256).astype(F32) - kk[0])
        - wi * (dk[1].reshape(128, 256).astype(F32) - kk[1]),
        wi * pk[1] - wr * pk[0],
        wi * ok[1] - wr * ok[0],
    ] + [dens[i] for i in range(4)]
    for s in range(4):
        for t in range(4):
            for b, part in enumerate(parts):
                lo = 32 * t + 8 * s
                slots[s, t, 8 * b : 8 * b + 8] = part[lo : lo + 8]
    for d, out in enumerate((slot0, slot1, slot2, slot3)):
        out[...] = slots[lax.rem(x + d, 4)].astype(BF)


def sum_kernel(a0, a1, a2, a3, t0, t1, t2, t3, acc):
    x, z, y, c = place()
    acc[...] = (
        a0[...].astype(F32) + a1[...].astype(F32) + a2[...].astype(F32) + a3[...].astype(F32)
    )
    for d, out in enumerate((t0, t1, t2, t3)):
        out[...] = acc[lax.rem(y + d, 4)].astype(BF)


def gather_kernel(t0, t1, t2, t3, out):
    x, z, y, c = place()
    for d, t in enumerate((t0, t1, t2, t3)):
        out[lax.rem(y + 4 - d, 4)] = t[...]


NODE = (3, 5, 4, 6)


def out_index(y):
    k = NODE[y]
    p = 1 + y % 2
    pair = 2 * (k - 3) + 2
    first = [k, 7 + pair, 7 + pair + 1, 17 + pair, 17 + pair + 1]
    if y < 2:
        return first + [p, 0 if y == 0 else None]
    return first + [17 + p - 1, 7 + p - 1]


def final_kernel(g0, g1, g2, g3, out):
    x, z, y, c = place()
    for d, g in enumerate((g0, g1, g2, g3)):
        at = pl.multiple_of(8 * lax.rem(x + 4 - d, 4), 8)
        for s in range(4):
            rows = g[s].astype(F32)
            for b, index in enumerate(out_index(s)):
                if index is not None:
                    out[index, pl.ds(at, 8), :] = rows[8 * b : 8 * b + 8]


def body(lower_factor, upper_factor, diag_inverse, residues, widths, pattern):
    lower, upper, diag = lower_factor[0], upper_factor[0], diag_inverse[0]
    tile = (2, 32, 256)
    zbuf, *ybuf = call(
        pack_kernel,
        [shape(5, *tile)] + [shape(6, *tile)] * 4,
        [vm(), vm(), vm(), sm(), sm()],
        [vm()] * 5,
        nbytes=2 << 20,
    )(lower, upper, diag, widths, pattern)
    y_in = [ybuf[0]] + [lax.ppermute(ybuf[d], "row", ring_y(d)) for d in (1, 2, 3)]
    z_in = [zbuf] + [lax.ppermute(zbuf, "row", ring_z(d)) for d in (1, 2, 3)]
    zb, uk, dk = call(
        merge_y_kernel,
        [shape(3, 2, 4, 32, 256), shape(2, 2, 4, 32, 256), shape(2, 4, 32, 256)],
        [hbm()] * 4,
        [hbm()] * 3,
        [pltpu.SemaphoreType.DMA((12,))],
        nbytes=2 << 20,
    )(*y_in)
    own, other = call(
        merge_z_kernel,
        [shape(3, 2, 4, 32, 256)] * 2,
        [hbm()] * 4,
        [hbm()] * 2,
        [pltpu.SemaphoreType.DMA((16,))],
        nbytes=2 << 20,
    )(*z_in)
    zz = [zb] + [lax.ppermute(zb, "row", ring_z(d)) for d in (1, 2, 3)]
    yy = [own] + [lax.ppermute(own if d == 2 else other, "row", ring_y(d)) for d in (1, 2, 3)]
    uks = lax.ppermute(uk, "col", SWAP)
    ss = [lax.ppermute(a, "col", SWAP) for a in yy]
    edge, wide, dens = call(
        first_kernel,
        [shape(3, 2, 128, 256), shape(3, 2, 128, 512), shape(4, 128, 256, dtype=F32)],
        [hbm()] * 14 + [sm()],
        [vm()] * 3,
        [
            pltpu.VMEM((2, 3, 2, 4, 4, 32, 256), BF),
            pltpu.VMEM((1, 2, 4, 4, 32, 256), BF),
            pltpu.VMEM((2, 2, 2, 4, 32, 256), BF),
            pltpu.SemaphoreType.DMA((14,)),
        ],
        flops=1342177280,
        nbytes=4 << 20,
    )(*yy, *ss, *zz, uk, uks, residues)
    edge_s = lax.ppermute(edge, "col", SWAP)
    slots = call(
        second_kernel,
        [shape(4, 56, 256)] * 4,
        [vm()] * 4 + [hbm()] * 4 + [vm(), sm()],
        [vm()] * 4,
        [
            pltpu.VMEM((2, 2, 4, 4, 32, 256), BF),
            pltpu.VMEM((4, 4, 56, 256), F32),
            pltpu.SemaphoreType.DMA((4,)),
        ],
        flops=805306368,
        nbytes=4 << 20,
    )(edge, edge_s, wide, dens, *zz, dk, residues)
    at_x = [slots[0]] + [lax.ppermute(slots[d], "pole", ring_x(d)) for d in (1, 2, 3)]
    sums = call(
        sum_kernel,
        [shape(56, 256)] * 4,
        [vm()] * 4,
        [vm()] * 4,
        [pltpu.VMEM((4, 56, 256), F32)],
        nbytes=1 << 20,
    )(*at_x)
    at_y = [sums[0]] + [lax.ppermute(sums[d], "row", ring_y(d)) for d in (1, 2, 3)]
    mine = call(
        gather_kernel, [shape(4, 56, 256)], [vm()] * 4, [vm()], nbytes=1 << 18
    )(*at_y)[0]
    full = [mine] + [lax.ppermute(mine, "pole", ring_x(d)) for d in (1, 2, 3)]
    return call(
        final_kernel, [shape(27, 32, 256, dtype=F32)], [vm()] * 4, [vm()], nbytes=2 << 20
    )(*full)[0]


def solution(mesh):
    return jax.shard_map(
        body,
        mesh=mesh,
        in_specs=(
            P("pole", None, None, "row", "col"),
            P("pole", None, None, "row", "col"),
            P("pole", None, None, "row", "col"),
            P("pole", None),
            P(),
            P(),
        ),
        out_specs=P(None, "row", "col"),
        check_vma=False,
    )
```

```python
import jax
import jax.numpy as jnp
from jax import lax
from jax.experimental import pallas as pl
from jax.experimental.pallas import tpu as pltpu
from jax.sharding import PartitionSpec as P

BF = jnp.bfloat16
F32 = jnp.float32
VMEM_LIMIT = 24 * 1024 * 1024


def ring_both(step):
    pairs = []
    for z in range(4):
        for y in range(4):
            here = (z * 4 + y) * 2
            pairs.append((here, (z * 4 + (y + step) % 4) * 2))
            pairs.append((here + 1, (((z + step) % 4) * 4 + y) * 2 + 1))
    return pairs


def ring_other(step):
    pairs = []
    for z in range(4):
        for y in range(4):
            here = (z * 4 + y) * 2
            pairs.append((here, (((z + step) % 4) * 4 + y) * 2))
            pairs.append((here + 1, (z * 4 + (y + step) % 4) * 2 + 1))
    return pairs


def ring_x(step):
    return [(x, (x + step) % 4) for x in range(4)]


SWAP = [(0, 1), (1, 0)]


def place():
    row = lax.axis_index("row")
    return lax.axis_index("pole"), lax.div(row, 4), lax.rem(row, 4), lax.axis_index("col")


def node_of(y):
    return 3 + 2 * lax.rem(y, 2) + lax.div(y, 2)


def vm():
    return pl.BlockSpec(memory_space=pltpu.VMEM)


def sm():
    return pl.BlockSpec(memory_space=pltpu.SMEM)


def far():
    return pl.BlockSpec(memory_space=pltpu.HBM)


def hbm():
    return pl.BlockSpec(memory_space=pl.ANY)


def call(kernel, outs, in_specs, out_specs, scratch=(), flops=0, nbytes=0, vmem=VMEM_LIMIT):
    return pl.pallas_call(
        kernel,
        out_shape=outs,
        in_specs=in_specs,
        out_specs=out_specs,
        scratch_shapes=list(scratch),
        compiler_params=pltpu.CompilerParams(vmem_limit_bytes=vmem),
        cost_estimate=pl.CostEstimate(flops=flops, bytes_accessed=nbytes, transcendentals=0),
    )


def shape(*dims, dtype=BF):
    return jax.ShapeDtypeStruct(dims, dtype)


def pack_kernel(
    low, up, dia, low_s, up_s, dia_s, widths, pattern, out0, out1, out2, out3
):
    x, z, y, c = place()
    rows = (32 * (4 * z + y)) + lax.broadcasted_iota(jnp.int32, (32, 256), 0)
    cols = lax.broadcasted_iota(jnp.int32, (32, 256), 1)

    def mask(row_node, col_node, on, half):
        keep = (rows < widths[row_node]) & (cols + 256 * half < widths[col_node]) & (on != 0)
        return jnp.where(keep, 1.0, 0.0).astype(BF)[None]

    @pl.when(c == 0)
    def _():
        for d, out in enumerate((out0, out1, out2, out3)):
            k = node_of(lax.rem(y + d, 4))
            p = lax.div(k - 1, 2)
            at = 2 * (k - 3) + 2
            for h, (lo, u, di) in enumerate(((low, up, dia), (low_s, up_s, dia_s))):
                out[0, h] = di[p] * mask(p, p, 1, h)
                out[1, h] = lo[at] * mask(p, k, pattern[at], h)
                out[2, h] = lo[at + 1] * mask(0, k, pattern[at + 1], h)
                out[3, h] = u[at] * mask(k, p, pattern[at], h)
                out[4, h] = u[at + 1] * mask(k, 0, pattern[at + 1], h)
                out[5, h] = di[k] * mask(k, k, 1, h)

    @pl.when(c == 1)
    def _():
        for h, (lo, u, di) in enumerate(((low_s, up_s, dia_s), (low, up, dia))):
            tiles = [di[0] * mask(0, 0, 1, h)]
            for i in range(2):
                tiles.append(u[i] * mask(1 + i, 0, pattern[i], h))
                tiles.append(lo[i] * mask(0, 1 + i, pattern[i], h))
            for out in (out0, out1, out2, out3):
                for t in range(5):
                    out[t, h] = tiles[t]


def run_copies(copies, sems):
    made = [pltpu.make_async_copy(s, t, sems.at[i]) for i, (s, t) in enumerate(copies)]
    for m in made:
        m.start()
    for m in made:
        m.wait()


def merge_kernel(b0, b1, b2, b3, near, far, uk, sems):
    x, z, y, c = place()
    p = lax.rem(y, 2)

    @pl.when(c == 0)
    def _():
        copies = []
        for d, buf in enumerate((b0, b1, b2, b3)):
            at = lax.rem(y + 4 - d, 4)
            copies.append((buf.at[pl.ds(0, 3)], near.at[:, :, :, at]))
            copies.append((buf.at[pl.ds(0, 3)], far.at[:, :, :, at]))
            copies.append((buf.at[pl.ds(3, 3)], uk.at[:, :, :, at]))
        run_copies(copies, sems)

    @pl.when(c == 1)
    def _():
        copies = []
        for d, buf in enumerate((b0, b1, b2, b3)):
            at = lax.rem(z + 4 - d, 4)
            copies.append((buf.at[0], near.at[0, :, :, at]))
            copies.append((buf.at[0], far.at[0, :, :, at]))
            copies.append((buf.at[pl.ds(1 + 2 * p, 2)], far.at[pl.ds(1, 2), :, :, at]))
            copies.append((buf.at[pl.ds(3 - 2 * p, 2)], near.at[pl.ds(1, 2), :, :, at]))
        run_copies(copies, sems)


def left_of(pairs):
    real = [jnp.concatenate([r, -i], axis=1) for r, i in pairs]
    imag = [jnp.concatenate([i, r], axis=1) for r, i in pairs]
    return jnp.concatenate(real + imag, axis=0)


def dot(a, b):
    return jnp.dot(a, b, preferred_element_type=F32)


def pairs_of(res, count):
    half = 128 * count
    return [
        (res[128 * i : 128 * i + 128], res[half + 128 * i : half + 128 * i + 128])
        for i in range(count)
    ]


def split_kernel(r0, r1, r2, r3, first, second, sems):
    x, z, y, c = place()

    @pl.when(c == 0)
    def _():
        copies = []
        for d, buf in enumerate((r0, r1, r2, r3)):
            at = lax.rem(z + 4 - d, 4)
            copies.append((buf.at[pl.ds(1, 2), 0], first.at[:, :, at]))
            copies.append((buf.at[pl.ds(1, 2), 1], second.at[:, :, at]))
        run_copies(copies, sems)


def first_kernel(r0, r1, r2, r3, uk, uks, out, right, sems):
    x, z, y, c = place()

    def wide_rows(get):
        return tuple(jnp.concatenate([get(0, part), get(1, part)], axis=1) for part in range(2))

    def times(left, count, block):
        got = [pairs_of(dot(left, right[block, h].reshape(1024, 256)), count) for h in range(2)]
        return [
            tuple(jnp.concatenate([got[0][n][i], got[1][n][i]], axis=1) for i in range(2))
            for n in range(count)
        ]

    def rows_of(block):
        return wide_rows(lambda h, part: right[block, h, part, z].reshape(128, 256))

    def put(slot, pair, sign=1):
        for i in range(2):
            out[slot, i] = (pair[i] if sign > 0 else -pair[i]).astype(BF)

    @pl.when(c == 0)
    def _():
        copies = []
        for d, buf in enumerate((r0, r1, r2, r3)):
            copies.append((buf.at[0], right.at[0, :, :, lax.rem(z + 4 - d, 4)]))
        run_copies(copies, sems)
        ukp = wide_rows(lambda h, part: uk[0, h, part].reshape(128, 256))
        (kd,) = times(left_of([ukp]), 1, 0)
        put(0, kd)
        put(1, rows_of(0))

    @pl.when(c == 1)
    def _():
        copies = []
        for d, buf in enumerate((r0, r1, r2, r3)):
            copies.append((buf, right.at[:, :, :, :, lax.rem(y + 4 - d, 4)]))
        run_copies(copies, sems)
        ukp = wide_rows(lambda h, part: uks[0, h, part].reshape(128, 256))
        uk0 = wide_rows(lambda h, part: uks[1, h, part].reshape(128, 256))
        (kv,) = times(left_of([ukp]), 1, 1)
        v = tuple((uk0[i].astype(F32) - kv[i]).astype(BF) for i in range(2))
        xk0, xp0 = [
            tuple((-part).astype(BF) for part in pair)
            for pair in times(left_of([v, rows_of(1)]), 2, 0)
        ]
        d0r = rows_of(0)
        kl, pl_, dl = times(left_of([xk0, xp0, d0r]), 3, 2)
        put(0, pl_)
        put(1, dl, -1)
        put(2, kl)
        put(3, xp0)
        put(4, d0r)
        put(5, xk0)


def second_kernel(
    edge, edge_s, half0, half1, uk, uks, res, slot0, slot1, slot2, slot3, parts
):
    x, z, y, c = place()
    wr, wi = res[0, 0], res[0, 1]

    def density(re, im):
        return wr * re.astype(F32) - wi * im.astype(F32)

    def work(e0, e1, right, dk, half):
        own = slice(256 * half, 256 * half + 256)
        xpp = [e0[1, i].astype(F32) - e1[0, i].astype(F32) for i in range(2)]
        xkp = [-(e0[0, i].astype(F32) + e1[2, i].astype(F32)) for i in range(2)]
        left_p = left_of(
            [
                tuple(v.astype(BF) for v in xpp),
                (e1[1, 0], e1[1, 1]),
                tuple(v.astype(BF) for v in xkp),
            ]
        )
        left_0 = left_of([(e1[i, 0], e1[i, 1]) for i in (3, 4, 5)])
        total = dot(left_p, right[0].reshape(1024, 256)) + dot(
            left_0, right[1].reshape(1024, 256)
        )
        pk, ok, kk = pairs_of(total, 3)
        parts[0] = density(
            dk[2, half, 0].reshape(128, 256).astype(F32) - kk[0],
            dk[2, half, 1].reshape(128, 256).astype(F32) - kk[1],
        )
        parts[1] = density(-pk[0], -pk[1])
        parts[2] = density(-ok[0], -ok[1])
        parts[3] = density(xkp[0][:, own], xkp[1][:, own])
        parts[4] = density(e1[5, 0, :, own], e1[5, 1, :, own])

        @pl.when(y < 2)
        def _():
            parts[5] = density(xpp[0][:, own], xpp[1][:, own])
            parts[6] = density(e1[4, 0, :, own], e1[4, 1, :, own])

        @pl.when(y >= 2)
        def _():
            parts[5] = density(e1[3, 0, :, own], e1[3, 1, :, own])
            parts[6] = density(e1[1, 0, :, own], e1[1, 1, :, own])

    @pl.when(c == 0)
    def _():
        work(edge, edge_s, half0, uk, 0)

    @pl.when(c == 1)
    def _():
        work(edge_s, edge, half1, uks, 1)

    for d, out in enumerate((slot0, slot1, slot2, slot3)):
        at = pl.multiple_of(32 * lax.rem(x + d, 4), 32)
        for b in range(7):
            out[b] = parts[b, pl.ds(at, 32), :].astype(BF)


def sum_kernel(a0, a1, a2, a3, out):
    total = a0[...].astype(F32) + a1[...].astype(F32)
    out[...] = (total + (a2[...].astype(F32) + a3[...].astype(F32))).astype(BF)


def spread(step):
    return [
        (x * 16 + z * 4 + y, ((y + step) % 4) * 16 + z * 4 + x)
        for x in range(4)
        for z in range(4)
        for y in range(4)
    ]


def final_kernel(g0, g1, g2, g3, out):
    x, z, y, c = place()
    for d, g in enumerate((g0, g1, g2, g3)):
        b = lax.rem(x + 4 - d, 4)
        k = node_of(b)
        p = 1 + lax.rem(b, 2)
        pair = 2 * (k - 3) + 2
        low = b < 2
        out[k] = g[0].astype(F32)
        out[7 + pair] = g[1].astype(F32)
        out[8 + pair] = g[2].astype(F32)
        out[17 + pair] = g[3].astype(F32)
        out[18 + pair] = g[4].astype(F32)
        out[jnp.where(low, p, 16 + p)] = g[5].astype(F32)

        @pl.when(b != 1)
        def _():
            out[jnp.where(low, 0, 6 + p)] = g[6].astype(F32)


def body(lower_factor, upper_factor, diag_inverse, residues, widths, pattern):
    mine = (lower_factor[0], upper_factor[0], diag_inverse[0])
    swapped = [lax.ppermute(a, "col", SWAP) for a in mine]
    grid = ("row", "col")
    bufs = call(
        pack_kernel,
        [shape(6, 2, 2, 32, 256)] * 4,
        [vm()] * 6 + [sm()] * 2,
        [vm()] * 4,
        nbytes=4 << 20,
    )(*mine, *swapped, widths, pattern)
    came = {d: lax.ppermute(bufs[d], grid, ring_both(d)) for d in (1, 3, 2)}
    near, far, uk = call(
        merge_kernel,
        [shape(3, 2, 2, 4, 32, 256)] * 3,
        [hbm()] * 4,
        [hbm()] * 3,
        [pltpu.SemaphoreType.DMA((16,))],
        nbytes=4 << 20,
    )(bufs[0], came[1], came[2], came[3])
    came = {d: lax.ppermute(near, grid, ring_other(d)) for d in (1, 3)}
    came[2] = lax.ppermute(far, grid, ring_other(2))
    uks = lax.ppermute(uk, "col", SWAP)
    blocks = (far, came[1], came[2], came[3])
    half0, half1 = call(
        split_kernel,
        [shape(2, 2, 4, 4, 32, 256)] * 2,
        [hbm()] * 4,
        [hbm()] * 2,
        [pltpu.SemaphoreType.DMA((8,))],
        nbytes=4 << 20,
    )(*blocks)
    half1 = lax.ppermute(half1, "col", SWAP)
    edge = call(
        first_kernel,
        [shape(6, 2, 128, 512)],
        [hbm()] * 4 + [vm()] * 2,
        [vm()],
        [pltpu.VMEM((3, 2, 2, 4, 4, 32, 256), BF), pltpu.SemaphoreType.DMA((4,))],
        flops=1610612736,
        nbytes=4 << 20,
    )(*blocks, uk, uks)[0]
    edge_s = lax.ppermute(edge, "col", SWAP)
    slots = call(
        second_kernel,
        [shape(7, 32, 256)] * 4,
        [vm()] * 6 + [sm()],
        [vm()] * 4,
        [pltpu.VMEM((7, 128, 256), F32)],
        flops=805306368,
        nbytes=4 << 20,
    )(edge, edge_s, half0, half1, uk, uks, residues)
    at_x = [slots[0]] + [lax.ppermute(slots[d], "pole", ring_x(d)) for d in (1, 3, 2)]
    total = call(sum_kernel, [shape(7, 32, 256)], [vm()] * 4, [vm()], nbytes=1 << 20)(*at_x)[0]
    full = [lax.ppermute(total, ("pole", "row"), spread(d)) for d in range(4)]
    return call(
        final_kernel, [shape(27, 32, 256, dtype=F32)], [vm()] * 4, [vm()], nbytes=2 << 20
    )(*full)[0]


def solution(mesh):
    return jax.shard_map(
        body,
        mesh=mesh,
        in_specs=(
            P("pole", None, None, "row", "col"),
            P("pole", None, None, "row", "col"),
            P("pole", None, None, "row", "col"),
            P("pole", None),
            P(),
            P(),
        ),
        out_specs=P(None, "row", "col"),
        check_vma=False,
    )
```

```python
import jax
import jax.numpy as jnp
from jax import lax
from jax.experimental import pallas as pl
from jax.experimental.pallas import tpu as pltpu
from jax.sharding import PartitionSpec as P

BF = jnp.bfloat16
F32 = jnp.float32
VMEM_LIMIT = 24 * 1024 * 1024


def ring_both(step):
    pairs = []
    for z in range(4):
        for y in range(4):
            here = (z * 4 + y) * 2
            pairs.append((here, (z * 4 + (y + step) % 4) * 2))
            pairs.append((here + 1, (((z + step) % 4) * 4 + y) * 2 + 1))
    return pairs


def ring_other(step):
    pairs = []
    for z in range(4):
        for y in range(4):
            here = (z * 4 + y) * 2
            pairs.append((here, (((z + step) % 4) * 4 + y) * 2))
            pairs.append((here + 1, (z * 4 + (y + step) % 4) * 2 + 1))
    return pairs


def pairs_x(step):
    return [(x, x ^ step) for x in range(4)]


SWAP = [(0, 1), (1, 0)]


def place():
    row = lax.axis_index("row")
    return lax.axis_index("pole"), lax.div(row, 4), lax.rem(row, 4), lax.axis_index("col")


def node_of(y):
    return 3 + 2 * lax.rem(y, 2) + lax.div(y, 2)


def vm():
    return pl.BlockSpec(memory_space=pltpu.VMEM)


def sm():
    return pl.BlockSpec(memory_space=pltpu.SMEM)


def in_hbm():
    return pl.BlockSpec(memory_space=pltpu.HBM)


def hbm():
    return pl.BlockSpec(memory_space=pl.ANY)


def call(kernel, outs, in_specs, out_specs, scratch=(), flops=0, nbytes=0, aliases={}):
    return pl.pallas_call(
        kernel,
        out_shape=outs,
        in_specs=in_specs,
        out_specs=out_specs,
        scratch_shapes=list(scratch),
        input_output_aliases=aliases,
        compiler_params=pltpu.CompilerParams(vmem_limit_bytes=VMEM_LIMIT),
        cost_estimate=pl.CostEstimate(flops=flops, bytes_accessed=nbytes, transcendentals=0),
    )


def shape(*dims, dtype=BF):
    return jax.ShapeDtypeStruct(dims, dtype)


def pack(low, up, dia, widths, pattern, outs, own):
    x, z, y, c = place()
    rows = (32 * (4 * z + y)) + lax.broadcasted_iota(jnp.int32, (32, 256), 0)
    cols = lax.broadcasted_iota(jnp.int32, (32, 256), 1)

    def mask(row_node, col_node, on, half):
        keep = (rows < widths[row_node]) & (cols + 256 * half < widths[col_node]) & (on != 0)
        return jnp.where(keep, 1.0, 0.0).astype(BF)[None]

    @pl.when(c == 0)
    def _():
        h = 0 if own else 1
        for d, out in enumerate(outs):
            k = node_of(lax.rem(y + d, 4))
            p = lax.div(k - 1, 2)
            at = 2 * (k - 3) + 2
            out[0, h] = dia[p] * mask(p, p, 1, h)
            out[1, h] = low[at] * mask(p, k, pattern[at], h)
            out[2, h] = low[at + 1] * mask(0, k, pattern[at + 1], h)
            out[3, h] = up[at] * mask(k, p, pattern[at], h)
            out[4, h] = up[at + 1] * mask(k, 0, pattern[at + 1], h)
            out[5, h] = dia[k] * mask(k, k, 1, h)

    @pl.when(c == 1)
    def _():
        h = 1 if own else 0
        tiles = [dia[0] * mask(0, 0, 1, h)]
        for i in range(2):
            tiles.append(up[i] * mask(1 + i, 0, pattern[i], h))
            tiles.append(low[i] * mask(0, 1 + i, pattern[i], h))
        for out in outs:
            for t in range(5):
                out[t, h] = tiles[t]


def pack_own_kernel(
    low_in, up_in, dia_in, widths_in, pattern_in, o0, o1, o2, o3, widths, pattern, low, up, dia, sems
):
    run_copies(
        [(low_in, low), (up_in, up), (dia_in, dia), (widths_in, widths), (pattern_in, pattern)],
        sems,
    )
    pack(low, up, dia, widths, pattern, (o0, o1, o2, o3), True)


def pack_other_kernel(low, up, dia, widths, pattern, i0, i1, i2, i3, *outs):
    pack(low, up, dia, widths, pattern, outs, False)


def run_copies(copies, sems):
    made = [pltpu.make_async_copy(s, t, sems.at[i]) for i, (s, t) in enumerate(copies)]
    for m in made:
        m.start()
    for m in made:
        m.wait()


def merge_kernel(b0, b2, b3, b1, near, far, uk, sems):
    x, z, y, c = place()
    p = lax.rem(y, 2)

    @pl.when(c == 0)
    def _():
        copies = []
        for d, buf in enumerate((b0, b1, b2, b3)):
            at = lax.rem(y + 4 - d, 4)
            copies.append((buf.at[pl.ds(0, 3)], near.at[:, :, :, at]))
            copies.append((buf.at[pl.ds(0, 3)], far.at[:, :, :, at]))
            copies.append((buf.at[pl.ds(3, 3)], uk.at[:, :, :, at]))
        run_copies(copies, sems)

    @pl.when(c == 1)
    def _():
        copies = []
        for d, buf in enumerate((b0, b1, b2, b3)):
            at = lax.rem(z + 4 - d, 4)
            copies.append((buf.at[0], near.at[0, :, :, at]))
            copies.append((buf.at[0], far.at[0, :, :, at]))
            copies.append((buf.at[pl.ds(1 + 2 * p, 2)], far.at[pl.ds(1, 2), :, :, at]))
            copies.append((buf.at[pl.ds(3 - 2 * p, 2)], near.at[pl.ds(1, 2), :, :, at]))
        run_copies(copies, sems)


def left_of(pairs):
    real = [jnp.concatenate([r, -i], axis=1) for r, i in pairs]
    imag = [jnp.concatenate([i, r], axis=1) for r, i in pairs]
    return jnp.concatenate(real + imag, axis=0)


def dot(a, b):
    return jnp.dot(a, b, preferred_element_type=F32)


def pairs_of(res, count):
    half = 128 * count
    return [
        (res[128 * i : 128 * i + 128], res[half + 128 * i : half + 128 * i + 128])
        for i in range(count)
    ]


def split_kernel(r0, r3, r2, r1, after, first, second, sems):
    x, z, y, c = place()

    @pl.when(c == 0)
    def _():
        copies = []
        for d, buf in enumerate((r0, r1, r2, r3)):
            at = lax.rem(z + 4 - d, 4)
            copies.append((buf.at[pl.ds(1, 2), 0], first.at[:, :, at]))
            copies.append((buf.at[pl.ds(1, 2), 1], second.at[:, :, at]))
        run_copies(copies, sems)


def wide_rows(get):
    return tuple(jnp.concatenate([get(0, part), get(1, part)], axis=1) for part in range(2))


def times(left, count, right):
    got = [pairs_of(dot(left, right[h].reshape(1024, 256)), count) for h in range(2)]
    return [
        tuple(jnp.concatenate([got[0][n][i], got[1][n][i]], axis=1) for i in range(2))
        for n in range(count)
    ]


def put(out, slot, pair, sign=1):
    for i in range(2):
        out[slot, i] = (pair[i] if sign > 0 else -pair[i]).astype(BF)


def first_kernel(r0, r3, r2, r1, uk, uks, after, out, last, right, sems):
    x, z, y, c = place()

    def rows_of(block):
        return wide_rows(lambda h, part: right[block, h, part, z].reshape(128, 256))

    @pl.when(c == 0)
    def _():
        copies = []
        for d, buf in enumerate((r0, r1, r2, r3)):
            copies.append((buf.at[0], right.at[0, :, :, lax.rem(z + 4 - d, 4)]))
        run_copies(copies, sems)
        ukp = wide_rows(lambda h, part: uk[0, h, part].reshape(128, 256))
        (kd,) = times(left_of([ukp]), 1, right[0])
        put(out, 0, kd)
        put(out, 1, rows_of(0))

    @pl.when(c == 1)
    def _():
        copies = []
        for d, buf in enumerate((r0, r1, r2, r3)):
            at = lax.rem(y + 4 - d, 4)
            copies.append((buf.at[pl.ds(0, 2)], right.at[:, :, :, :, at]))
            copies.append((buf.at[2], last.at[:, :, :, at]))
        run_copies(copies, sems)
        ukp = wide_rows(lambda h, part: uks[0, h, part].reshape(128, 256))
        uk0 = wide_rows(lambda h, part: uks[1, h, part].reshape(128, 256))
        (kv,) = times(left_of([ukp]), 1, right[1])
        v = tuple((uk0[i].astype(F32) - kv[i]).astype(BF) for i in range(2))
        xk0, xp0 = times(left_of([v, rows_of(1)]), 2, right[0])
        put(out, 0, xp0, -1)
        put(out, 1, rows_of(0))
        put(out, 2, xk0, -1)


def next_kernel(edge, last, after, out):
    x, z, y, c = place()

    @pl.when(c == 1)
    def _():
        pl_, dl, kl = times(left_of([(edge[n, 0], edge[n, 1]) for n in range(3)]), 3, last)
        put(out, 0, pl_)
        put(out, 1, dl, -1)
        put(out, 2, kl)


def density_of(res):
    wr, wi = res[0, 0], res[0, 1]
    return lambda re, im: wr * re.astype(F32) - wi * im.astype(F32)


def third_kernel(edge, edge_s, half0, half1, res, prod, dens):
    x, z, y, c = place()
    density = density_of(res)

    def work(e, right, half):
        own = slice(256 * half, 256 * half + 256)
        left = left_of([(e[n, 0], e[n, 1]) for n in range(3)])
        prod[...] = dot(left, right[1].reshape(1024, 256))
        dens[0] = density(e[2, 0, :, own], e[2, 1, :, own])

        @pl.when(y < 2)
        def _():
            dens[1] = density(e[1, 0, :, own], e[1, 1, :, own])

        @pl.when(y >= 2)
        def _():
            dens[1] = density(e[0, 0, :, own], e[0, 1, :, own])

    @pl.when(c == 0)
    def _():
        work(edge_s, half0, 0)

    @pl.when(c == 1)
    def _():
        work(edge, half1, 1)


def last_kernel(
    edge, edge_s, more, more_s, half0, half1, prod, dens, uk, uks, res,
    slot0, slot1, slot2, slot3, parts,
):
    x, z, y, c = place()
    density = density_of(res)

    def work(e0, e1, right, dk, half):
        own = slice(256 * half, 256 * half + 256)
        xpp = [e0[1, i].astype(F32) - e1[0, i].astype(F32) for i in range(2)]
        xkp = [-(e0[0, i].astype(F32) + e1[2, i].astype(F32)) for i in range(2)]
        left = left_of(
            [
                tuple(v.astype(BF) for v in xpp),
                (e1[1, 0], e1[1, 1]),
                tuple(v.astype(BF) for v in xkp),
            ]
        )
        pk, ok, kk = pairs_of(prod[...] + dot(left, right[0].reshape(1024, 256)), 3)
        parts[0] = density(
            dk[2, half, 0].reshape(128, 256).astype(F32) - kk[0],
            dk[2, half, 1].reshape(128, 256).astype(F32) - kk[1],
        )
        parts[1] = density(-pk[0], -pk[1])
        parts[2] = density(-ok[0], -ok[1])
        parts[3] = density(xkp[0][:, own], xkp[1][:, own])
        parts[4] = dens[0]
        parts[5] = dens[1]

        @pl.when(y < 2)
        def _():
            parts[6] = density(xpp[0][:, own], xpp[1][:, own])

        @pl.when(y >= 2)
        def _():
            parts[6] = density(e1[1, 0, :, own], e1[1, 1, :, own])

    @pl.when(c == 0)
    def _():
        work(edge, more_s, half0, uk, 0)

    @pl.when(c == 1)
    def _():
        work(edge_s, more, half1, uks, 1)

    for d, out in enumerate((slot0, slot1, slot2, slot3)):
        at = pl.multiple_of(32 * lax.rem((x ^ d) + y, 4), 32)
        for b in range(7):
            out[b] = parts[b, pl.ds(at, 32), :].astype(BF)


def sum_kernel(a0, a1, a2, a3, out):
    total = a0[...].astype(F32) + a1[...].astype(F32)
    out[...] = (total + (a2[...].astype(F32) + a3[...].astype(F32))).astype(BF)


def spread(step):
    return [
        (x * 16 + z * 4 + y, ((x + step) % 4) * 16 + z * 4 + (x + y) % 4)
        for x in range(4)
        for z in range(4)
        for y in range(4)
    ]


def final_kernel(g0, g1, g3, g2, out):
    x, z, y, c = place()
    for d, g in enumerate((g0, g1, g2, g3)):
        b = lax.rem(y + 8 - x + d, 4)
        k = node_of(b)
        p = 1 + lax.rem(b, 2)
        pair = 2 * (k - 3) + 2
        low = b < 2
        out[k] = g[0].astype(F32)
        out[7 + pair] = g[1].astype(F32)
        out[8 + pair] = g[2].astype(F32)
        out[17 + pair] = g[3].astype(F32)
        out[18 + pair] = g[4].astype(F32)
        out[jnp.where(low, p, 6 + p)] = g[6].astype(F32)

        @pl.when(b != 1)
        def _():
            out[jnp.where(low, 0, 16 + p)] = g[5].astype(F32)


def body(lower_factor, upper_factor, diag_inverse, residues, widths, pattern):
    mine = (lower_factor[0], upper_factor[0], diag_inverse[0])
    swapped = [lax.ppermute(a, "col", SWAP) for a in mine]
    grid = ("row", "col")
    *bufs, widths, pattern = call(
        pack_own_kernel,
        [shape(6, 2, 2, 32, 256)] * 4 + [shape(7, dtype=jnp.int32), shape(10, dtype=jnp.int32)],
        [in_hbm()] * 5,
        [vm()] * 4 + [sm()] * 2,
        [
            pltpu.VMEM((10, 2, 32, 256), BF),
            pltpu.VMEM((10, 2, 32, 256), BF),
            pltpu.VMEM((7, 2, 32, 256), BF),
            pltpu.SemaphoreType.DMA((5,)),
        ],
        nbytes=4 << 20,
    )(*[pltpu.with_memory_space_constraint(a, pltpu.HBM) for a in (*mine, widths, pattern)])
    bufs = call(
        pack_other_kernel,
        [shape(6, 2, 2, 32, 256)] * 4,
        [vm()] * 3 + [sm()] * 2 + [hbm()] * 4,
        [vm()] * 4,
        nbytes=4 << 20,
        aliases={5: 0, 6: 1, 7: 2, 8: 3},
    )(*swapped, widths, pattern, *bufs)
    came = {d: lax.ppermute(bufs[d], grid, ring_both(d)) for d in (1, 3, 2)}
    near, far, uk = call(
        merge_kernel,
        [shape(3, 2, 2, 4, 32, 256)] * 3,
        [hbm()] * 4,
        [hbm()] * 3,
        [pltpu.SemaphoreType.DMA((16,))],
        nbytes=4 << 20,
    )(bufs[0], came[2], came[3], came[1])
    came = {d: lax.ppermute(near, grid, ring_other(d)) for d in (1, 3)}
    came[2] = lax.ppermute(far, grid, ring_other(2))
    uks = lax.ppermute(uk, "col", SWAP)
    blocks = (far, came[3], came[2], came[1])
    half0, half1 = call(
        split_kernel,
        [shape(2, 2, 4, 4, 32, 256)] * 2,
        [hbm()] * 5,
        [hbm()] * 2,
        [pltpu.SemaphoreType.DMA((8,))],
        nbytes=4 << 20,
    )(*blocks, uks)
    half1 = lax.ppermute(half1, "col", SWAP)
    edge, last = call(
        first_kernel,
        [shape(3, 2, 128, 512), shape(2, 2, 4, 4, 32, 256)],
        [hbm()] * 4 + [vm()] * 2 + [hbm()],
        [vm(), hbm()],
        [pltpu.VMEM((2, 2, 2, 4, 4, 32, 256), BF), pltpu.SemaphoreType.DMA((8,))],
        flops=805306368,
        nbytes=4 << 20,
    )(*blocks, uk, uks, half0)
    edge_s = lax.ppermute(edge, "col", SWAP)
    more = call(
        next_kernel,
        [shape(3, 2, 128, 512)],
        [vm(), vm(), hbm()],
        [vm()],
        flops=805306368,
        nbytes=2 << 20,
    )(edge, last, half1)[0]
    more_s = lax.ppermute(more, "col", SWAP)
    prod, dens = call(
        third_kernel,
        [shape(768, 256, dtype=F32), shape(2, 128, 256, dtype=F32)],
        [vm()] * 4 + [sm()],
        [vm()] * 2,
        flops=402653184,
        nbytes=2 << 20,
    )(edge, edge_s, half0, half1, residues)
    slots = call(
        last_kernel,
        [shape(7, 32, 256)] * 4,
        [vm()] * 10 + [sm()],
        [vm()] * 4,
        [pltpu.VMEM((7, 128, 256), F32)],
        flops=402653184,
        nbytes=4 << 20,
    )(edge, edge_s, more, more_s, half0, half1, prod, dens, uk, uks, residues)
    at_x = [slots[0]] + [lax.ppermute(slots[d], "pole", pairs_x(d)) for d in (2, 3, 1)]
    total = call(sum_kernel, [shape(7, 32, 256)], [vm()] * 4, [vm()], nbytes=1 << 20)(*at_x)[0]
    sent = {d: lax.ppermute(total, ("pole", "row"), spread(d)) for d in (0, 1, 3, 2)}
    full = [sent[d] for d in (0, 1, 3, 2)]
    return call(
        final_kernel, [shape(27, 32, 256, dtype=F32)], [vm()] * 4, [vm()], nbytes=2 << 20
    )(*full)[0]


def solution(mesh):
    return jax.shard_map(
        body,
        mesh=mesh,
        in_specs=(
            P("pole", None, None, "row", "col"),
            P("pole", None, None, "row", "col"),
            P("pole", None, None, "row", "col"),
            P("pole", None),
            P(),
            P(),
        ),
        out_specs=P(None, "row", "col"),
        check_vma=False,
    )
```

```python
import jax
import jax.numpy as jnp
from jax import lax
from jax.experimental import pallas as pl
from jax.experimental.pallas import tpu as pltpu
from jax.sharding import PartitionSpec as P

BF = jnp.bfloat16
F32 = jnp.float32
VMEM_LIMIT = 24 * 1024 * 1024


def ring_both(step):
    pairs = []
    for z in range(4):
        for y in range(4):
            here = (z * 4 + y) * 2
            pairs.append((here, (z * 4 + (y + step) % 4) * 2))
            pairs.append((here + 1, (((z + step) % 4) * 4 + y) * 2 + 1))
    return pairs


def ring_other(step):
    pairs = []
    for z in range(4):
        for y in range(4):
            here = (z * 4 + y) * 2
            pairs.append((here, (((z + step) % 4) * 4 + y) * 2))
            pairs.append((here + 1, (z * 4 + (y + step) % 4) * 2 + 1))
    return pairs


def pairs_x(step):
    return [(x, x ^ step) for x in range(4)]


SWAP = [(0, 1), (1, 0)]


def place():
    row = lax.axis_index("row")
    return lax.axis_index("pole"), lax.div(row, 4), lax.rem(row, 4), lax.axis_index("col")


def node_of(y):
    return 3 + 2 * lax.rem(y, 2) + lax.div(y, 2)


def vm():
    return pl.BlockSpec(memory_space=pltpu.VMEM)


def sm():
    return pl.BlockSpec(memory_space=pltpu.SMEM)


def in_hbm():
    return pl.BlockSpec(memory_space=pltpu.HBM)


def hbm():
    return pl.BlockSpec(memory_space=pl.ANY)


def call(kernel, outs, in_specs, out_specs, scratch=(), flops=0, nbytes=0, aliases={}):
    return pl.pallas_call(
        kernel,
        out_shape=outs,
        in_specs=in_specs,
        out_specs=out_specs,
        scratch_shapes=list(scratch),
        input_output_aliases=aliases,
        compiler_params=pltpu.CompilerParams(vmem_limit_bytes=VMEM_LIMIT),
        cost_estimate=pl.CostEstimate(flops=flops, bytes_accessed=nbytes, transcendentals=0),
    )


def shape(*dims, dtype=BF):
    return jax.ShapeDtypeStruct(dims, dtype)


def pack(low, up, dia, widths, pattern, outs, own):
    x, z, y, c = place()
    rows = (32 * (4 * z + y)) + lax.broadcasted_iota(jnp.int32, (32, 256), 0)
    cols = lax.broadcasted_iota(jnp.int32, (32, 256), 1)

    def mask(row_node, col_node, on, half):
        keep = (rows < widths[row_node]) & (cols + 256 * half < widths[col_node]) & (on != 0)
        return jnp.where(keep, 1.0, 0.0).astype(BF)[None]

    @pl.when(c == 0)
    def _():
        h = 0 if own else 1
        for d, out in enumerate(outs):
            k = node_of(lax.rem(y + d, 4))
            p = lax.div(k - 1, 2)
            at = 2 * (k - 3) + 2
            out[0, h] = dia[p] * mask(p, p, 1, h)
            out[1, h] = low[at] * mask(p, k, pattern[at], h)
            out[2, h] = low[at + 1] * mask(0, k, pattern[at + 1], h)
            out[3, h] = up[at] * mask(k, p, pattern[at], h)
            out[4, h] = up[at + 1] * mask(k, 0, pattern[at + 1], h)
            out[5, h] = dia[k] * mask(k, k, 1, h)

    @pl.when(c == 1)
    def _():
        h = 1 if own else 0
        tiles = [dia[0] * mask(0, 0, 1, h)]
        for i in range(2):
            tiles.append(up[i] * mask(1 + i, 0, pattern[i], h))
            tiles.append(low[i] * mask(0, 1 + i, pattern[i], h))
        for out in outs:
            for t in range(5):
                out[t, h] = tiles[t]


def pack_own_kernel(
    low_in, up_in, dia_in, widths_in, pattern_in, o0, o1, o2, o3, widths, pattern, low, up, dia, sems
):
    run_copies(
        [(low_in, low), (up_in, up), (dia_in, dia), (widths_in, widths), (pattern_in, pattern)],
        sems,
    )
    pack(low, up, dia, widths, pattern, (o0, o1, o2, o3), True)


def pack_other_kernel(low, up, dia, widths, pattern, i0, i1, i2, i3, *outs):
    pack(low, up, dia, widths, pattern, outs, False)


def run_copies(copies, sems):
    made = [pltpu.make_async_copy(s, t, sems.at[i]) for i, (s, t) in enumerate(copies)]
    for m in made:
        m.start()
    for m in made:
        m.wait()


def merge_kernel(b0, b2, b3, b1, near, far, uk, sems):
    x, z, y, c = place()
    p = lax.rem(y, 2)

    @pl.when(c == 0)
    def _():
        copies = []
        for d, buf in enumerate((b0, b1, b2, b3)):
            at = lax.rem(y + 4 - d, 4)
            copies.append((buf.at[pl.ds(0, 3)], near.at[:, :, :, at]))
            copies.append((buf.at[pl.ds(0, 3)], far.at[:, :, :, at]))
            copies.append((buf.at[pl.ds(3, 3)], uk.at[:, :, :, at]))
        run_copies(copies, sems)

    @pl.when(c == 1)
    def _():
        copies = []
        for d, buf in enumerate((b0, b1, b2, b3)):
            at = lax.rem(z + 4 - d, 4)
            copies.append((buf.at[0], near.at[0, :, :, at]))
            copies.append((buf.at[0], far.at[0, :, :, at]))
            copies.append((buf.at[pl.ds(1 + 2 * p, 2)], far.at[pl.ds(1, 2), :, :, at]))
            copies.append((buf.at[pl.ds(3 - 2 * p, 2)], near.at[pl.ds(1, 2), :, :, at]))
        run_copies(copies, sems)


def left_of(pairs):
    real = [jnp.concatenate([r, -i], axis=1) for r, i in pairs]
    imag = [jnp.concatenate([i, r], axis=1) for r, i in pairs]
    return jnp.concatenate(real + imag, axis=0)


def dot(a, b):
    return jnp.dot(a, b, preferred_element_type=F32)


def pairs_of(res, count):
    half = 128 * count
    return [
        (res[128 * i : 128 * i + 128], res[half + 128 * i : half + 128 * i + 128])
        for i in range(count)
    ]


def split_kernel(r0, r3, r2, r1, after, stay, go, sems):
    x, z, y, c = place()

    @pl.when(c == 0)
    def _():
        copies = []
        for d, buf in enumerate((r0, r1, r2, r3)):
            at = lax.rem(z + 4 - d, 4)
            copies.append((buf.at[pl.ds(1, 2), 0], stay.at[:, :, at]))
            copies.append((buf.at[pl.ds(1, 2), 1], go.at[:, :, at]))
        run_copies(copies, sems)

    @pl.when(c == 1)
    def _():
        copies = []
        for d, buf in enumerate((r0, r1, r2, r3)):
            copies.append((buf.at[2], go.at[:, :, :, lax.rem(y + 4 - d, 4)]))
        run_copies(copies, sems)


def wide_rows(get):
    return tuple(jnp.concatenate([get(0, part), get(1, part)], axis=1) for part in range(2))


def times(left, count, right):
    got = [pairs_of(dot(left, right[h].reshape(1024, 256)), count) for h in range(2)]
    return [
        tuple(jnp.concatenate([got[0][n][i], got[1][n][i]], axis=1) for i in range(2))
        for n in range(count)
    ]


def put(out, slot, pair, sign=1):
    for i in range(2):
        out[slot, i] = (pair[i] if sign > 0 else -pair[i]).astype(BF)


def first_kernel(r0, r3, r2, r1, uk, uks, after, out, right, sems):
    x, z, y, c = place()

    def rows_of(block):
        return wide_rows(lambda h, part: right[block, h, part, z].reshape(128, 256))

    @pl.when(c == 0)
    def _():
        copies = []
        for d, buf in enumerate((r0, r1, r2, r3)):
            copies.append((buf.at[0], right.at[0, :, :, lax.rem(z + 4 - d, 4)]))
        run_copies(copies, sems)
        ukp = wide_rows(lambda h, part: uk[0, h, part].reshape(128, 256))
        (kd,) = times(left_of([ukp]), 1, right[0])
        put(out, 0, kd)
        put(out, 1, rows_of(0))

    @pl.when(c == 1)
    def _():
        copies = []
        for d, buf in enumerate((r0, r1, r2, r3)):
            at = lax.rem(y + 4 - d, 4)
            copies.append((buf.at[pl.ds(0, 2)], right.at[:, :, :, :, at]))
        run_copies(copies, sems)
        ukp = wide_rows(lambda h, part: uks[0, h, part].reshape(128, 256))
        uk0 = wide_rows(lambda h, part: uks[1, h, part].reshape(128, 256))
        (kv,) = times(left_of([ukp]), 1, right[1])
        v = tuple((uk0[i].astype(F32) - kv[i]).astype(BF) for i in range(2))
        xk0, xp0 = times(left_of([v, rows_of(1)]), 2, right[0])
        put(out, 0, xp0, -1)
        put(out, 1, rows_of(0))
        put(out, 2, xk0, -1)


def inner_kernel(stay, go, got, out):
    x, z, y, c = place()

    def work(last, own):
        lp = wide_rows(lambda h, part: last[h, part].reshape(512, 256))
        prod = dot(left_of([lp]), own[0].reshape(1024, 256))
        out[...] = (own[1].reshape(1024, 256).astype(F32) - prod).astype(BF)

    @pl.when(c == 0)
    def _():
        work(got, stay)

    @pl.when(c == 1)
    def _():
        work(go, got)


def last_kernel(
    edge, edge_s, inner, stay, go, got, uk, uks, res, slot0, slot1, slot2, slot3, parts
):
    x, z, y, c = place()
    wr, wi = res[0, 0], res[0, 1]

    def density(re, im):
        return wr * re.astype(F32) - wi * im.astype(F32)

    def work(e0, e1, last, own, dk, half):
        cols = slice(256 * half, 256 * half + 256)
        xp0, d0r, xk0 = [(e1[n, 0], e1[n, 1]) for n in range(3)]
        kd, dpr = [(e0[n, 0], e0[n, 1]) for n in range(2)]
        left = left_of([xp0, d0r, xk0])
        pg, og, kg = pairs_of(dot(left, inner[...]), 3)
        pe, oe, ke = pairs_of(dot(left, last[half].reshape(1024, 256)), 3)
        kl, pl_ = pairs_of(dot(left_of([kd, dpr]), own[0].reshape(1024, 256)), 2)
        xkk = [dk[2, half, i].reshape(128, 256).astype(F32) + kl[i] - kg[i] for i in range(2)]
        parts[0] = density(*xkk)
        parts[1] = density(*[-(pl_[i] + pg[i]) for i in range(2)])
        parts[2] = density(-og[0], -og[1])
        parts[3] = density(*[-(kd[i][:, cols].astype(F32) + ke[i]) for i in range(2)])
        parts[4] = density(xk0[0][:, cols], xk0[1][:, cols])

        @pl.when(y < 2)
        def _():
            parts[5] = density(d0r[0][:, cols], d0r[1][:, cols])
            parts[6] = density(*[dpr[i][:, cols].astype(F32) - pe[i] for i in range(2)])

        @pl.when(y >= 2)
        def _():
            parts[5] = density(xp0[0][:, cols], xp0[1][:, cols])
            parts[6] = density(-oe[0], -oe[1])

    @pl.when(c == 0)
    def _():
        work(edge, edge_s, got, stay, uk, 0)

    @pl.when(c == 1)
    def _():
        work(edge_s, edge, go, got, uks, 1)

    for d, out in enumerate((slot0, slot1, slot2, slot3)):
        at = pl.multiple_of(32 * lax.rem((x ^ d) + y, 4), 32)
        for b in range(7):
            out[b] = parts[b, pl.ds(at, 32), :].astype(BF)


def sum_kernel(a0, a1, a2, a3, out):
    total = a0[...].astype(F32) + a1[...].astype(F32)
    out[...] = (total + (a2[...].astype(F32) + a3[...].astype(F32))).astype(BF)


def spread(step):
    return [
        (x * 16 + z * 4 + y, ((x + step) % 4) * 16 + z * 4 + (x + y) % 4)
        for x in range(4)
        for z in range(4)
        for y in range(4)
    ]


def final_kernel(g0, g1, g3, g2, out):
    x, z, y, c = place()
    for d, g in enumerate((g0, g1, g2, g3)):
        b = lax.rem(y + 8 - x + d, 4)
        k = node_of(b)
        p = 1 + lax.rem(b, 2)
        pair = 2 * (k - 3) + 2
        low = b < 2
        out[k] = g[0].astype(F32)
        out[7 + pair] = g[1].astype(F32)
        out[8 + pair] = g[2].astype(F32)
        out[17 + pair] = g[3].astype(F32)
        out[18 + pair] = g[4].astype(F32)
        out[jnp.where(low, p, 6 + p)] = g[6].astype(F32)

        @pl.when(b != 1)
        def _():
            out[jnp.where(low, 0, 16 + p)] = g[5].astype(F32)


def body(lower_factor, upper_factor, diag_inverse, residues, widths, pattern):
    mine = (lower_factor[0], upper_factor[0], diag_inverse[0])
    swapped = [lax.ppermute(a, "col", SWAP) for a in mine]
    grid = ("row", "col")
    *bufs, widths, pattern = call(
        pack_own_kernel,
        [shape(6, 2, 2, 32, 256)] * 4 + [shape(7, dtype=jnp.int32), shape(10, dtype=jnp.int32)],
        [in_hbm()] * 5,
        [vm()] * 4 + [sm()] * 2,
        [
            pltpu.VMEM((10, 2, 32, 256), BF),
            pltpu.VMEM((10, 2, 32, 256), BF),
            pltpu.VMEM((7, 2, 32, 256), BF),
            pltpu.SemaphoreType.DMA((5,)),
        ],
        nbytes=4 << 20,
    )(*[pltpu.with_memory_space_constraint(a, pltpu.HBM) for a in (*mine, widths, pattern)])
    bufs = call(
        pack_other_kernel,
        [shape(6, 2, 2, 32, 256)] * 4,
        [vm()] * 3 + [sm()] * 2 + [hbm()] * 4,
        [vm()] * 4,
        nbytes=4 << 20,
        aliases={5: 0, 6: 1, 7: 2, 8: 3},
    )(*swapped, widths, pattern, *bufs)
    came = {d: lax.ppermute(bufs[d], grid, ring_both(d)) for d in (1, 3, 2)}
    near, far, uk = call(
        merge_kernel,
        [shape(3, 2, 2, 4, 32, 256)] * 3,
        [hbm()] * 4,
        [hbm()] * 3,
        [pltpu.SemaphoreType.DMA((16,))],
        nbytes=4 << 20,
    )(bufs[0], came[2], came[3], came[1])
    came = {d: lax.ppermute(near, grid, ring_other(d)) for d in (1, 3)}
    came[2] = lax.ppermute(far, grid, ring_other(2))
    uks = lax.ppermute(uk, "col", SWAP)
    blocks = (far, came[3], came[2], came[1])
    stay, go = call(
        split_kernel,
        [shape(2, 2, 4, 4, 32, 256)] * 2,
        [hbm()] * 5,
        [hbm()] * 2,
        [pltpu.SemaphoreType.DMA((8,))],
        nbytes=4 << 20,
    )(*blocks, uks)
    got = lax.ppermute(go, "col", SWAP)
    edge = call(
        first_kernel,
        [shape(3, 2, 128, 512)],
        [hbm()] * 4 + [vm()] * 2 + [hbm()],
        [vm()],
        [pltpu.VMEM((2, 2, 2, 4, 4, 32, 256), BF), pltpu.SemaphoreType.DMA((8,))],
        flops=805306368,
        nbytes=4 << 20,
    )(*blocks, uk, uks, stay)[0]
    edge_s = lax.ppermute(edge, "col", SWAP)
    inner = call(
        inner_kernel,
        [shape(1024, 256)],
        [vm()] * 3,
        [vm()],
        flops=536870912,
        nbytes=3 << 20,
    )(stay, go, got)[0]
    slots = call(
        last_kernel,
        [shape(7, 32, 256)] * 4,
        [vm()] * 8 + [sm()],
        [vm()] * 4,
        [pltpu.VMEM((7, 128, 256), F32)],
        flops=1073741824,
        nbytes=4 << 20,
    )(edge, edge_s, inner, stay, go, got, uk, uks, residues)
    at_x = [slots[0]] + [lax.ppermute(slots[d], "pole", pairs_x(d)) for d in (2, 3, 1)]
    total = call(sum_kernel, [shape(7, 32, 256)], [vm()] * 4, [vm()], nbytes=1 << 20)(*at_x)[0]
    sent = {d: lax.ppermute(total, ("pole", "row"), spread(d)) for d in (0, 1, 3, 2)}
    full = [sent[d] for d in (0, 1, 3, 2)]
    return call(
        final_kernel, [shape(27, 32, 256, dtype=F32)], [vm()] * 4, [vm()], nbytes=2 << 20
    )(*full)[0]


def solution(mesh):
    return jax.shard_map(
        body,
        mesh=mesh,
        in_specs=(
            P("pole", None, None, "row", "col"),
            P("pole", None, None, "row", "col"),
            P("pole", None, None, "row", "col"),
            P("pole", None),
            P(),
            P(),
        ),
        out_specs=P(None, "row", "col"),
        check_vma=False,
    )
```

```python
import jax
import jax.numpy as jnp
from jax import lax
from jax.experimental import pallas as pl
from jax.experimental.pallas import tpu as pltpu
from jax.sharding import PartitionSpec as P

BF = jnp.bfloat16
F32 = jnp.float32
VMEM_LIMIT = 24 * 1024 * 1024


def ring_both(step):
    pairs = []
    for z in range(4):
        for y in range(4):
            here = (z * 4 + y) * 2
            pairs.append((here, (z * 4 + (y + step) % 4) * 2))
            pairs.append((here + 1, (((z + step) % 4) * 4 + y) * 2 + 1))
    return pairs


def ring_other(step):
    pairs = []
    for z in range(4):
        for y in range(4):
            here = (z * 4 + y) * 2
            pairs.append((here, (((z + step) % 4) * 4 + y) * 2))
            pairs.append((here + 1, (z * 4 + (y + step) % 4) * 2 + 1))
    return pairs


def pairs_x(step):
    return [(x, x ^ step) for x in range(4)]


def pairs_xy(step):
    return [
        (x * 16 + z * 4 + y, (x ^ (4 - step)) * 16 + z * 4 + (y ^ step))
        for x in range(4)
        for z in range(4)
        for y in range(4)
    ]


SWAP = [(0, 1), (1, 0)]


def place():
    row = lax.axis_index("row")
    return lax.axis_index("pole"), lax.div(row, 4), lax.rem(row, 4), lax.axis_index("col")


def index_of(x, y):
    return x ^ lax.rem(8 - y, 4)


def node_of(m):
    return 3 + 2 * lax.rem(m, 2) + lax.div(m, 2)


def vm():
    return pl.BlockSpec(memory_space=pltpu.VMEM)


def sm():
    return pl.BlockSpec(memory_space=pltpu.SMEM)


def in_hbm():
    return pl.BlockSpec(memory_space=pltpu.HBM)


def hbm():
    return pl.BlockSpec(memory_space=pl.ANY)


def call(kernel, outs, in_specs, out_specs, scratch=(), flops=0, nbytes=0, aliases={}):
    return pl.pallas_call(
        kernel,
        out_shape=outs,
        in_specs=in_specs,
        out_specs=out_specs,
        scratch_shapes=list(scratch),
        input_output_aliases=aliases,
        compiler_params=pltpu.CompilerParams(vmem_limit_bytes=VMEM_LIMIT),
        cost_estimate=pl.CostEstimate(flops=flops, bytes_accessed=nbytes, transcendentals=0),
    )


def shape(*dims, dtype=BF):
    return jax.ShapeDtypeStruct(dims, dtype)


def pack(low, up, dia, widths, pattern, outs, own):
    x, z, y, c = place()
    rows = (32 * (4 * z + y)) + lax.broadcasted_iota(jnp.int32, (32, 256), 0)
    cols = lax.broadcasted_iota(jnp.int32, (32, 256), 1)

    def mask(row_node, col_node, on, half):
        keep = (rows < widths[row_node]) & (cols + 256 * half < widths[col_node]) & (on != 0)
        return jnp.where(keep, 1.0, 0.0).astype(BF)[None]

    @pl.when(c == 0)
    def _():
        h = 0 if own else 1
        for d, out in enumerate(outs):
            k = node_of(index_of(x, lax.rem(y + d, 4)))
            p = lax.div(k - 1, 2)
            at = 2 * (k - 3) + 2
            out[0, h] = dia[p] * mask(p, p, 1, h)
            out[1, h] = low[at] * mask(p, k, pattern[at], h)
            out[2, h] = low[at + 1] * mask(0, k, pattern[at + 1], h)
            out[3, h] = up[at] * mask(k, p, pattern[at], h)
            out[4, h] = up[at + 1] * mask(k, 0, pattern[at + 1], h)
            out[5, h] = dia[k] * mask(k, k, 1, h)

    @pl.when(c == 1)
    def _():
        h = 1 if own else 0
        tiles = [dia[0] * mask(0, 0, 1, h)]
        for i in range(2):
            tiles.append(up[i] * mask(1 + i, 0, pattern[i], h))
            tiles.append(low[i] * mask(0, 1 + i, pattern[i], h))
        for out in outs:
            for t in range(5):
                out[t, h] = tiles[t]


def pack_own_kernel(
    low_in, up_in, dia_in, widths_in, pattern_in, o0, o1, o2, o3, widths, pattern, low, up, dia, sems
):
    run_copies(
        [(low_in, low), (up_in, up), (dia_in, dia), (widths_in, widths), (pattern_in, pattern)],
        sems,
    )
    pack(low, up, dia, widths, pattern, (o0, o1, o2, o3), True)


def pack_other_kernel(low, up, dia, widths, pattern, i0, i1, i2, i3, *outs):
    pack(low, up, dia, widths, pattern, outs, False)


def run_copies(copies, sems):
    made = [pltpu.make_async_copy(s, t, sems.at[i]) for i, (s, t) in enumerate(copies)]
    for m in made:
        m.start()
    for m in made:
        m.wait()


def merge_kernel(b0, b2, b3, b1, near, far, uk, sems):
    x, z, y, c = place()
    p = lax.rem(index_of(x, y), 2)

    @pl.when(c == 0)
    def _():
        copies = []
        for d, buf in enumerate((b0, b1, b2, b3)):
            at = lax.rem(y + 4 - d, 4)
            copies.append((buf.at[pl.ds(0, 3)], near.at[:, :, :, at]))
            copies.append((buf.at[pl.ds(0, 3)], far.at[:, :, :, at]))
            copies.append((buf.at[pl.ds(3, 3)], uk.at[:, :, :, at]))
        run_copies(copies, sems)

    @pl.when(c == 1)
    def _():
        copies = []
        for d, buf in enumerate((b0, b1, b2, b3)):
            at = lax.rem(z + 4 - d, 4)
            copies.append((buf.at[0], near.at[0, :, :, at]))
            copies.append((buf.at[0], far.at[0, :, :, at]))
            copies.append((buf.at[pl.ds(1 + 2 * p, 2)], far.at[pl.ds(1, 2), :, :, at]))
            copies.append((buf.at[pl.ds(3 - 2 * p, 2)], near.at[pl.ds(1, 2), :, :, at]))
        run_copies(copies, sems)


def left_of(pairs):
    real = [jnp.concatenate([r, -i], axis=1) for r, i in pairs]
    imag = [jnp.concatenate([i, r], axis=1) for r, i in pairs]
    return jnp.concatenate(real + imag, axis=0)


def dot(a, b):
    return jnp.dot(a, b, preferred_element_type=F32)


def pairs_of(res, count):
    half = 128 * count
    return [
        (res[128 * i : 128 * i + 128], res[half + 128 * i : half + 128 * i + 128])
        for i in range(count)
    ]


def split_kernel(r0, r3, r2, r1, after, stay, go, sems):
    x, z, y, c = place()

    @pl.when(c == 0)
    def _():
        copies = []
        for d, buf in enumerate((r0, r1, r2, r3)):
            at = lax.rem(z + 4 - d, 4)
            copies.append((buf.at[pl.ds(1, 2), 0], stay.at[:, :, at]))
            copies.append((buf.at[pl.ds(1, 2), 1], go.at[:, :, at]))
        run_copies(copies, sems)

    @pl.when(c == 1)
    def _():
        copies = []
        for d, buf in enumerate((r0, r1, r2, r3)):
            copies.append((buf.at[2], go.at[:, :, :, lax.rem(y + 4 - d, 4)]))
        run_copies(copies, sems)


def wide_rows(get):
    return tuple(jnp.concatenate([get(0, part), get(1, part)], axis=1) for part in range(2))


def times(left, count, right):
    got = [pairs_of(dot(left, right[h].reshape(1024, 256)), count) for h in range(2)]
    return [
        tuple(jnp.concatenate([got[0][n][i], got[1][n][i]], axis=1) for i in range(2))
        for n in range(count)
    ]


def put(out, slot, pair, sign=1):
    for i in range(2):
        out[slot, i] = (pair[i] if sign > 0 else -pair[i]).astype(BF)


def first_kernel(r0, r3, r2, r1, uk, uks, after, out, right, sems):
    x, z, y, c = place()

    def rows_of(block):
        return wide_rows(lambda h, part: right[block, h, part, z].reshape(128, 256))

    @pl.when(c == 0)
    def _():
        copies = []
        for d, buf in enumerate((r0, r1, r2, r3)):
            copies.append((buf.at[0], right.at[0, :, :, lax.rem(z + 4 - d, 4)]))
        run_copies(copies, sems)
        ukp = wide_rows(lambda h, part: uk[0, h, part].reshape(128, 256))
        (kd,) = times(left_of([ukp]), 1, right[0])
        put(out, 0, kd)
        put(out, 1, rows_of(0))

    @pl.when(c == 1)
    def _():
        copies = []
        for d, buf in enumerate((r0, r1, r2, r3)):
            at = lax.rem(y + 4 - d, 4)
            copies.append((buf.at[pl.ds(0, 2)], right.at[:, :, :, :, at]))
        run_copies(copies, sems)
        ukp = wide_rows(lambda h, part: uks[0, h, part].reshape(128, 256))
        uk0 = wide_rows(lambda h, part: uks[1, h, part].reshape(128, 256))
        (kv,) = times(left_of([ukp]), 1, right[1])
        v = tuple((uk0[i].astype(F32) - kv[i]).astype(BF) for i in range(2))
        xk0, xp0 = times(left_of([v, rows_of(1)]), 2, right[0])
        put(out, 0, xp0, -1)
        put(out, 1, rows_of(0))
        put(out, 2, xk0, -1)


def inner_kernel(stay, go, got, out):
    x, z, y, c = place()

    def work(last, own):
        lp = wide_rows(lambda h, part: last[h, part].reshape(512, 256))
        prod = dot(left_of([lp]), own[0].reshape(1024, 256))
        out[...] = (own[1].reshape(1024, 256).astype(F32) - prod).astype(BF)

    @pl.when(c == 0)
    def _():
        work(got, stay)

    @pl.when(c == 1)
    def _():
        work(go, got)


def last_kernel(
    edge, edge_s, inner, stay, go, got, uk, uks, res, slot0, slot1, slot2, slot3, parts
):
    x, z, y, c = place()
    wr, wi = res[0, 0], res[0, 1]

    def density(re, im):
        return wr * re.astype(F32) - wi * im.astype(F32)

    def work(e0, e1, last, own, dk, half):
        cols = slice(256 * half, 256 * half + 256)
        xp0, d0r, xk0 = [(e1[n, 0], e1[n, 1]) for n in range(3)]
        kd, dpr = [(e0[n, 0], e0[n, 1]) for n in range(2)]
        left = left_of([xp0, d0r, xk0])
        pg, og, kg = pairs_of(dot(left, inner[...]), 3)
        pe, oe, ke = pairs_of(dot(left, last[half].reshape(1024, 256)), 3)
        kl, pl_ = pairs_of(dot(left_of([kd, dpr]), own[0].reshape(1024, 256)), 2)
        xkk = [dk[2, half, i].reshape(128, 256).astype(F32) + kl[i] - kg[i] for i in range(2)]
        parts[0] = density(*xkk)
        parts[1] = density(*[-(pl_[i] + pg[i]) for i in range(2)])
        parts[2] = density(-og[0], -og[1])
        parts[3] = density(*[-(kd[i][:, cols].astype(F32) + ke[i]) for i in range(2)])
        parts[4] = density(xk0[0][:, cols], xk0[1][:, cols])

        @pl.when(index_of(x, y) < 2)
        def _():
            parts[5] = density(d0r[0][:, cols], d0r[1][:, cols])
            parts[6] = density(*[dpr[i][:, cols].astype(F32) - pe[i] for i in range(2)])

        @pl.when(index_of(x, y) >= 2)
        def _():
            parts[5] = density(xp0[0][:, cols], xp0[1][:, cols])
            parts[6] = density(-oe[0], -oe[1])

    @pl.when(c == 0)
    def _():
        work(edge, edge_s, got, stay, uk, 0)

    @pl.when(c == 1)
    def _():
        work(edge_s, edge, go, got, uks, 1)

    for d, out in enumerate((slot0, slot1, slot2, slot3)):
        at = pl.multiple_of(32 * (y ^ d), 32)
        for b in range(7):
            out[b] = parts[b, pl.ds(at, 32), :].astype(BF)


def sum_kernel(a0, a1, a2, a3, out):
    total = a0[...].astype(F32) + a1[...].astype(F32)
    out[...] = (total + (a2[...].astype(F32) + a3[...].astype(F32))).astype(BF)


def final_kernel(g0, g1, g3, g2, out):
    x, z, y, c = place()
    for d, g in enumerate((g0, g1, g2, g3)):
        b = index_of(x ^ d, y)
        k = node_of(b)
        p = 1 + lax.rem(b, 2)
        pair = 2 * (k - 3) + 2
        low = b < 2
        out[k] = g[0].astype(F32)
        out[7 + pair] = g[1].astype(F32)
        out[8 + pair] = g[2].astype(F32)
        out[17 + pair] = g[3].astype(F32)
        out[18 + pair] = g[4].astype(F32)
        out[jnp.where(low, p, 6 + p)] = g[6].astype(F32)

        @pl.when(b != 1)
        def _():
            out[jnp.where(low, 0, 16 + p)] = g[5].astype(F32)


def body(lower_factor, upper_factor, diag_inverse, residues, widths, pattern):
    mine = (lower_factor[0], upper_factor[0], diag_inverse[0])
    swapped = [lax.ppermute(a, "col", SWAP) for a in mine]
    grid = ("row", "col")
    *bufs, widths, pattern = call(
        pack_own_kernel,
        [shape(6, 2, 2, 32, 256)] * 4 + [shape(7, dtype=jnp.int32), shape(10, dtype=jnp.int32)],
        [in_hbm()] * 5,
        [vm()] * 4 + [sm()] * 2,
        [
            pltpu.VMEM((10, 2, 32, 256), BF),
            pltpu.VMEM((10, 2, 32, 256), BF),
            pltpu.VMEM((7, 2, 32, 256), BF),
            pltpu.SemaphoreType.DMA((5,)),
        ],
        nbytes=4 << 20,
    )(*[pltpu.with_memory_space_constraint(a, pltpu.HBM) for a in (*mine, widths, pattern)])
    bufs = call(
        pack_other_kernel,
        [shape(6, 2, 2, 32, 256)] * 4,
        [vm()] * 3 + [sm()] * 2 + [hbm()] * 4,
        [vm()] * 4,
        nbytes=4 << 20,
        aliases={5: 0, 6: 1, 7: 2, 8: 3},
    )(*swapped, widths, pattern, *bufs)
    came = {d: lax.ppermute(bufs[d], grid, ring_both(d)) for d in (1, 3, 2)}
    near, far, uk = call(
        merge_kernel,
        [shape(3, 2, 2, 4, 32, 256)] * 3,
        [hbm()] * 4,
        [hbm()] * 3,
        [pltpu.SemaphoreType.DMA((16,))],
        nbytes=4 << 20,
    )(bufs[0], came[2], came[3], came[1])
    came = {d: lax.ppermute(near, grid, ring_other(d)) for d in (1, 3)}
    came[2] = lax.ppermute(far, grid, ring_other(2))
    uks = lax.ppermute(uk, "col", SWAP)
    blocks = (far, came[3], came[2], came[1])
    stay, go = call(
        split_kernel,
        [shape(2, 2, 4, 4, 32, 256)] * 2,
        [hbm()] * 5,
        [hbm()] * 2,
        [pltpu.SemaphoreType.DMA((8,))],
        nbytes=4 << 20,
    )(*blocks, uks)
    got = lax.ppermute(go, "col", SWAP)
    edge = call(
        first_kernel,
        [shape(3, 2, 128, 512)],
        [hbm()] * 4 + [vm()] * 2 + [hbm()],
        [vm()],
        [pltpu.VMEM((2, 2, 2, 4, 4, 32, 256), BF), pltpu.SemaphoreType.DMA((8,))],
        flops=805306368,
        nbytes=4 << 20,
    )(*blocks, uk, uks, stay)[0]
    edge_s = lax.ppermute(edge, "col", SWAP)
    inner = call(
        inner_kernel,
        [shape(1024, 256)],
        [vm()] * 3,
        [vm()],
        flops=536870912,
        nbytes=3 << 20,
    )(stay, go, got)[0]
    slots = call(
        last_kernel,
        [shape(7, 32, 256)] * 4,
        [vm()] * 8 + [sm()],
        [vm()] * 4,
        [pltpu.VMEM((7, 128, 256), F32)],
        flops=1073741824,
        nbytes=4 << 20,
    )(edge, edge_s, inner, stay, go, got, uk, uks, residues)
    at_x = [slots[0]] + [lax.ppermute(slots[d], ("pole", "row"), pairs_xy(d)) for d in (2, 3, 1)]
    total = call(sum_kernel, [shape(7, 32, 256)], [vm()] * 4, [vm()], nbytes=1 << 20)(*at_x)[0]
    full = [total] + [lax.ppermute(total, "pole", pairs_x(d)) for d in (1, 3, 2)]
    return call(
        final_kernel, [shape(27, 32, 256, dtype=F32)], [vm()] * 4, [vm()], nbytes=2 << 20
    )(*full)[0]


def solution(mesh):
    return jax.shard_map(
        body,
        mesh=mesh,
        in_specs=(
            P("pole", None, None, "row", "col"),
            P("pole", None, None, "row", "col"),
            P("pole", None, None, "row", "col"),
            P("pole", None),
            P(),
            P(),
        ),
        out_specs=P(None, "row", "col"),
        check_vma=False,
    )
```

```python
import jax
import jax.numpy as jnp
from jax import lax
from jax.experimental import pallas as pl
from jax.experimental.pallas import tpu as pltpu
from jax.sharding import PartitionSpec as P

BF = jnp.bfloat16
F32 = jnp.float32
VMEM_LIMIT = 24 * 1024 * 1024


def ring_both(step):
    pairs = []
    for z in range(4):
        for y in range(4):
            here = (z * 4 + y) * 2
            pairs.append((here, (z * 4 + (y + step) % 4) * 2))
            pairs.append((here + 1, (((z + step) % 4) * 4 + y) * 2 + 1))
    return pairs


def ring_other(step):
    pairs = []
    for z in range(4):
        for y in range(4):
            here = (z * 4 + y) * 2
            pairs.append((here, (((z + step) % 4) * 4 + y) * 2))
            pairs.append((here + 1, (z * 4 + (y + step) % 4) * 2 + 1))
    return pairs


def pairs_x(step):
    return [(x, x ^ step) for x in range(4)]


def pairs_xy(step):
    return [
        (x * 16 + z * 4 + y, (x ^ (4 - step)) * 16 + z * 4 + (y ^ step))
        for x in range(4)
        for z in range(4)
        for y in range(4)
    ]


SWAP = [(0, 1), (1, 0)]


def place():
    row = lax.axis_index("row")
    return lax.axis_index("pole"), lax.div(row, 4), lax.rem(row, 4), lax.axis_index("col")


def index_of(x, y):
    return x ^ lax.rem(8 - y, 4)


def node_of(m):
    return 3 + 2 * lax.rem(m, 2) + lax.div(m, 2)


def vm():
    return pl.BlockSpec(memory_space=pltpu.VMEM)


def sm():
    return pl.BlockSpec(memory_space=pltpu.SMEM)


def in_hbm():
    return pl.BlockSpec(memory_space=pltpu.HBM)


def hbm():
    return pl.BlockSpec(memory_space=pl.ANY)


def call(kernel, outs, in_specs, out_specs, scratch=(), flops=0, nbytes=0, aliases={}):
    return pl.pallas_call(
        kernel,
        out_shape=outs,
        in_specs=in_specs,
        out_specs=out_specs,
        scratch_shapes=list(scratch),
        input_output_aliases=aliases,
        compiler_params=pltpu.CompilerParams(vmem_limit_bytes=VMEM_LIMIT),
        cost_estimate=pl.CostEstimate(flops=flops, bytes_accessed=nbytes, transcendentals=0),
    )


def shape(*dims, dtype=BF):
    return jax.ShapeDtypeStruct(dims, dtype)


def pack(low, up, dia, widths, pattern, outs, own):
    x, z, y, c = place()
    rows = (32 * (4 * z + y)) + lax.broadcasted_iota(jnp.int32, (32, 256), 0)
    cols = lax.broadcasted_iota(jnp.int32, (32, 256), 1)

    def mask(row_node, col_node, on, half):
        keep = (rows < widths[row_node]) & (cols + 256 * half < widths[col_node]) & (on != 0)
        return jnp.where(keep, 1.0, 0.0).astype(BF)[None]

    @pl.when(c == 0)
    def _():
        h = 0 if own else 1
        for d, out in enumerate(outs):
            k = node_of(index_of(x, lax.rem(y + d, 4)))
            p = lax.div(k - 1, 2)
            at = 2 * (k - 3) + 2
            out[0, h] = dia[p] * mask(p, p, 1, h)
            out[1, h] = low[at] * mask(p, k, pattern[at], h)
            out[2, h] = low[at + 1] * mask(0, k, pattern[at + 1], h)
            out[3, h] = up[at] * mask(k, p, pattern[at], h)
            out[4, h] = up[at + 1] * mask(k, 0, pattern[at + 1], h)
            out[5, h] = dia[k] * mask(k, k, 1, h)

    @pl.when(c == 1)
    def _():
        h = 1 if own else 0
        tiles = [dia[0] * mask(0, 0, 1, h)]
        for i in range(2):
            tiles.append(up[i] * mask(1 + i, 0, pattern[i], h))
            tiles.append(low[i] * mask(0, 1 + i, pattern[i], h))
        for out in outs:
            for t in range(5):
                out[t, h] = tiles[t]


def pack_own_kernel(
    low_in, up_in, dia_in, widths_in, pattern_in, o0, o1, o2, o3, widths, pattern, low, up, dia, sems
):
    run_copies(
        [(low_in, low), (up_in, up), (dia_in, dia), (widths_in, widths), (pattern_in, pattern)],
        sems,
    )
    pack(low, up, dia, widths, pattern, (o0, o1, o2, o3), True)


def pack_other_kernel(low, up, dia, widths, pattern, i0, i1, i2, i3, *outs):
    pack(low, up, dia, widths, pattern, outs, False)


def run_copies(copies, sems):
    made = [pltpu.make_async_copy(s, t, sems.at[i]) for i, (s, t) in enumerate(copies)]
    for m in made:
        m.start()
    for m in made:
        m.wait()


def merge_kernel(b0, b2, b3, b1, near, far, uk, sems):
    x, z, y, c = place()
    p = lax.rem(index_of(x, y), 2)

    @pl.when(c == 0)
    def _():
        copies = []
        for d, buf in enumerate((b0, b1, b2, b3)):
            at = lax.rem(y + 4 - d, 4)
            copies.append((buf.at[pl.ds(0, 3)], near.at[:, :, :, at]))
            copies.append((buf.at[pl.ds(0, 3)], far.at[:, :, :, at]))
            copies.append((buf.at[pl.ds(3, 3)], uk.at[:, :, :, at]))
        run_copies(copies, sems)

    @pl.when(c == 1)
    def _():
        copies = []
        for d, buf in enumerate((b0, b1, b2, b3)):
            at = lax.rem(z + 4 - d, 4)
            copies.append((buf.at[0], near.at[0, :, :, at]))
            copies.append((buf.at[0], far.at[0, :, :, at]))
            copies.append((buf.at[pl.ds(1 + 2 * p, 2)], far.at[pl.ds(1, 2), :, :, at]))
            copies.append((buf.at[pl.ds(3 - 2 * p, 2)], near.at[pl.ds(1, 2), :, :, at]))
        run_copies(copies, sems)


def left_of(pairs):
    real = [jnp.concatenate([r, -i], axis=1) for r, i in pairs]
    imag = [jnp.concatenate([i, r], axis=1) for r, i in pairs]
    return jnp.concatenate(real + imag, axis=0)


def dot(a, b):
    return jnp.dot(a, b, preferred_element_type=F32)


def pairs_of(res, count):
    half = 128 * count
    return [
        (res[128 * i : 128 * i + 128], res[half + 128 * i : half + 128 * i + 128])
        for i in range(count)
    ]


def wide_rows(get):
    return tuple(jnp.concatenate([get(0, part), get(1, part)], axis=1) for part in range(2))


def times(left, count, right):
    got = [pairs_of(dot(left, right[h].reshape(1024, 256)), count) for h in range(2)]
    return [
        tuple(jnp.concatenate([got[0][n][i], got[1][n][i]], axis=1) for i in range(2))
        for n in range(count)
    ]


def put(out, slot, pair, sign=1):
    for i in range(2):
        out[slot, i] = (pair[i] if sign > 0 else -pair[i]).astype(BF)


def first_kernel(r0, r3, r2, r1, uks, out, stay, go, lead, right, sems):
    x, z, y, c = place()

    def rows_of(block):
        return wide_rows(lambda h, part: right[block, h, part, z].reshape(128, 256))

    @pl.when(c == 0)
    def _():
        copies = []
        for d, buf in enumerate((r0, r1, r2, r3)):
            at = lax.rem(z + 4 - d, 4)
            copies.append((buf.at[pl.ds(1, 2), 0], stay.at[:, :, at]))
            copies.append((buf.at[pl.ds(1, 2), 1], go.at[:, :, at]))
            copies.append((buf.at[0], lead.at[:, :, at]))
        run_copies(copies, sems)

    @pl.when(c == 1)
    def _():
        copies = []
        for d, buf in enumerate((r0, r1, r2, r3)):
            copies.append((buf.at[pl.ds(0, 2)], right.at[:, :, :, :, lax.rem(y + 4 - d, 4)]))
        for d, buf in enumerate((r0, r1, r2, r3)):
            copies.append((buf.at[2], go.at[:, :, :, lax.rem(y + 4 - d, 4)]))
        run_copies(copies, sems)
        ukp = wide_rows(lambda h, part: uks[0, h, part].reshape(128, 256))
        uk0 = wide_rows(lambda h, part: uks[1, h, part].reshape(128, 256))
        (kv,) = times(left_of([ukp]), 1, right[1])
        v = tuple((uk0[i].astype(F32) - kv[i]).astype(BF) for i in range(2))
        xk0, xp0 = times(left_of([v, rows_of(1)]), 2, right[0])
        put(out, 0, xp0, -1)
        put(out, 1, rows_of(0))
        put(out, 2, xk0, -1)


def next_kernel(edge, lead, uk, after, out):
    x, z, y, c = place()

    @pl.when(c == 0)
    def _():
        ukp = wide_rows(lambda h, part: uk[0, h, part].reshape(128, 256))
        (kd,) = times(left_of([ukp]), 1, lead)
        put(out, 0, kd)
        put(out, 1, wide_rows(lambda h, part: lead[h, part, z].reshape(128, 256)))


def inner_kernel(stay, go, got, out):
    x, z, y, c = place()

    def work(last, own):
        lp = wide_rows(lambda h, part: last[h, part].reshape(512, 256))
        prod = dot(left_of([lp]), own[0].reshape(1024, 256))
        out[...] = (own[1].reshape(1024, 256).astype(F32) - prod).astype(BF)

    @pl.when(c == 0)
    def _():
        work(got, stay)

    @pl.when(c == 1)
    def _():
        work(go, got)


def last_kernel(
    edge, edge_s, inner, stay, go, got, uk, uks, res, slot0, slot1, slot2, slot3, parts
):
    x, z, y, c = place()
    wr, wi = res[0, 0], res[0, 1]

    def density(re, im):
        return (wr * re.astype(F32) - wi * im.astype(F32)).astype(BF)

    def work(e0, e1, last, own, dk, half):
        cols = slice(256 * half, 256 * half + 256)
        xp0, d0r, xk0 = [(e1[n, 0], e1[n, 1]) for n in range(3)]
        kd, dpr = [(e0[n, 0], e0[n, 1]) for n in range(2)]
        left = left_of([xp0, d0r, xk0])
        pg, og, kg = pairs_of(dot(left, inner[...]), 3)
        pe, oe, ke = pairs_of(dot(left, last[half].reshape(1024, 256)), 3)
        kl, pl_ = pairs_of(dot(left_of([kd, dpr]), own[0].reshape(1024, 256)), 2)
        xkk = [dk[2, half, i].reshape(128, 256).astype(F32) + kl[i] - kg[i] for i in range(2)]
        parts[0] = density(*xkk)
        parts[1] = density(*[-(pl_[i] + pg[i]) for i in range(2)])
        parts[2] = density(-og[0], -og[1])
        parts[3] = density(*[-(kd[i][:, cols].astype(F32) + ke[i]) for i in range(2)])
        parts[4] = density(xk0[0][:, cols], xk0[1][:, cols])

        @pl.when(index_of(x, y) < 2)
        def _():
            parts[5] = density(d0r[0][:, cols], d0r[1][:, cols])
            parts[6] = density(*[dpr[i][:, cols].astype(F32) - pe[i] for i in range(2)])

        @pl.when(index_of(x, y) >= 2)
        def _():
            parts[5] = density(xp0[0][:, cols], xp0[1][:, cols])
            parts[6] = density(-oe[0], -oe[1])

    @pl.when(c == 0)
    def _():
        work(edge, edge_s, got, stay, uk, 0)

    @pl.when(c == 1)
    def _():
        work(edge_s, edge, go, got, uks, 1)

    for d, out in enumerate((slot0, slot1, slot2, slot3)):
        at = pl.multiple_of(32 * (y ^ d), 32)
        for b in range(7):
            out[b] = parts[b, pl.ds(at, 32), :]


def sum_kernel(a0, a1, a2, a3, out):
    total = a0[...].astype(F32) + a1[...].astype(F32)
    out[...] = (total + (a2[...].astype(F32) + a3[...].astype(F32))).astype(BF)


def final_kernel(g0, g1, g3, g2, out):
    x, z, y, c = place()
    for d, g in enumerate((g0, g1, g2, g3)):
        b = index_of(x ^ d, y)
        k = node_of(b)
        p = 1 + lax.rem(b, 2)
        pair = 2 * (k - 3) + 2
        low = b < 2
        out[k] = g[0].astype(F32)
        out[7 + pair] = g[1].astype(F32)
        out[8 + pair] = g[2].astype(F32)
        out[17 + pair] = g[3].astype(F32)
        out[18 + pair] = g[4].astype(F32)
        out[jnp.where(low, p, 6 + p)] = g[6].astype(F32)

        @pl.when(b != 1)
        def _():
            out[jnp.where(low, 0, 16 + p)] = g[5].astype(F32)


def body(lower_factor, upper_factor, diag_inverse, residues, widths, pattern):
    mine = (lower_factor[0], upper_factor[0], diag_inverse[0])
    swapped = [lax.ppermute(a, "col", SWAP) for a in mine]
    grid = ("row", "col")
    *bufs, widths, pattern = call(
        pack_own_kernel,
        [shape(6, 2, 2, 32, 256)] * 4 + [shape(7, dtype=jnp.int32), shape(10, dtype=jnp.int32)],
        [in_hbm()] * 5,
        [vm()] * 4 + [sm()] * 2,
        [
            pltpu.VMEM((10, 2, 32, 256), BF),
            pltpu.VMEM((10, 2, 32, 256), BF),
            pltpu.VMEM((7, 2, 32, 256), BF),
            pltpu.SemaphoreType.DMA((5,)),
        ],
        nbytes=4 << 20,
    )(*[pltpu.with_memory_space_constraint(a, pltpu.HBM) for a in (*mine, widths, pattern)])
    bufs = call(
        pack_other_kernel,
        [shape(6, 2, 2, 32, 256)] * 4,
        [vm()] * 3 + [sm()] * 2 + [hbm()] * 4,
        [vm()] * 4,
        nbytes=4 << 20,
        aliases={5: 0, 6: 1, 7: 2, 8: 3},
    )(*swapped, widths, pattern, *bufs)
    came = {d: lax.ppermute(bufs[d], grid, ring_both(d)) for d in (1, 3, 2)}
    near, far, uk = call(
        merge_kernel,
        [shape(3, 2, 2, 4, 32, 256)] * 3,
        [hbm()] * 4,
        [hbm()] * 3,
        [pltpu.SemaphoreType.DMA((16,))],
        nbytes=4 << 20,
    )(bufs[0], came[2], came[3], came[1])
    came = {d: lax.ppermute(near, grid, ring_other(d)) for d in (1, 3)}
    came[2] = lax.ppermute(far, grid, ring_other(2))
    uks = lax.ppermute(uk, "col", SWAP)
    blocks = (far, came[3], came[2], came[1])
    edge, stay, go, lead = call(
        first_kernel,
        [shape(3, 2, 128, 512)] + [shape(2, 2, 4, 4, 32, 256)] * 3,
        [hbm()] * 4 + [vm()],
        [vm()] + [hbm()] * 3,
        [pltpu.VMEM((2, 2, 2, 4, 4, 32, 256), BF), pltpu.SemaphoreType.DMA((12,))],
        flops=805306368,
        nbytes=4 << 20,
    )(*blocks, uks)
    got = lax.ppermute(go, "col", SWAP)
    edge = call(
        next_kernel,
        [shape(3, 2, 128, 512)],
        [hbm()] + [vm()] * 2 + [hbm()],
        [vm()],
        flops=268435456,
        nbytes=2 << 20,
        aliases={0: 0},
    )(edge, lead, uk, stay)[0]
    edge_s = lax.ppermute(edge, "col", SWAP)
    inner = call(
        inner_kernel,
        [shape(1024, 256)],
        [vm()] * 3,
        [vm()],
        flops=536870912,
        nbytes=3 << 20,
    )(stay, go, got)[0]
    slots = call(
        last_kernel,
        [shape(7, 32, 256)] * 4,
        [vm()] * 8 + [sm()],
        [vm()] * 4,
        [pltpu.VMEM((7, 128, 256), BF)],
        flops=1073741824,
        nbytes=4 << 20,
    )(edge, edge_s, inner, stay, go, got, uk, uks, residues)
    at_x = [slots[0]] + [lax.ppermute(slots[d], ("pole", "row"), pairs_xy(d)) for d in (2, 3, 1)]
    total = call(sum_kernel, [shape(7, 32, 256)], [vm()] * 4, [vm()], nbytes=1 << 20)(*at_x)[0]
    full = [total] + [lax.ppermute(total, "pole", pairs_x(d)) for d in (1, 3, 2)]
    return call(
        final_kernel, [shape(27, 32, 256, dtype=F32)], [vm()] * 4, [vm()], nbytes=2 << 20
    )(*full)[0]


def solution(mesh):
    return jax.shard_map(
        body,
        mesh=mesh,
        in_specs=(
            P("pole", None, None, "row", "col"),
            P("pole", None, None, "row", "col"),
            P("pole", None, None, "row", "col"),
            P("pole", None),
            P(),
            P(),
        ),
        out_specs=P(None, "row", "col"),
        check_vma=False,
    )
```

```python
import jax
import jax.numpy as jnp
from jax import lax
from jax.experimental import pallas as pl
from jax.experimental.pallas import tpu as pltpu
from jax.sharding import PartitionSpec as P

BF = jnp.bfloat16
F32 = jnp.float32
VMEM_LIMIT = 24 * 1024 * 1024


def ring_both(step):
    pairs = []
    for z in range(4):
        for y in range(4):
            here = (z * 4 + y) * 2
            pairs.append((here, (z * 4 + (y + step) % 4) * 2))
            pairs.append((here + 1, (((z + step) % 4) * 4 + y) * 2 + 1))
    return pairs


def ring_other(step):
    pairs = []
    for z in range(4):
        for y in range(4):
            here = (z * 4 + y) * 2
            pairs.append((here, (((z + step) % 4) * 4 + y) * 2))
            pairs.append((here + 1, (z * 4 + (y + step) % 4) * 2 + 1))
    return pairs


def pairs_x(step):
    return [(x, x ^ step) for x in range(4)]


def pairs_xy(step):
    return [
        (x * 16 + z * 4 + y, (x ^ (4 - step)) * 16 + z * 4 + (y ^ step))
        for x in range(4)
        for z in range(4)
        for y in range(4)
    ]


SWAP = [(0, 1), (1, 0)]


def place():
    row = lax.axis_index("row")
    return lax.axis_index("pole"), lax.div(row, 4), lax.rem(row, 4), lax.axis_index("col")


def index_of(x, y):
    return x ^ lax.rem(8 - y, 4)


def node_of(m):
    return 3 + 2 * lax.rem(m, 2) + lax.div(m, 2)


def vm():
    return pl.BlockSpec(memory_space=pltpu.VMEM)


def sm():
    return pl.BlockSpec(memory_space=pltpu.SMEM)


def in_hbm():
    return pl.BlockSpec(memory_space=pltpu.HBM)


def hbm():
    return pl.BlockSpec(memory_space=pl.ANY)


def call(kernel, outs, in_specs, out_specs, scratch=(), flops=0, nbytes=0, aliases={}):
    return pl.pallas_call(
        kernel,
        out_shape=outs,
        in_specs=in_specs,
        out_specs=out_specs,
        scratch_shapes=list(scratch),
        input_output_aliases=aliases,
        compiler_params=pltpu.CompilerParams(vmem_limit_bytes=VMEM_LIMIT),
        cost_estimate=pl.CostEstimate(flops=flops, bytes_accessed=nbytes, transcendentals=0),
    )


def shape(*dims, dtype=BF):
    return jax.ShapeDtypeStruct(dims, dtype)


def pack(low, up, dia, widths, pattern, outs, own):
    x, z, y, c = place()
    rows = (32 * (4 * z + y)) + lax.broadcasted_iota(jnp.int32, (32, 256), 0)
    cols = lax.broadcasted_iota(jnp.int32, (32, 256), 1)

    def mask(row_node, col_node, on, half):
        keep = (rows < widths[row_node]) & (cols + 256 * half < widths[col_node]) & (on != 0)
        return jnp.where(keep, 1.0, 0.0).astype(BF)[None]

    @pl.when(c == 0)
    def _():
        h = 0 if own else 1
        for d, out in enumerate(outs):
            k = node_of(index_of(x, lax.rem(y + d, 4)))
            p = lax.div(k - 1, 2)
            at = 2 * (k - 3) + 2
            out[0, h] = dia[p] * mask(p, p, 1, h)
            out[1, h] = low[at] * mask(p, k, pattern[at], h)
            out[2, h] = low[at + 1] * mask(0, k, pattern[at + 1], h)
            out[3, h] = up[at] * mask(k, p, pattern[at], h)
            out[4, h] = up[at + 1] * mask(k, 0, pattern[at + 1], h)

    @pl.when(c == 1)
    def _():
        h = 1 if own else 0
        tiles = [dia[0] * mask(0, 0, 1, h)]
        for i in range(2):
            tiles.append(up[i] * mask(1 + i, 0, pattern[i], h))
            tiles.append(low[i] * mask(0, 1 + i, pattern[i], h))
        for out in outs:
            for t in range(5):
                out[t, h] = tiles[t]


def pack_own_kernel(low_in, up_in, dia_in, widths_in, pattern_in, res_in, *refs):
    outs, parts, (widths, pattern, low, up, dia, res, sems) = refs[:4], refs[4:8], refs[8:]
    run_copies(
        [
            (low_in, low),
            (up_in, up),
            (dia_in, dia),
            (widths_in, widths),
            (pattern_in, pattern),
            (res_in, res),
        ],
        sems,
    )
    pack(low, up, dia, widths, pattern, outs, True)
    x, z, y, c = place()
    rows = (32 * (4 * z + y)) + lax.broadcasted_iota(jnp.int32, (32, 256), 0)
    cols = (256 * c) + lax.broadcasted_iota(jnp.int32, (32, 256), 1)
    for d, part in enumerate(parts):
        k = node_of(index_of(x ^ d, y))
        dens = res[0, 0] * dia[k, 0].astype(F32) - res[0, 1] * dia[k, 1].astype(F32)
        part[...] = jnp.where((rows < widths[k]) & (cols < widths[k]), dens, 0.0).astype(BF)


def pack_other_kernel(low, up, dia, widths, pattern, i0, i1, i2, i3, *outs):
    pack(low, up, dia, widths, pattern, outs, False)


def run_copies(copies, sems):
    made = [pltpu.make_async_copy(s, t, sems.at[i]) for i, (s, t) in enumerate(copies)]
    for m in made:
        m.start()
    for m in made:
        m.wait()


def merge_kernel(b0, b2, b3, b1, near, far, uk, sems):
    x, z, y, c = place()
    p = lax.rem(index_of(x, y), 2)

    @pl.when(c == 0)
    def _():
        copies = []
        for d, buf in enumerate((b0, b1, b2, b3)):
            at = lax.rem(y + 4 - d, 4)
            copies.append((buf.at[pl.ds(0, 3)], near.at[:, :, :, at]))
            copies.append((buf.at[pl.ds(0, 3)], far.at[:, :, :, at]))
            copies.append((buf.at[pl.ds(3, 2)], uk.at[:, :, :, at]))
        run_copies(copies, sems)

    @pl.when(c == 1)
    def _():
        copies = []
        for d, buf in enumerate((b0, b1, b2, b3)):
            at = lax.rem(z + 4 - d, 4)
            copies.append((buf.at[0], near.at[0, :, :, at]))
            copies.append((buf.at[0], far.at[0, :, :, at]))
            copies.append((buf.at[pl.ds(1 + 2 * p, 2)], far.at[pl.ds(1, 2), :, :, at]))
            copies.append((buf.at[pl.ds(3 - 2 * p, 2)], near.at[pl.ds(1, 2), :, :, at]))
        run_copies(copies, sems)


def left_of(pairs):
    real = [jnp.concatenate([r, -i], axis=1) for r, i in pairs]
    imag = [jnp.concatenate([i, r], axis=1) for r, i in pairs]
    return jnp.concatenate(real + imag, axis=0)


def dot(a, b):
    return jnp.dot(a, b, preferred_element_type=F32)


def pairs_of(res, count):
    half = 128 * count
    return [
        (res[128 * i : 128 * i + 128], res[half + 128 * i : half + 128 * i + 128])
        for i in range(count)
    ]


def wide_rows(get):
    return tuple(jnp.concatenate([get(0, part), get(1, part)], axis=1) for part in range(2))


def times(left, count, right):
    got = [pairs_of(dot(left, right[h].reshape(1024, 256)), count) for h in range(2)]
    return [
        tuple(jnp.concatenate([got[0][n][i], got[1][n][i]], axis=1) for i in range(2))
        for n in range(count)
    ]


def put(out, slot, pair, sign=1):
    for i in range(2):
        out[slot, i] = (pair[i] if sign > 0 else -pair[i]).astype(BF)


def first_kernel(r0, r3, r2, r1, uks, p2, p3, p1, out, stay, go, lead, right, sems):
    x, z, y, c = place()

    def rows_of(block):
        return wide_rows(lambda h, part: right[block, h, part, z].reshape(128, 256))

    @pl.when(c == 0)
    def _():
        copies = []
        for d, buf in enumerate((r0, r1, r2, r3)):
            at = lax.rem(z + 4 - d, 4)
            copies.append((buf.at[pl.ds(1, 2), 0], stay.at[:, :, at]))
            copies.append((buf.at[pl.ds(1, 2), 1], go.at[:, :, at]))
            copies.append((buf.at[0], lead.at[:, :, at]))
        run_copies(copies, sems)

    @pl.when(c == 1)
    def _():
        copies = []
        for d, buf in enumerate((r0, r1, r2, r3)):
            copies.append((buf.at[pl.ds(0, 2)], right.at[:, :, :, :, lax.rem(y + 4 - d, 4)]))
        for d, buf in enumerate((r0, r1, r2, r3)):
            copies.append((buf.at[2], go.at[:, :, :, lax.rem(y + 4 - d, 4)]))
        run_copies(copies, sems)
        ukp = wide_rows(lambda h, part: uks[0, h, part].reshape(128, 256))
        uk0 = wide_rows(lambda h, part: uks[1, h, part].reshape(128, 256))
        (kv,) = times(left_of([ukp]), 1, right[1])
        v = tuple((uk0[i].astype(F32) - kv[i]).astype(BF) for i in range(2))
        xk0, xp0 = times(left_of([v, rows_of(1)]), 2, right[0])
        put(out, 0, xp0, -1)
        put(out, 1, rows_of(0))
        put(out, 2, xk0, -1)


def next_kernel(edge, lead, uk, after, out):
    x, z, y, c = place()

    @pl.when(c == 0)
    def _():
        ukp = wide_rows(lambda h, part: uk[0, h, part].reshape(128, 256))
        (kd,) = times(left_of([ukp]), 1, lead)
        put(out, 0, kd)
        put(out, 1, wide_rows(lambda h, part: lead[h, part, z].reshape(128, 256)))


def inner_kernel(stay, go, got, out):
    x, z, y, c = place()

    def work(last, own):
        lp = wide_rows(lambda h, part: last[h, part].reshape(512, 256))
        prod = dot(left_of([lp]), own[0].reshape(1024, 256))
        out[...] = (own[1].reshape(1024, 256).astype(F32) - prod).astype(BF)

    @pl.when(c == 0)
    def _():
        work(got, stay)

    @pl.when(c == 1)
    def _():
        work(go, got)


def last_kernel(
    edge, edge_s, inner, stay, go, got, res, slot0, slot1, slot2, slot3, parts
):
    x, z, y, c = place()
    wr, wi = res[0, 0], res[0, 1]

    def density(re, im):
        return (wr * re.astype(F32) - wi * im.astype(F32)).astype(BF)

    def work(e0, e1, last, own, half):
        cols = slice(256 * half, 256 * half + 256)
        xp0, d0r, xk0 = [(e1[n, 0], e1[n, 1]) for n in range(3)]
        kd, dpr = [(e0[n, 0], e0[n, 1]) for n in range(2)]
        left = left_of([xp0, d0r, xk0])
        pg, og, kg = pairs_of(dot(left, inner[...]), 3)
        pe, oe, ke = pairs_of(dot(left, last[half].reshape(1024, 256)), 3)
        kl, pl_ = pairs_of(dot(left_of([kd, dpr]), own[0].reshape(1024, 256)), 2)
        parts[0] = density(*[kl[i] - kg[i] for i in range(2)])
        parts[1] = density(*[-(pl_[i] + pg[i]) for i in range(2)])
        parts[2] = density(-og[0], -og[1])
        parts[3] = density(*[-(kd[i][:, cols].astype(F32) + ke[i]) for i in range(2)])
        parts[4] = density(xk0[0][:, cols], xk0[1][:, cols])

        @pl.when(index_of(x, y) < 2)
        def _():
            parts[5] = density(d0r[0][:, cols], d0r[1][:, cols])
            parts[6] = density(*[dpr[i][:, cols].astype(F32) - pe[i] for i in range(2)])

        @pl.when(index_of(x, y) >= 2)
        def _():
            parts[5] = density(xp0[0][:, cols], xp0[1][:, cols])
            parts[6] = density(-oe[0], -oe[1])

    @pl.when(c == 0)
    def _():
        work(edge, edge_s, got, stay, 0)

    @pl.when(c == 1)
    def _():
        work(edge_s, edge, go, got, 1)

    for d, out in enumerate((slot0, slot1, slot2, slot3)):
        at = pl.multiple_of(32 * (y ^ d), 32)
        for b in range(7):
            out[b] = parts[b, pl.ds(at, 32), :]


def sum_kernel(a0, a1, a2, a3, d0, d1, d2, d3, out):
    total = a0[...].astype(F32) + a1[...].astype(F32)
    total = total + (a2[...].astype(F32) + a3[...].astype(F32))
    diag = d0[...].astype(F32) + d1[...].astype(F32) + d2[...].astype(F32) + d3[...].astype(F32)
    out[0] = (total[0] + diag).astype(BF)
    out[1:] = total[1:].astype(BF)


def final_kernel(g0, g1, g3, g2, out):
    x, z, y, c = place()
    for d, g in enumerate((g0, g1, g2, g3)):
        b = index_of(x ^ d, y)
        k = node_of(b)
        p = 1 + lax.rem(b, 2)
        pair = 2 * (k - 3) + 2
        low = b < 2
        out[k] = g[0].astype(F32)
        out[7 + pair] = g[1].astype(F32)
        out[8 + pair] = g[2].astype(F32)
        out[17 + pair] = g[3].astype(F32)
        out[18 + pair] = g[4].astype(F32)
        out[jnp.where(low, p, 6 + p)] = g[6].astype(F32)

        @pl.when(b != 1)
        def _():
            out[jnp.where(low, 0, 16 + p)] = g[5].astype(F32)


def body(lower_factor, upper_factor, diag_inverse, residues, widths, pattern):
    mine = (lower_factor[0], upper_factor[0], diag_inverse[0])
    swapped = [lax.ppermute(a, "col", SWAP) for a in mine]
    grid = ("row", "col")
    *bufs, widths, pattern = call(
        pack_own_kernel,
        [shape(5, 2, 2, 32, 256)] * 4
        + [shape(32, 256)] * 4
        + [shape(7, dtype=jnp.int32), shape(10, dtype=jnp.int32)],
        [in_hbm()] * 6,
        [vm()] * 8 + [sm()] * 2,
        [
            pltpu.VMEM((10, 2, 32, 256), BF),
            pltpu.VMEM((10, 2, 32, 256), BF),
            pltpu.VMEM((7, 2, 32, 256), BF),
            pltpu.SMEM((1, 2), F32),
            pltpu.SemaphoreType.DMA((6,)),
        ],
        nbytes=4 << 20,
    )(*[pltpu.with_memory_space_constraint(a, pltpu.HBM) for a in (*mine, widths, pattern, residues)])
    bufs, parts = bufs[:4], bufs[4:]
    bufs = call(
        pack_other_kernel,
        [shape(5, 2, 2, 32, 256)] * 4,
        [vm()] * 3 + [sm()] * 2 + [hbm()] * 4,
        [vm()] * 4,
        nbytes=4 << 20,
        aliases={5: 0, 6: 1, 7: 2, 8: 3},
    )(*swapped, widths, pattern, *bufs)
    came = {d: lax.ppermute(bufs[d], grid, ring_both(d)) for d in (1, 3, 2)}
    parts = [parts[0]] + [lax.ppermute(parts[d], "pole", pairs_x(d)) for d in (2, 3, 1)]
    near, far, uk = call(
        merge_kernel,
        [shape(3, 2, 2, 4, 32, 256)] * 2 + [shape(2, 2, 2, 4, 32, 256)],
        [hbm()] * 4,
        [hbm()] * 3,
        [pltpu.SemaphoreType.DMA((16,))],
        nbytes=4 << 20,
    )(bufs[0], came[2], came[3], came[1])
    came = {d: lax.ppermute(near, grid, ring_other(d)) for d in (1, 3)}
    came[2] = lax.ppermute(far, grid, ring_other(2))
    uks = lax.ppermute(uk, "col", SWAP)
    blocks = (far, came[3], came[2], came[1])
    edge, stay, go, lead = call(
        first_kernel,
        [shape(3, 2, 128, 512)] + [shape(2, 2, 4, 4, 32, 256)] * 3,
        [hbm()] * 4 + [vm()] + [hbm()] * 3,
        [vm()] + [hbm()] * 3,
        [pltpu.VMEM((2, 2, 2, 4, 4, 32, 256), BF), pltpu.SemaphoreType.DMA((12,))],
        flops=805306368,
        nbytes=4 << 20,
    )(*blocks, uks, *parts[1:])
    got = lax.ppermute(go, "col", SWAP)
    edge = call(
        next_kernel,
        [shape(3, 2, 128, 512)],
        [hbm()] + [vm()] * 2 + [hbm()],
        [vm()],
        flops=268435456,
        nbytes=2 << 20,
        aliases={0: 0},
    )(edge, lead, uk, stay)[0]
    edge_s = lax.ppermute(edge, "col", SWAP)
    inner = call(
        inner_kernel,
        [shape(1024, 256)],
        [vm()] * 3,
        [vm()],
        flops=536870912,
        nbytes=3 << 20,
    )(stay, go, got)[0]
    slots = call(
        last_kernel,
        [shape(7, 32, 256)] * 4,
        [vm()] * 6 + [sm()],
        [vm()] * 4,
        [pltpu.VMEM((7, 128, 256), BF)],
        flops=1073741824,
        nbytes=4 << 20,
    )(edge, edge_s, inner, stay, go, got, residues)
    at_x = [slots[0]] + [lax.ppermute(slots[d], ("pole", "row"), pairs_xy(d)) for d in (2, 3, 1)]
    total = call(sum_kernel, [shape(7, 32, 256)], [vm()] * 8, [vm()], nbytes=1 << 20)(
        *at_x, *parts
    )[0]
    full = [total] + [lax.ppermute(total, "pole", pairs_x(d)) for d in (1, 3, 2)]
    return call(
        final_kernel, [shape(27, 32, 256, dtype=F32)], [vm()] * 4, [vm()], nbytes=2 << 20
    )(*full)[0]


def solution(mesh):
    return jax.shard_map(
        body,
        mesh=mesh,
        in_specs=(
            P("pole", None, None, "row", "col"),
            P("pole", None, None, "row", "col"),
            P("pole", None, None, "row", "col"),
            P("pole", None),
            P(),
            P(),
        ),
        out_specs=P(None, "row", "col"),
        check_vma=False,
    )
```

```python
import jax
import jax.numpy as jnp
from jax import lax
from jax.experimental import pallas as pl
from jax.experimental.pallas import tpu as pltpu
from jax.sharding import PartitionSpec as P

BF = jnp.bfloat16
F32 = jnp.float32
VMEM_LIMIT = 24 * 1024 * 1024


def ring_both(step):
    pairs = []
    for z in range(4):
        for y in range(4):
            here = (z * 4 + y) * 2
            pairs.append((here, (z * 4 + (y + step) % 4) * 2))
            pairs.append((here + 1, (((z + step) % 4) * 4 + y) * 2 + 1))
    return pairs


def ring_other(step):
    pairs = []
    for z in range(4):
        for y in range(4):
            here = (z * 4 + y) * 2
            pairs.append((here, (((z + step) % 4) * 4 + y) * 2))
            pairs.append((here + 1, (z * 4 + (y + step) % 4) * 2 + 1))
    return pairs


def pairs_x(step):
    return [(x, x ^ step) for x in range(4)]


def pairs_xy(step):
    return [
        (x * 16 + z * 4 + y, (x ^ (4 - step)) * 16 + z * 4 + (y ^ step))
        for x in range(4)
        for z in range(4)
        for y in range(4)
    ]


SWAP = [(0, 1), (1, 0)]


def place():
    row = lax.axis_index("row")
    return lax.axis_index("pole"), lax.div(row, 4), lax.rem(row, 4), lax.axis_index("col")


def index_of(x, y):
    return x ^ lax.rem(8 - y, 4)


def node_of(m):
    return 3 + 2 * lax.rem(m, 2) + lax.div(m, 2)


def vm():
    return pl.BlockSpec(memory_space=pltpu.VMEM)


def sm():
    return pl.BlockSpec(memory_space=pltpu.SMEM)


def in_hbm():
    return pl.BlockSpec(memory_space=pltpu.HBM)


def hbm():
    return pl.BlockSpec(memory_space=pl.ANY)


def call(kernel, outs, in_specs, out_specs, scratch=(), flops=0, nbytes=0, aliases={}):
    return pl.pallas_call(
        kernel,
        out_shape=outs,
        in_specs=in_specs,
        out_specs=out_specs,
        scratch_shapes=list(scratch),
        input_output_aliases=aliases,
        compiler_params=pltpu.CompilerParams(vmem_limit_bytes=VMEM_LIMIT),
        cost_estimate=pl.CostEstimate(flops=flops, bytes_accessed=nbytes, transcendentals=0),
    )


def shape(*dims, dtype=BF):
    return jax.ShapeDtypeStruct(dims, dtype)


def pack(low, up, dia, widths, pattern, outs, own):
    x, z, y, c = place()
    rows = (32 * (4 * z + y)) + lax.broadcasted_iota(jnp.int32, (32, 256), 0)
    cols = lax.broadcasted_iota(jnp.int32, (32, 256), 1)

    def mask(row_node, col_node, on, half):
        keep = (rows < widths[row_node]) & (cols + 256 * half < widths[col_node]) & (on != 0)
        return jnp.where(keep, 1.0, 0.0).astype(BF)[None]

    @pl.when(c == 0)
    def _():
        h = 0 if own else 1
        for d, out in enumerate(outs):
            k = node_of(index_of(x, lax.rem(y + d, 4)))
            p = lax.div(k - 1, 2)
            at = 2 * (k - 3) + 2
            out[0, h] = dia[p] * mask(p, p, 1, h)
            out[1, h] = low[at] * mask(p, k, pattern[at], h)
            out[2, h] = low[at + 1] * mask(0, k, pattern[at + 1], h)
            out[3, h] = up[at] * mask(k, p, pattern[at], h)
            out[4, h] = up[at + 1] * mask(k, 0, pattern[at + 1], h)

    @pl.when(c == 1)
    def _():
        h = 1 if own else 0
        tiles = [dia[0] * mask(0, 0, 1, h)]
        for i in range(2):
            tiles.append(up[i] * mask(1 + i, 0, pattern[i], h))
            tiles.append(low[i] * mask(0, 1 + i, pattern[i], h))
        for out in outs:
            for t in range(5):
                out[t, h] = tiles[t]


def pack_own_kernel(low_in, up_in, dia_in, widths_in, pattern_in, res_in, *refs):
    outs, parts, (widths, pattern, res, low, up, dia, sems) = refs[:4], refs[4:8], refs[8:]
    run_copies(
        [
            (low_in, low),
            (up_in, up),
            (dia_in, dia),
            (widths_in, widths),
            (pattern_in, pattern),
            (res_in, res),
        ],
        sems,
    )
    pack(low, up, dia, widths, pattern, outs, True)
    x, z, y, c = place()
    rows = (32 * (4 * z + y)) + lax.broadcasted_iota(jnp.int32, (32, 256), 0)
    cols = (256 * c) + lax.broadcasted_iota(jnp.int32, (32, 256), 1)
    for d, part in enumerate(parts):
        k = node_of(index_of(x ^ d, y))
        dens = res[0, 0] * dia[k, 0].astype(F32) - res[0, 1] * dia[k, 1].astype(F32)
        part[...] = jnp.where((rows < widths[k]) & (cols < widths[k]), dens, 0.0).astype(BF)


def pack_other_kernel(low, up, dia, widths, pattern, i0, i1, i2, i3, *outs):
    pack(low, up, dia, widths, pattern, outs, False)


def run_copies(copies, sems):
    made = [pltpu.make_async_copy(s, t, sems.at[i]) for i, (s, t) in enumerate(copies)]
    for m in made:
        m.start()
    for m in made:
        m.wait()


def merge_kernel(b0, b2, b3, b1, near, far, uk, sems):
    x, z, y, c = place()
    p = lax.rem(index_of(x, y), 2)

    @pl.when(c == 0)
    def _():
        copies = []
        for d, buf in enumerate((b0, b1, b2, b3)):
            at = lax.rem(y + 4 - d, 4)
            copies.append((buf.at[pl.ds(0, 3)], near.at[:, :, :, at]))
            copies.append((buf.at[pl.ds(0, 3)], far.at[:, :, :, at]))
            copies.append((buf.at[pl.ds(3, 2)], uk.at[:, :, :, at]))
        run_copies(copies, sems)

    @pl.when(c == 1)
    def _():
        copies = []
        for d, buf in enumerate((b0, b1, b2, b3)):
            at = lax.rem(z + 4 - d, 4)
            copies.append((buf.at[0], near.at[0, :, :, at]))
            copies.append((buf.at[0], far.at[0, :, :, at]))
            copies.append((buf.at[pl.ds(1 + 2 * p, 2)], far.at[pl.ds(1, 2), :, :, at]))
            copies.append((buf.at[pl.ds(3 - 2 * p, 2)], near.at[pl.ds(1, 2), :, :, at]))
        run_copies(copies, sems)


def left_of(pairs):
    real = [jnp.concatenate([r, -i], axis=1) for r, i in pairs]
    imag = [jnp.concatenate([i, r], axis=1) for r, i in pairs]
    return jnp.concatenate(real + imag, axis=0)


def dot(a, b):
    return jnp.dot(a, b, preferred_element_type=F32)


def pairs_of(res, count):
    half = 128 * count
    return [
        (res[128 * i : 128 * i + 128], res[half + 128 * i : half + 128 * i + 128])
        for i in range(count)
    ]


def wide_rows(get):
    return tuple(jnp.concatenate([get(0, part), get(1, part)], axis=1) for part in range(2))


def times(left, count, right):
    got = [pairs_of(dot(left, right[h].reshape(1024, 256)), count) for h in range(2)]
    return [
        tuple(jnp.concatenate([got[0][n][i], got[1][n][i]], axis=1) for i in range(2))
        for n in range(count)
    ]


def put(out, pair, sign=1):
    for i in range(2):
        out[i] = (pair[i] if sign > 0 else -pair[i]).astype(BF)


def early_kernel(r0, r2, p2, p3, p1, go, sems):
    x, z, y, c = place()
    part_of_last(((0, r0), (2, r2)), go, sems)


def part_of_last(given, go, sems):
    x, z, y, c = place()

    @pl.when(c == 0)
    def _():
        copies = []
        for d, buf in given:
            at = lax.div(lax.rem(z + 4 - d, 4), 2)
            copies.append((buf.at[pl.ds(1, 2), 1], go.at[:, :, at]))
        run_copies(copies, sems)

    @pl.when(c == 1)
    def _():
        copies = []
        for d, buf in given:
            at = lax.div(lax.rem(y + 4 - d, 4), 2)
            copies.append((buf.at[2], go.at[:, :, at]))
        run_copies(copies, sems)


def first_kernel(
    r0, r3, r2, r1, uks, before, out0, out1, out2, stay, go, lead, right, sems
):
    x, z, y, c = place()
    part_of_last(((1, r1), (3, r3)), go, sems)

    def rows_of(block):
        return wide_rows(lambda h, part: right[block, h, part, z].reshape(128, 256))

    @pl.when(c == 0)
    def _():
        copies = []
        for d, buf in enumerate((r0, r1, r2, r3)):
            at = lax.rem(z + 4 - d, 4)
            copies.append((buf.at[pl.ds(1, 2), 0], stay.at[:, :, at]))
            copies.append((buf.at[0], lead.at[:, :, at]))
        run_copies(copies, sems)

    @pl.when(c == 1)
    def _():
        copies = []
        for d, buf in enumerate((r0, r1, r2, r3)):
            at = lax.rem(y + 4 - d, 4)
            copies.append((buf.at[pl.ds(0, 2)], right.at[:, :, :, :, at]))
            copies.append((buf.at[2], stay.at[:, :, :, at]))
        run_copies(copies, sems)
        ukp = wide_rows(lambda h, part: uks[0, h, part].reshape(128, 256))
        uk0 = wide_rows(lambda h, part: uks[1, h, part].reshape(128, 256))
        (kv,) = times(left_of([ukp]), 1, right[1])
        v = tuple((uk0[i].astype(F32) - kv[i]).astype(BF) for i in range(2))
        xk0, xp0 = times(left_of([v, rows_of(1)]), 2, right[0])
        put(out0, xp0, -1)
        put(out1, rows_of(0))
        put(out2, xk0, -1)


def next_kernel(edge0, edge1, lead, uk, after, out0, out1):
    x, z, y, c = place()

    @pl.when(c == 0)
    def _():
        ukp = wide_rows(lambda h, part: uk[0, h, part].reshape(128, 256))
        (kd,) = times(left_of([ukp]), 1, lead)
        put(out0, kd)
        put(out1, wide_rows(lambda h, part: lead[h, part, z].reshape(128, 256)))


def inner_kernel(edge0, edge1, edge2, stay, got_a, got_b, out, early, other, sems):
    x, z, y, c = place()

    def work(last, own):
        lp = wide_rows(lambda h, part: last[h, part].reshape(512, 256))
        prod = dot(left_of([lp]), own[0].reshape(1024, 256))
        out[...] = (own[1].reshape(1024, 256).astype(F32) - prod).astype(BF)

    @pl.when(c == 0)
    def _():
        copies = []
        for buf, low in ((got_a, lax.rem(y, 2)), (got_b, 1 - lax.rem(y, 2))):
            for n in range(2):
                copies.append((buf.at[:, :, n], other.at[:, :, :, 2 * n + low]))
        run_copies(copies, sems)
        work(other, stay)
        left = left_of([(e[0], e[1]) for e in (edge0, edge1)])
        early[0:512] = dot(left, stay[0].reshape(1024, 256))

    @pl.when(c == 1)
    def _():
        copies = []
        for buf, low in ((got_a, lax.rem(z, 2)), (got_b, 1 - lax.rem(z, 2))):
            for n in range(2):
                copies.append((buf.at[:, :, n], other.at[:, :, 2 * n + low]))
        run_copies(copies, sems)
        work(stay, other)
        left = left_of([(e[0], e[1]) for e in (edge0, edge1, edge2)])
        early[...] = dot(left, stay[1].reshape(1024, 256))


def last_kernel(
    edge0, edge1, edge2, swap0, swap1, swap2, inner, early, got, res,
    slot0, slot1, slot2, slot3, parts,
):
    edge, edge_s = (edge0, edge1, edge2), (swap0, swap1, swap2)
    x, z, y, c = place()
    wr, wi = res[0, 0], res[0, 1]

    def density(re, im):
        return (wr * re.astype(F32) - wi * im.astype(F32)).astype(BF)

    def work(e0, e1, half):
        cols = slice(256 * half, 256 * half + 256)
        xp0, d0r, xk0 = [(e1[n][0], e1[n][1]) for n in range(3)]
        kd, dpr = [(e0[n][0], e0[n][1]) for n in range(2)]
        left = left_of([xp0, d0r, xk0])
        pg, og, kg = pairs_of(dot(left, inner[...]), 3)
        if half == 0:
            pe, oe, ke = pairs_of(dot(left, got[0].reshape(1024, 256)), 3)
            kl, pl_ = pairs_of(early[0:512], 2)
        else:
            pe, oe, ke = pairs_of(early[...], 3)
            kl, pl_ = pairs_of(dot(left_of([kd, dpr]), got[0].reshape(1024, 256)), 2)
        parts[0] = density(*[kl[i] - kg[i] for i in range(2)])
        parts[1] = density(*[-(pl_[i] + pg[i]) for i in range(2)])
        parts[2] = density(-og[0], -og[1])
        parts[3] = density(*[-(kd[i][:, cols].astype(F32) + ke[i]) for i in range(2)])
        parts[4] = density(xk0[0][:, cols], xk0[1][:, cols])

        @pl.when(index_of(x, y) < 2)
        def _():
            parts[5] = density(d0r[0][:, cols], d0r[1][:, cols])
            parts[6] = density(*[dpr[i][:, cols].astype(F32) - pe[i] for i in range(2)])

        @pl.when(index_of(x, y) >= 2)
        def _():
            parts[5] = density(xp0[0][:, cols], xp0[1][:, cols])
            parts[6] = density(-oe[0], -oe[1])

    @pl.when(c == 0)
    def _():
        work(edge, edge_s, 0)

    @pl.when(c == 1)
    def _():
        work(edge_s, edge, 1)

    for d, out in enumerate((slot0, slot1, slot2, slot3)):
        at = pl.multiple_of(32 * (y ^ d), 32)
        for b in range(7):
            out[b] = parts[b, pl.ds(at, 32), :]


def sum_kernel(a0, a1, a2, a3, d0, d1, d2, d3, out):
    total = a0[...].astype(F32) + a1[...].astype(F32)
    total = total + (a2[...].astype(F32) + a3[...].astype(F32))
    diag = d0[...].astype(F32) + d1[...].astype(F32) + d2[...].astype(F32) + d3[...].astype(F32)
    out[0] = (total[0] + diag).astype(BF)
    out[1:] = total[1:].astype(BF)


def final_kernel(g0, g1, g3, g2, out):
    x, z, y, c = place()
    for d, g in enumerate((g0, g1, g2, g3)):
        b = index_of(x ^ d, y)
        k = node_of(b)
        p = 1 + lax.rem(b, 2)
        pair = 2 * (k - 3) + 2
        low = b < 2
        out[k] = g[0].astype(F32)
        out[7 + pair] = g[1].astype(F32)
        out[8 + pair] = g[2].astype(F32)
        out[17 + pair] = g[3].astype(F32)
        out[18 + pair] = g[4].astype(F32)
        out[jnp.where(low, p, 6 + p)] = g[6].astype(F32)

        @pl.when(b != 1)
        def _():
            out[jnp.where(low, 0, 16 + p)] = g[5].astype(F32)


def body(lower_factor, upper_factor, diag_inverse, residues, widths, pattern):
    mine = (lower_factor[0], upper_factor[0], diag_inverse[0])
    swapped = [lax.ppermute(a, "col", SWAP) for a in mine]
    grid = ("row", "col")
    *bufs, widths, pattern, weights = call(
        pack_own_kernel,
        [shape(5, 2, 2, 32, 256)] * 4
        + [shape(32, 256)] * 4
        + [shape(7, dtype=jnp.int32), shape(10, dtype=jnp.int32), shape(1, 2, dtype=F32)],
        [in_hbm()] * 6,
        [vm()] * 8 + [sm()] * 3,
        [
            pltpu.VMEM((10, 2, 32, 256), BF),
            pltpu.VMEM((10, 2, 32, 256), BF),
            pltpu.VMEM((7, 2, 32, 256), BF),
            pltpu.SemaphoreType.DMA((6,)),
        ],
        nbytes=4 << 20,
    )(*[pltpu.with_memory_space_constraint(a, pltpu.HBM) for a in (*mine, widths, pattern, residues)])
    bufs, parts = bufs[:4], bufs[4:]
    bufs = call(
        pack_other_kernel,
        [shape(5, 2, 2, 32, 256)] * 4,
        [vm()] * 3 + [sm()] * 2 + [hbm()] * 4,
        [vm()] * 4,
        nbytes=4 << 20,
        aliases={5: 0, 6: 1, 7: 2, 8: 3},
    )(*swapped, widths, pattern, *bufs)
    came = {d: lax.ppermute(bufs[d], grid, ring_both(d)) for d in (1, 3, 2)}
    parts = [parts[0]] + [lax.ppermute(parts[d], "pole", pairs_x(d)) for d in (2, 3, 1)]
    near, far, uk = call(
        merge_kernel,
        [shape(3, 2, 2, 4, 32, 256)] * 2 + [shape(2, 2, 2, 4, 32, 256)],
        [hbm()] * 4,
        [hbm()] * 3,
        [pltpu.SemaphoreType.DMA((16,))],
        nbytes=4 << 20,
    )(bufs[0], came[2], came[3], came[1])
    came = {d: lax.ppermute(near, grid, ring_other(d)) for d in (1, 3)}
    came[2] = lax.ppermute(far, grid, ring_other(2))
    uks = lax.ppermute(uk, "col", SWAP)
    blocks = (far, came[3], came[2], came[1])
    half = shape(2, 2, 2, 4, 32, 256)
    go = call(
        early_kernel,
        [half],
        [hbm()] * 5,
        [hbm()],
        [pltpu.SemaphoreType.DMA((2,))],
        nbytes=1 << 20,
    )(far, came[2], *parts[1:])[0]
    got_early = lax.ppermute(go, "col", SWAP)
    whole = shape(2, 2, 4, 4, 32, 256)
    slab = shape(2, 128, 512)
    *edge, stay, go, lead = call(
        first_kernel,
        [slab] * 3 + [whole, half, whole],
        [hbm()] * 4 + [vm()] + [hbm()],
        [vm()] * 3 + [hbm()] * 3,
        [pltpu.VMEM((2, 2, 2, 4, 4, 32, 256), BF), pltpu.SemaphoreType.DMA((8,))],
        flops=805306368,
        nbytes=4 << 20,
    )(*blocks, uks, got_early)
    got = lax.ppermute(go, "col", SWAP)
    edge[:2] = call(
        next_kernel,
        [slab] * 2,
        [hbm()] * 2 + [vm()] * 2 + [hbm()],
        [vm()] * 2,
        flops=268435456,
        nbytes=2 << 20,
        aliases={0: 0, 1: 1},
    )(*edge[:2], lead, uk, stay)
    edge_s = [lax.ppermute(e, "col", SWAP) for e in edge]
    inner, early, other = call(
        inner_kernel,
        [shape(1024, 256), shape(768, 256, dtype=F32), whole],
        [vm()] * 4 + [hbm()] * 2,
        [vm()] * 3,
        [pltpu.SemaphoreType.DMA((4,))],
        flops=939524096,
        nbytes=4 << 20,
    )(*edge, stay, got_early, got)
    slots = call(
        last_kernel,
        [shape(7, 32, 256)] * 4,
        [vm()] * 9 + [sm()],
        [vm()] * 4,
        [pltpu.VMEM((7, 128, 256), BF)],
        flops=805306368,
        nbytes=4 << 20,
    )(*edge, *edge_s, inner, early, other, weights)
    at_x = [slots[0]] + [lax.ppermute(slots[d], ("pole", "row"), pairs_xy(d)) for d in (2, 3, 1)]
    total = call(sum_kernel, [shape(7, 32, 256)], [vm()] * 8, [vm()], nbytes=1 << 20)(
        *at_x, *parts
    )[0]
    full = [total] + [lax.ppermute(total, "pole", pairs_x(d)) for d in (1, 3, 2)]
    return call(
        final_kernel, [shape(27, 32, 256, dtype=F32)], [vm()] * 4, [vm()], nbytes=2 << 20
    )(*full)[0]


def solution(mesh):
    return jax.shard_map(
        body,
        mesh=mesh,
        in_specs=(
            P("pole", None, None, "row", "col"),
            P("pole", None, None, "row", "col"),
            P("pole", None, None, "row", "col"),
            P("pole", None),
            P(),
            P(),
        ),
        out_specs=P(None, "row", "col"),
        check_vma=False,
    )
```

```python
import jax
import jax.numpy as jnp
from jax import lax
from jax.experimental import pallas as pl
from jax.experimental.pallas import tpu as pltpu
from jax.sharding import PartitionSpec as P

BF = jnp.bfloat16
F32 = jnp.float32
VMEM_LIMIT = 24 * 1024 * 1024


def ring_both(step):
    pairs = []
    for z in range(4):
        for y in range(4):
            here = (z * 4 + y) * 2
            pairs.append((here, (z * 4 + (y + step) % 4) * 2))
            pairs.append((here + 1, (((z + step) % 4) * 4 + y) * 2 + 1))
    return pairs


def ring_other(step):
    pairs = []
    for z in range(4):
        for y in range(4):
            here = (z * 4 + y) * 2
            pairs.append((here, (((z + step) % 4) * 4 + y) * 2))
            pairs.append((here + 1, (z * 4 + (y + step) % 4) * 2 + 1))
    return pairs


def pairs_x(step):
    return [(x, x ^ step) for x in range(4)]


def pairs_xy(step):
    return [
        (x * 16 + z * 4 + y, (x ^ (4 - step)) * 16 + z * 4 + (y ^ step))
        for x in range(4)
        for z in range(4)
        for y in range(4)
    ]


SWAP = [(0, 1), (1, 0)]


def place():
    row = lax.axis_index("row")
    return lax.axis_index("pole"), lax.div(row, 4), lax.rem(row, 4), lax.axis_index("col")


def index_of(x, y):
    return x ^ lax.rem(8 - y, 4)


def node_of(m):
    return 3 + 2 * lax.rem(m, 2) + lax.div(m, 2)


def vm():
    return pl.BlockSpec(memory_space=pltpu.VMEM)


def sm():
    return pl.BlockSpec(memory_space=pltpu.SMEM)


def in_hbm():
    return pl.BlockSpec(memory_space=pltpu.HBM)


def hbm():
    return pl.BlockSpec(memory_space=pl.ANY)


def call(kernel, outs, in_specs, out_specs, scratch=(), flops=0, nbytes=0, aliases={}):
    return pl.pallas_call(
        kernel,
        out_shape=outs,
        in_specs=in_specs,
        out_specs=out_specs,
        scratch_shapes=list(scratch),
        input_output_aliases=aliases,
        compiler_params=pltpu.CompilerParams(vmem_limit_bytes=VMEM_LIMIT),
        cost_estimate=pl.CostEstimate(flops=flops, bytes_accessed=nbytes, transcendentals=0),
    )


def shape(*dims, dtype=BF):
    return jax.ShapeDtypeStruct(dims, dtype)


def pack(low, up, dia, widths, pattern, outs, own):
    x, z, y, c = place()
    rows = (32 * (4 * z + y)) + lax.broadcasted_iota(jnp.int32, (32, 256), 0)
    cols = lax.broadcasted_iota(jnp.int32, (32, 256), 1)

    def mask(row_node, col_node, on, half):
        keep = (rows < widths[row_node]) & (cols + 256 * half < widths[col_node]) & (on != 0)
        return jnp.where(keep, 1.0, 0.0).astype(BF)[None]

    @pl.when(c == 0)
    def _():
        h = 0 if own else 1
        for d, out in enumerate(outs):
            k = node_of(index_of(x, lax.rem(y + d, 4)))
            p = lax.div(k - 1, 2)
            at = 2 * (k - 3) + 2
            out[0, h] = dia[p] * mask(p, p, 1, h)
            out[1, h] = low[at] * mask(p, k, pattern[at], h)
            out[2, h] = low[at + 1] * mask(0, k, pattern[at + 1], h)
            out[3, h] = up[at] * mask(k, p, pattern[at], h)
            out[4, h] = up[at + 1] * mask(k, 0, pattern[at + 1], h)

    @pl.when(c == 1)
    def _():
        h = 1 if own else 0
        tiles = [dia[0] * mask(0, 0, 1, h)]
        for i in range(2):
            tiles.append(up[i] * mask(1 + i, 0, pattern[i], h))
            tiles.append(low[i] * mask(0, 1 + i, pattern[i], h))
        for out in outs:
            for t in range(5):
                out[t, h] = tiles[t]


def pack_own_kernel(low_in, up_in, dia_in, widths_in, pattern_in, res_in, *refs):
    outs, parts, (widths, pattern, res, low, up, dia, sems) = refs[:4], refs[4:8], refs[8:]
    run_copies(
        [
            (low_in, low),
            (up_in, up),
            (dia_in, dia),
            (widths_in, widths),
            (pattern_in, pattern),
            (res_in, res),
        ],
        sems,
    )
    pack(low, up, dia, widths, pattern, outs, True)
    x, z, y, c = place()
    rows = (32 * (4 * z + y)) + lax.broadcasted_iota(jnp.int32, (32, 256), 0)
    cols = (256 * c) + lax.broadcasted_iota(jnp.int32, (32, 256), 1)
    for d, part in enumerate(parts):
        k = node_of(index_of(x ^ d, y))
        dens = res[0, 0] * dia[k, 0].astype(F32) - res[0, 1] * dia[k, 1].astype(F32)
        part[...] = jnp.where((rows < widths[k]) & (cols < widths[k]), dens, 0.0).astype(BF)


def pack_other_kernel(low, up, dia, widths, pattern, *refs):
    given, outs = refs[:4], refs[4:]
    for half in range(2):

        @pl.when(lax.axis_index("col") == half)
        def _():
            for before, out in zip(given, outs):
                out[:, half] = before[:, half]

    pack(low, up, dia, widths, pattern, outs, False)


def run_copies(copies, sems):
    made = [pltpu.make_async_copy(s, t, sems.at[i]) for i, (s, t) in enumerate(copies)]
    for m in made:
        m.start()
    for m in made:
        m.wait()


def merge_kernel(b0, b2, b3, b1, near, far, uk, sems):
    x, z, y, c = place()
    p = lax.rem(index_of(x, y), 2)

    @pl.when(c == 0)
    def _():
        copies = []
        for d, buf in enumerate((b0, b1, b2, b3)):
            at = lax.rem(y + 4 - d, 4)
            copies.append((buf.at[pl.ds(0, 3)], near.at[:, :, :, at]))
            copies.append((buf.at[pl.ds(0, 3)], far.at[:, :, :, at]))
            copies.append((buf.at[pl.ds(3, 2)], uk.at[:, :, :, at]))
        run_copies(copies, sems)

    @pl.when(c == 1)
    def _():
        copies = []
        for d, buf in enumerate((b0, b1, b2, b3)):
            at = lax.rem(z + 4 - d, 4)
            copies.append((buf.at[0], near.at[0, :, :, at]))
            copies.append((buf.at[0], far.at[0, :, :, at]))
            copies.append((buf.at[pl.ds(1 + 2 * p, 2)], far.at[pl.ds(1, 2), :, :, at]))
            copies.append((buf.at[pl.ds(3 - 2 * p, 2)], near.at[pl.ds(1, 2), :, :, at]))
        run_copies(copies, sems)


def left_of(pairs):
    real = [jnp.concatenate([r, -i], axis=1) for r, i in pairs]
    imag = [jnp.concatenate([i, r], axis=1) for r, i in pairs]
    return jnp.concatenate(real + imag, axis=0)


def dot(a, b):
    return jnp.dot(a, b, preferred_element_type=F32)


def pairs_of(res, count):
    half = 128 * count
    return [
        (res[128 * i : 128 * i + 128], res[half + 128 * i : half + 128 * i + 128])
        for i in range(count)
    ]


def wide_rows(get):
    return tuple(jnp.concatenate([get(0, part), get(1, part)], axis=1) for part in range(2))


def times(left, count, right):
    got = [pairs_of(dot(left, right[h].reshape(1024, 256)), count) for h in range(2)]
    return [
        tuple(jnp.concatenate([got[0][n][i], got[1][n][i]], axis=1) for i in range(2))
        for n in range(count)
    ]


def put(out, pair, sign=1):
    for i in range(2):
        out[i] = (pair[i] if sign > 0 else -pair[i]).astype(BF)


def early_kernel(r0, r2, p2, p3, p1, go, sems):
    x, z, y, c = place()
    part_of_last(((0, r0), (2, r2)), go, sems)


def part_of_last(given, go, sems):
    x, z, y, c = place()

    @pl.when(c == 0)
    def _():
        copies = []
        for d, buf in given:
            at = lax.div(lax.rem(z + 4 - d, 4), 2)
            copies.append((buf.at[pl.ds(1, 2), 1], go.at[:, :, at]))
        run_copies(copies, sems)

    @pl.when(c == 1)
    def _():
        copies = []
        for d, buf in given:
            at = lax.div(lax.rem(y + 4 - d, 4), 2)
            copies.append((buf.at[2], go.at[:, :, at]))
        run_copies(copies, sems)


def first_kernel(
    r0, r3, r2, r1, uks, before, out0, out1, out2, stay, go, lead, right, sems
):
    x, z, y, c = place()
    part_of_last(((1, r1), (3, r3)), go, sems)

    def rows_of(block):
        return wide_rows(lambda h, part: right[block, h, part, z].reshape(128, 256))

    @pl.when(c == 0)
    def _():
        copies = []
        for d, buf in enumerate((r0, r1, r2, r3)):
            at = lax.rem(z + 4 - d, 4)
            copies.append((buf.at[pl.ds(1, 2), 0], stay.at[:, :, at]))
            copies.append((buf.at[0], lead.at[:, :, at]))
        run_copies(copies, sems)

    @pl.when(c == 1)
    def _():
        copies = []
        for d, buf in enumerate((r0, r1, r2, r3)):
            at = lax.rem(y + 4 - d, 4)
            copies.append((buf.at[pl.ds(0, 2)], right.at[:, :, :, :, at]))
            copies.append((buf.at[2], stay.at[:, :, :, at]))
        run_copies(copies, sems)
        ukp = wide_rows(lambda h, part: uks[0, h, part].reshape(128, 256))
        uk0 = wide_rows(lambda h, part: uks[1, h, part].reshape(128, 256))
        (kv,) = times(left_of([ukp]), 1, right[1])
        v = tuple((uk0[i].astype(F32) - kv[i]).astype(BF) for i in range(2))
        xk0, xp0 = times(left_of([v, rows_of(1)]), 2, right[0])
        put(out0, xp0, -1)
        put(out1, rows_of(0))
        put(out2, xk0, -1)


def next_kernel(edge0, edge1, lead, uk, after, out0, out1):
    x, z, y, c = place()

    @pl.when(c == 0)
    def _():
        ukp = wide_rows(lambda h, part: uk[0, h, part].reshape(128, 256))
        (kd,) = times(left_of([ukp]), 1, lead)
        put(out0, kd)
        put(out1, wide_rows(lambda h, part: lead[h, part, z].reshape(128, 256)))

    @pl.when(c == 1)
    def _():
        out0[...] = edge0[...]
        out1[...] = edge1[...]


def inner_kernel(edge0, edge1, edge2, stay, got_a, got_b, out, early, other, sems):
    x, z, y, c = place()

    def work(last, own):
        lp = wide_rows(lambda h, part: last[h, part].reshape(512, 256))
        prod = dot(left_of([lp]), own[0].reshape(1024, 256))
        out[...] = (own[1].reshape(1024, 256).astype(F32) - prod).astype(BF)

    @pl.when(c == 0)
    def _():
        copies = []
        for buf, low in ((got_a, lax.rem(y, 2)), (got_b, 1 - lax.rem(y, 2))):
            for n in range(2):
                copies.append((buf.at[:, :, n], other.at[:, :, :, 2 * n + low]))
        run_copies(copies, sems)
        work(other, stay)
        left = left_of([(e[0], e[1]) for e in (edge0, edge1)])
        early[0:512] = dot(left, stay[0].reshape(1024, 256))

    @pl.when(c == 1)
    def _():
        copies = []
        for buf, low in ((got_a, lax.rem(z, 2)), (got_b, 1 - lax.rem(z, 2))):
            for n in range(2):
                copies.append((buf.at[:, :, n], other.at[:, :, 2 * n + low]))
        run_copies(copies, sems)
        work(stay, other)
        left = left_of([(e[0], e[1]) for e in (edge0, edge1, edge2)])
        early[...] = dot(left, stay[1].reshape(1024, 256))


def last_kernel(
    edge0, edge1, edge2, swap0, swap1, swap2, inner, early, got, res,
    slot0, slot1, slot2, slot3, parts,
):
    edge, edge_s = (edge0, edge1, edge2), (swap0, swap1, swap2)
    x, z, y, c = place()
    wr, wi = res[0, 0], res[0, 1]

    def density(re, im):
        return (wr * re.astype(F32) - wi * im.astype(F32)).astype(BF)

    def work(e0, e1, half):
        cols = slice(256 * half, 256 * half + 256)
        xp0, d0r, xk0 = [(e1[n][0], e1[n][1]) for n in range(3)]
        kd, dpr = [(e0[n][0], e0[n][1]) for n in range(2)]
        left = left_of([xp0, d0r, xk0])
        pg, og, kg = pairs_of(dot(left, inner[...]), 3)
        if half == 0:
            pe, oe, ke = pairs_of(dot(left, got[0].reshape(1024, 256)), 3)
            kl, pl_ = pairs_of(early[0:512], 2)
        else:
            pe, oe, ke = pairs_of(early[...], 3)
            kl, pl_ = pairs_of(dot(left_of([kd, dpr]), got[0].reshape(1024, 256)), 2)
        parts[0] = density(*[kl[i] - kg[i] for i in range(2)])
        parts[1] = density(*[-(pl_[i] + pg[i]) for i in range(2)])
        parts[2] = density(-og[0], -og[1])
        parts[3] = density(*[-(kd[i][:, cols].astype(F32) + ke[i]) for i in range(2)])
        parts[4] = density(xk0[0][:, cols], xk0[1][:, cols])

        @pl.when(index_of(x, y) < 2)
        def _():
            parts[5] = density(d0r[0][:, cols], d0r[1][:, cols])
            parts[6] = density(*[dpr[i][:, cols].astype(F32) - pe[i] for i in range(2)])

        @pl.when(index_of(x, y) >= 2)
        def _():
            parts[5] = density(xp0[0][:, cols], xp0[1][:, cols])
            parts[6] = density(-oe[0], -oe[1])

    @pl.when(c == 0)
    def _():
        work(edge, edge_s, 0)

    @pl.when(c == 1)
    def _():
        work(edge_s, edge, 1)

    for d, out in enumerate((slot0, slot1, slot2, slot3)):
        at = pl.multiple_of(32 * (y ^ d), 32)
        for b in range(7):
            out[b] = parts[b, pl.ds(at, 32), :]


def sum_kernel(a0, a1, a2, a3, d0, d1, d2, d3, out):
    total = a0[...].astype(F32) + a1[...].astype(F32)
    total = total + (a2[...].astype(F32) + a3[...].astype(F32))
    diag = d0[...].astype(F32) + d1[...].astype(F32) + d2[...].astype(F32) + d3[...].astype(F32)
    out[0] = (total[0] + diag).astype(BF)
    out[1:] = total[1:].astype(BF)


def final_kernel(g0, g1, g3, g2, out):
    x, z, y, c = place()
    for d, g in enumerate((g0, g1, g2, g3)):
        b = index_of(x ^ d, y)
        k = node_of(b)
        p = 1 + lax.rem(b, 2)
        pair = 2 * (k - 3) + 2
        low = b < 2
        out[k] = g[0].astype(F32)
        out[7 + pair] = g[1].astype(F32)
        out[8 + pair] = g[2].astype(F32)
        out[17 + pair] = g[3].astype(F32)
        out[18 + pair] = g[4].astype(F32)
        out[jnp.where(low, p, 6 + p)] = g[6].astype(F32)

        @pl.when(b != 1)
        def _():
            out[jnp.where(low, 0, 16 + p)] = g[5].astype(F32)


def body(lower_factor, upper_factor, diag_inverse, residues, widths, pattern):
    mine = (lower_factor[0], upper_factor[0], diag_inverse[0])
    swapped = [lax.ppermute(a, "col", SWAP) for a in mine]
    grid = ("row", "col")
    *bufs, widths, pattern, weights = call(
        pack_own_kernel,
        [shape(5, 2, 2, 32, 256)] * 4
        + [shape(32, 256)] * 4
        + [shape(7, dtype=jnp.int32), shape(10, dtype=jnp.int32), shape(1, 2, dtype=F32)],
        [in_hbm()] * 6,
        [vm()] * 8 + [sm()] * 3,
        [
            pltpu.VMEM((10, 2, 32, 256), BF),
            pltpu.VMEM((10, 2, 32, 256), BF),
            pltpu.VMEM((7, 2, 32, 256), BF),
            pltpu.SemaphoreType.DMA((6,)),
        ],
        nbytes=4 << 20,
    )(*[pltpu.with_memory_space_constraint(a, pltpu.HBM) for a in (*mine, widths, pattern, residues)])
    bufs, parts = bufs[:4], bufs[4:]
    bufs = call(
        pack_other_kernel,
        [shape(5, 2, 2, 32, 256)] * 4,
        [vm()] * 3 + [sm()] * 2 + [vm()] * 4,
        [vm()] * 4,
        nbytes=4 << 20,
        aliases={5: 0, 6: 1, 7: 2, 8: 3},
    )(*swapped, widths, pattern, *bufs)
    came = {d: lax.ppermute(bufs[d], grid, ring_both(d)) for d in (1, 3, 2)}
    parts = [parts[0]] + [lax.ppermute(parts[d], "pole", pairs_x(d)) for d in (2, 3, 1)]
    near, far, uk = call(
        merge_kernel,
        [shape(3, 2, 2, 4, 32, 256)] * 2 + [shape(2, 2, 2, 4, 32, 256)],
        [hbm()] * 4,
        [hbm()] * 3,
        [pltpu.SemaphoreType.DMA((16,))],
        nbytes=4 << 20,
    )(bufs[0], came[2], came[3], came[1])
    came = {d: lax.ppermute(near, grid, ring_other(d)) for d in (1, 3)}
    came[2] = lax.ppermute(far, grid, ring_other(2))
    uks = lax.ppermute(uk, "col", SWAP)
    blocks = (far, came[3], came[2], came[1])
    half = shape(2, 2, 2, 4, 32, 256)
    go = call(
        early_kernel,
        [half],
        [hbm()] * 5,
        [hbm()],
        [pltpu.SemaphoreType.DMA((2,))],
        nbytes=1 << 20,
    )(far, came[2], *parts[1:])[0]
    got_early = lax.ppermute(go, "col", SWAP)
    whole = shape(2, 2, 4, 4, 32, 256)
    slab = shape(2, 128, 512)
    *edge, stay, go, lead = call(
        first_kernel,
        [slab] * 3 + [whole, half, whole],
        [hbm()] * 4 + [vm()] + [hbm()],
        [vm()] * 3 + [hbm()] * 3,
        [pltpu.VMEM((2, 2, 2, 4, 4, 32, 256), BF), pltpu.SemaphoreType.DMA((8,))],
        flops=805306368,
        nbytes=4 << 20,
    )(*blocks, uks, got_early)
    got = lax.ppermute(go, "col", SWAP)
    edge[:2] = call(
        next_kernel,
        [slab] * 2,
        [vm()] * 4 + [hbm()],
        [vm()] * 2,
        flops=268435456,
        nbytes=2 << 20,
        aliases={0: 0, 1: 1},
    )(*edge[:2], lead, uk, stay)
    edge_s = [lax.ppermute(e, "col", SWAP) for e in edge]
    inner, early, other = call(
        inner_kernel,
        [shape(1024, 256), shape(768, 256, dtype=F32), whole],
        [vm()] * 4 + [hbm()] * 2,
        [vm()] * 3,
        [pltpu.SemaphoreType.DMA((4,))],
        flops=939524096,
        nbytes=4 << 20,
    )(*edge, stay, got_early, got)
    slots = call(
        last_kernel,
        [shape(7, 32, 256)] * 4,
        [vm()] * 9 + [sm()],
        [vm()] * 4,
        [pltpu.VMEM((7, 128, 256), BF)],
        flops=805306368,
        nbytes=4 << 20,
    )(*edge, *edge_s, inner, early, other, weights)
    at_x = [slots[0]] + [lax.ppermute(slots[d], ("pole", "row"), pairs_xy(d)) for d in (2, 3, 1)]
    total = call(sum_kernel, [shape(7, 32, 256)], [vm()] * 8, [vm()], nbytes=1 << 20)(
        *at_x, *parts
    )[0]
    full = [total] + [lax.ppermute(total, "pole", pairs_x(d)) for d in (1, 3, 2)]
    return call(
        final_kernel, [shape(27, 32, 256, dtype=F32)], [vm()] * 4, [vm()], nbytes=2 << 20
    )(*full)[0]


def solution(mesh):
    return jax.shard_map(
        body,
        mesh=mesh,
        in_specs=(
            P("pole", None, None, "row", "col"),
            P("pole", None, None, "row", "col"),
            P("pole", None, None, "row", "col"),
            P("pole", None),
            P(),
            P(),
        ),
        out_specs=P(None, "row", "col"),
        check_vma=False,
    )
```

```python
import jax
import jax.numpy as jnp
from jax import lax
from jax.experimental import pallas as pl
from jax.experimental.pallas import tpu as pltpu
from jax.sharding import PartitionSpec as P

BF = jnp.bfloat16
F32 = jnp.float32
VMEM_LIMIT = 24 * 1024 * 1024


def ring_both(step):
    pairs = []
    for z in range(4):
        for y in range(4):
            here = (z * 4 + y) * 2
            pairs.append((here, (z * 4 + (y + step) % 4) * 2))
            pairs.append((here + 1, (((z + step) % 4) * 4 + y) * 2 + 1))
    return pairs


def ring_other(step):
    pairs = []
    for z in range(4):
        for y in range(4):
            here = (z * 4 + y) * 2
            pairs.append((here, (((z + step) % 4) * 4 + y) * 2))
            pairs.append((here + 1, (z * 4 + (y + step) % 4) * 2 + 1))
    return pairs


def pairs_x(step):
    return [(x, x ^ step) for x in range(4)]


def pairs_xy(step):
    return [
        (x * 16 + z * 4 + y, (x ^ (4 - step)) * 16 + z * 4 + (y ^ step))
        for x in range(4)
        for z in range(4)
        for y in range(4)
    ]


SWAP = [(0, 1), (1, 0)]


def place():
    row = lax.axis_index("row")
    return lax.axis_index("pole"), lax.div(row, 4), lax.rem(row, 4), lax.axis_index("col")


def index_of(x, y):
    return x ^ lax.rem(8 - y, 4)


def node_of(m):
    return 3 + 2 * lax.rem(m, 2) + lax.div(m, 2)


def vm():
    return pl.BlockSpec(memory_space=pltpu.VMEM)


def sm():
    return pl.BlockSpec(memory_space=pltpu.SMEM)


def in_hbm():
    return pl.BlockSpec(memory_space=pltpu.HBM)


def hbm():
    return pl.BlockSpec(memory_space=pl.ANY)


def call(kernel, outs, in_specs, out_specs, scratch=(), flops=0, nbytes=0, aliases={}):
    return pl.pallas_call(
        kernel,
        out_shape=outs,
        in_specs=in_specs,
        out_specs=out_specs,
        scratch_shapes=list(scratch),
        input_output_aliases=aliases,
        compiler_params=pltpu.CompilerParams(vmem_limit_bytes=VMEM_LIMIT),
        cost_estimate=pl.CostEstimate(flops=flops, bytes_accessed=nbytes, transcendentals=0),
    )


def shape(*dims, dtype=BF):
    return jax.ShapeDtypeStruct(dims, dtype)


def pack(low, up, dia, widths, pattern, outs, own):
    x, z, y, c = place()
    rows = (32 * (4 * z + y)) + lax.broadcasted_iota(jnp.int32, (32, 256), 0)
    cols = lax.broadcasted_iota(jnp.int32, (32, 256), 1)

    def mask(row_node, col_node, on, half):
        keep = (rows < widths[row_node]) & (cols + 256 * half < widths[col_node]) & (on != 0)
        return jnp.where(keep, 1.0, 0.0).astype(BF)[None]

    @pl.when(c == 0)
    def _():
        h = 0 if own else 1
        for d, out in enumerate(outs):
            k = node_of(index_of(x, lax.rem(y + d, 4)))
            p = lax.div(k - 1, 2)
            at = 2 * (k - 3) + 2
            out[0, h] = dia[p] * mask(p, p, 1, h)
            out[1, h] = low[at] * mask(p, k, pattern[at], h)
            out[2, h] = low[at + 1] * mask(0, k, pattern[at + 1], h)
            out[3, h] = up[at] * mask(k, p, pattern[at], h)
            out[4, h] = up[at + 1] * mask(k, 0, pattern[at + 1], h)

    @pl.when(c == 1)
    def _():
        h = 1 if own else 0
        tiles = [dia[0] * mask(0, 0, 1, h)]
        for i in range(2):
            tiles.append(up[i] * mask(1 + i, 0, pattern[i], h))
            tiles.append(low[i] * mask(0, 1 + i, pattern[i], h))
        for out in outs:
            for t in range(5):
                out[t, h] = tiles[t]


def pack_own_kernel(low_in, up_in, dia_in, widths_in, pattern_in, res_in, *refs):
    outs, parts, (widths, pattern, res, low, up, dia, sems) = refs[:4], refs[4:8], refs[8:]
    run_copies(
        [
            (low_in, low),
            (up_in, up),
            (dia_in, dia),
            (widths_in, widths),
            (pattern_in, pattern),
            (res_in, res),
        ],
        sems,
    )
    pack(low, up, dia, widths, pattern, outs, True)
    x, z, y, c = place()
    rows = (32 * (4 * z + y)) + lax.broadcasted_iota(jnp.int32, (32, 256), 0)
    cols = (256 * c) + lax.broadcasted_iota(jnp.int32, (32, 256), 1)
    for d, part in enumerate(parts):
        k = node_of(index_of(x ^ d, y))
        dens = res[0, 0] * dia[k, 0].astype(F32) - res[0, 1] * dia[k, 1].astype(F32)
        part[...] = jnp.where((rows < widths[k]) & (cols < widths[k]), dens, 0.0).astype(BF)


def pack_other_kernel(low, up, dia, widths, pattern, *refs):
    given, outs = refs[:4], refs[4:]
    for half in range(2):

        @pl.when(lax.axis_index("col") == half)
        def _():
            for before, out in zip(given, outs):
                out[:, half] = before[:, half]

    pack(low, up, dia, widths, pattern, outs, False)


def run_copies(copies, sems):
    made = [pltpu.make_async_copy(s, t, sems.at[i]) for i, (s, t) in enumerate(copies)]
    for m in made:
        m.start()
    for m in made:
        m.wait()


def merge_kernel(b0, b2, b3, b1, near, far, uk, sems):
    x, z, y, c = place()
    p = lax.rem(index_of(x, y), 2)

    @pl.when(c == 0)
    def _():
        copies = []
        for d, buf in enumerate((b0, b1, b2, b3)):
            at = lax.rem(y + 4 - d, 4)
            copies.append((buf.at[pl.ds(0, 3)], near.at[:, :, :, at]))
            copies.append((buf.at[pl.ds(0, 3)], far.at[:, :, :, at]))
            copies.append((buf.at[pl.ds(3, 2)], uk.at[:, :, :, at]))
        run_copies(copies, sems)

    @pl.when(c == 1)
    def _():
        copies = []
        for d, buf in enumerate((b0, b1, b2, b3)):
            at = lax.rem(z + 4 - d, 4)
            copies.append((buf.at[0], near.at[0, :, :, at]))
            copies.append((buf.at[0], far.at[0, :, :, at]))
            copies.append((buf.at[pl.ds(1 + 2 * p, 2)], far.at[pl.ds(1, 2), :, :, at]))
            copies.append((buf.at[pl.ds(3 - 2 * p, 2)], near.at[pl.ds(1, 2), :, :, at]))
        run_copies(copies, sems)


def left_of(pairs):
    real = [jnp.concatenate([r, -i], axis=1) for r, i in pairs]
    imag = [jnp.concatenate([i, r], axis=1) for r, i in pairs]
    return jnp.concatenate(real + imag, axis=0)


def dot(a, b):
    return jnp.dot(a, b, preferred_element_type=F32)


def pairs_of(res, count):
    half = 128 * count
    return [
        (res[128 * i : 128 * i + 128], res[half + 128 * i : half + 128 * i + 128])
        for i in range(count)
    ]


def wide_rows(get):
    return tuple(jnp.concatenate([get(0, part), get(1, part)], axis=1) for part in range(2))


def times(left, count, right):
    got = [pairs_of(dot(left, right[h].reshape(1024, 256)), count) for h in range(2)]
    return [
        tuple(jnp.concatenate([got[0][n][i], got[1][n][i]], axis=1) for i in range(2))
        for n in range(count)
    ]


def put(out, pair, sign=1):
    for i in range(2):
        out[i] = (pair[i] if sign > 0 else -pair[i]).astype(BF)


def early_kernel(r0, r2, p2, p3, p1, go, sems):
    zero, one = part_of_last(((0, r0), (2, r2)), go)
    for half, copies in enumerate((zero, one)):

        @pl.when(lax.axis_index("col") == half)
        def _():
            run_copies(copies, sems)


def part_of_last(given, go):
    x, z, y, c = place()
    zero, one = [], []
    for d, buf in given:
        at = lax.div(lax.rem(z + 4 - d, 4), 2)
        zero.append((buf.at[pl.ds(1, 2), 1], go.at[:, :, at]))
        at = lax.div(lax.rem(y + 4 - d, 4), 2)
        one.append((buf.at[2], go.at[:, :, at]))
    return zero, one


def first_kernel(
    r0, r3, r2, r1, uks, before, out0, out1, out2, stay, go, lead, right, sems
):
    x, z, y, c = place()
    zero, one = part_of_last(((1, r1), (3, r3)), go)

    def rows_of(block):
        return wide_rows(lambda h, part: right[block, h, part, z].reshape(128, 256))

    @pl.when(c == 0)
    def _():
        copies = list(zero)
        for d, buf in enumerate((r0, r1, r2, r3)):
            at = lax.rem(z + 4 - d, 4)
            copies.append((buf.at[pl.ds(1, 2), 0], stay.at[:, :, at]))
            copies.append((buf.at[0], lead.at[:, :, at]))
        run_copies(copies, sems)

    @pl.when(c == 1)
    def _():
        copies, late = [], list(one)
        for d, buf in enumerate((r0, r1, r2, r3)):
            at = lax.rem(y + 4 - d, 4)
            copies.append((buf.at[pl.ds(0, 2)], right.at[:, :, :, :, at]))
            late.append((buf.at[2], stay.at[:, :, :, at]))
        made = [
            pltpu.make_async_copy(s, t, sems.at[i]) for i, (s, t) in enumerate(copies + late)
        ]
        for m in made:
            m.start()
        for m in made[: len(copies)]:
            m.wait()
        ukp = wide_rows(lambda h, part: uks[0, h, part].reshape(128, 256))
        uk0 = wide_rows(lambda h, part: uks[1, h, part].reshape(128, 256))
        (kv,) = times(left_of([ukp]), 1, right[1])
        v = tuple((uk0[i].astype(F32) - kv[i]).astype(BF) for i in range(2))
        xk0, xp0 = times(left_of([v, rows_of(1)]), 2, right[0])
        put(out0, xp0, -1)
        put(out1, rows_of(0))
        put(out2, xk0, -1)
        for m in made[len(copies) :]:
            m.wait()


def next_kernel(edge0, edge1, lead, uk, after, out0, out1):
    x, z, y, c = place()

    @pl.when(c == 0)
    def _():
        ukp = wide_rows(lambda h, part: uk[0, h, part].reshape(128, 256))
        (kd,) = times(left_of([ukp]), 1, lead)
        put(out0, kd)
        put(out1, wide_rows(lambda h, part: lead[h, part, z].reshape(128, 256)))

    @pl.when(c == 1)
    def _():
        out0[...] = edge0[...]
        out1[...] = edge1[...]


def inner_kernel(edge0, edge1, edge2, stay, got_a, got_b, out, early, other, sems):
    x, z, y, c = place()

    def work(last, own):
        lp = wide_rows(lambda h, part: last[h, part].reshape(512, 256))
        prod = dot(left_of([lp]), own[0].reshape(1024, 256))
        out[...] = (own[1].reshape(1024, 256).astype(F32) - prod).astype(BF)

    @pl.when(c == 0)
    def _():
        copies = []
        for buf, low in ((got_a, lax.rem(y, 2)), (got_b, 1 - lax.rem(y, 2))):
            for n in range(2):
                copies.append((buf.at[:, :, n], other.at[:, :, :, 2 * n + low]))
        run_copies(copies, sems)
        work(other, stay)
        left = left_of([(e[0], e[1]) for e in (edge0, edge1)])
        early[0:512] = dot(left, stay[0].reshape(1024, 256))

    @pl.when(c == 1)
    def _():
        copies = []
        for buf, low in ((got_a, lax.rem(z, 2)), (got_b, 1 - lax.rem(z, 2))):
            for n in range(2):
                copies.append((buf.at[:, :, n], other.at[:, :, 2 * n + low]))
        run_copies(copies, sems)
        work(stay, other)
        left = left_of([(e[0], e[1]) for e in (edge0, edge1, edge2)])
        early[...] = dot(left, stay[1].reshape(1024, 256))


def last_kernel(
    edge0, edge1, edge2, swap0, swap1, swap2, inner, early, got, res,
    slot0, slot1, slot2, slot3, parts,
):
    edge, edge_s = (edge0, edge1, edge2), (swap0, swap1, swap2)
    x, z, y, c = place()
    wr, wi = res[0, 0], res[0, 1]

    def density(re, im):
        return (wr * re.astype(F32) - wi * im.astype(F32)).astype(BF)

    def work(e0, e1, half):
        cols = slice(256 * half, 256 * half + 256)
        xp0, d0r, xk0 = [(e1[n][0], e1[n][1]) for n in range(3)]
        kd, dpr = [(e0[n][0], e0[n][1]) for n in range(2)]
        left = left_of([xp0, d0r, xk0])
        pg, og, kg = pairs_of(dot(left, inner[...]), 3)
        if half == 0:
            pe, oe, ke = pairs_of(dot(left, got[0].reshape(1024, 256)), 3)
            kl, pl_ = pairs_of(early[0:512], 2)
        else:
            pe, oe, ke = pairs_of(early[...], 3)
            kl, pl_ = pairs_of(dot(left_of([kd, dpr]), got[0].reshape(1024, 256)), 2)
        parts[0] = density(*[kl[i] - kg[i] for i in range(2)])
        parts[1] = density(*[-(pl_[i] + pg[i]) for i in range(2)])
        parts[2] = density(-og[0], -og[1])
        parts[3] = density(*[-(kd[i][:, cols].astype(F32) + ke[i]) for i in range(2)])
        parts[4] = density(xk0[0][:, cols], xk0[1][:, cols])

        @pl.when(index_of(x, y) < 2)
        def _():
            parts[5] = density(d0r[0][:, cols], d0r[1][:, cols])
            parts[6] = density(*[dpr[i][:, cols].astype(F32) - pe[i] for i in range(2)])

        @pl.when(index_of(x, y) >= 2)
        def _():
            parts[5] = density(xp0[0][:, cols], xp0[1][:, cols])
            parts[6] = density(-oe[0], -oe[1])

    @pl.when(c == 0)
    def _():
        work(edge, edge_s, 0)

    @pl.when(c == 1)
    def _():
        work(edge_s, edge, 1)

    for d, out in enumerate((slot0, slot1, slot2, slot3)):
        at = pl.multiple_of(32 * (y ^ d), 32)
        for b in range(7):
            out[b] = parts[b, pl.ds(at, 32), :]


def sum_kernel(a0, a1, a2, a3, d0, d1, d2, d3, out):
    total = a0[...].astype(F32) + a1[...].astype(F32)
    total = total + (a2[...].astype(F32) + a3[...].astype(F32))
    diag = d0[...].astype(F32) + d1[...].astype(F32) + d2[...].astype(F32) + d3[...].astype(F32)
    out[0] = (total[0] + diag).astype(BF)
    out[1:] = total[1:].astype(BF)


def final_kernel(g0, g1, g3, g2, out):
    x, z, y, c = place()
    for d, g in enumerate((g0, g1, g2, g3)):
        b = index_of(x ^ d, y)
        k = node_of(b)
        p = 1 + lax.rem(b, 2)
        pair = 2 * (k - 3) + 2
        low = b < 2
        out[k] = g[0].astype(F32)
        out[7 + pair] = g[1].astype(F32)
        out[8 + pair] = g[2].astype(F32)
        out[17 + pair] = g[3].astype(F32)
        out[18 + pair] = g[4].astype(F32)
        out[jnp.where(low, p, 6 + p)] = g[6].astype(F32)

        @pl.when(b != 1)
        def _():
            out[jnp.where(low, 0, 16 + p)] = g[5].astype(F32)


def body(lower_factor, upper_factor, diag_inverse, residues, widths, pattern):
    mine = (lower_factor[0], upper_factor[0], diag_inverse[0])
    swapped = [lax.ppermute(a, "col", SWAP) for a in mine]
    grid = ("row", "col")
    *bufs, widths, pattern, weights = call(
        pack_own_kernel,
        [shape(5, 2, 2, 32, 256)] * 4
        + [shape(32, 256)] * 4
        + [shape(7, dtype=jnp.int32), shape(10, dtype=jnp.int32), shape(1, 2, dtype=F32)],
        [in_hbm()] * 6,
        [vm()] * 8 + [sm()] * 3,
        [
            pltpu.VMEM((10, 2, 32, 256), BF),
            pltpu.VMEM((10, 2, 32, 256), BF),
            pltpu.VMEM((7, 2, 32, 256), BF),
            pltpu.SemaphoreType.DMA((6,)),
        ],
        nbytes=4 << 20,
    )(*[pltpu.with_memory_space_constraint(a, pltpu.HBM) for a in (*mine, widths, pattern, residues)])
    bufs, parts = bufs[:4], bufs[4:]
    bufs = call(
        pack_other_kernel,
        [shape(5, 2, 2, 32, 256)] * 4,
        [vm()] * 3 + [sm()] * 2 + [vm()] * 4,
        [vm()] * 4,
        nbytes=4 << 20,
        aliases={5: 0, 6: 1, 7: 2, 8: 3},
    )(*swapped, widths, pattern, *bufs)
    came = {d: lax.ppermute(bufs[d], grid, ring_both(d)) for d in (1, 3, 2)}
    parts = [parts[0]] + [lax.ppermute(parts[d], "pole", pairs_x(d)) for d in (2, 3, 1)]
    near, far, uk = call(
        merge_kernel,
        [shape(3, 2, 2, 4, 32, 256)] * 2 + [shape(2, 2, 2, 4, 32, 256)],
        [hbm()] * 4,
        [hbm()] * 3,
        [pltpu.SemaphoreType.DMA((16,))],
        nbytes=4 << 20,
    )(bufs[0], came[2], came[3], came[1])
    came = {d: lax.ppermute(near, grid, ring_other(d)) for d in (1, 3)}
    came[2] = lax.ppermute(far, grid, ring_other(2))
    uks = lax.ppermute(uk, "col", SWAP)
    blocks = (far, came[3], came[2], came[1])
    half = shape(2, 2, 2, 4, 32, 256)
    go = call(
        early_kernel,
        [half],
        [hbm()] * 5,
        [hbm()],
        [pltpu.SemaphoreType.DMA((2,))],
        nbytes=1 << 20,
    )(far, came[2], *parts[1:])[0]
    got_early = lax.ppermute(go, "col", SWAP)
    whole = shape(2, 2, 4, 4, 32, 256)
    slab = shape(2, 128, 512)
    *edge, stay, go, lead = call(
        first_kernel,
        [slab] * 3 + [whole, half, whole],
        [hbm()] * 4 + [vm()] + [hbm()],
        [vm()] * 3 + [hbm()] * 3,
        [pltpu.VMEM((2, 2, 2, 4, 4, 32, 256), BF), pltpu.SemaphoreType.DMA((10,))],
        flops=805306368,
        nbytes=4 << 20,
    )(*blocks, uks, got_early)
    got = lax.ppermute(go, "col", SWAP)
    edge[:2] = call(
        next_kernel,
        [slab] * 2,
        [vm()] * 4 + [hbm()],
        [vm()] * 2,
        flops=268435456,
        nbytes=2 << 20,
        aliases={0: 0, 1: 1},
    )(*edge[:2], lead, uk, stay)
    edge_s = [lax.ppermute(e, "col", SWAP) for e in edge]
    inner, early, other = call(
        inner_kernel,
        [shape(1024, 256), shape(768, 256, dtype=F32), whole],
        [vm()] * 4 + [hbm()] * 2,
        [vm()] * 3,
        [pltpu.SemaphoreType.DMA((4,))],
        flops=939524096,
        nbytes=4 << 20,
    )(*edge, stay, got_early, got)
    slots = call(
        last_kernel,
        [shape(7, 32, 256)] * 4,
        [vm()] * 9 + [sm()],
        [vm()] * 4,
        [pltpu.VMEM((7, 128, 256), BF)],
        flops=805306368,
        nbytes=4 << 20,
    )(*edge, *edge_s, inner, early, other, weights)
    at_x = [slots[0]] + [lax.ppermute(slots[d], ("pole", "row"), pairs_xy(d)) for d in (2, 3, 1)]
    total = call(sum_kernel, [shape(7, 32, 256)], [vm()] * 8, [vm()], nbytes=1 << 20)(
        *at_x, *parts
    )[0]
    full = [total] + [lax.ppermute(total, "pole", pairs_x(d)) for d in (1, 3, 2)]
    return call(
        final_kernel, [shape(27, 32, 256, dtype=F32)], [vm()] * 4, [vm()], nbytes=2 << 20
    )(*full)[0]


def solution(mesh):
    return jax.shard_map(
        body,
        mesh=mesh,
        in_specs=(
            P("pole", None, None, "row", "col"),
            P("pole", None, None, "row", "col"),
            P("pole", None, None, "row", "col"),
            P("pole", None),
            P(),
            P(),
        ),
        out_specs=P(None, "row", "col"),
        check_vma=False,
    )
```

```python
import jax
import jax.numpy as jnp
from jax import lax
from jax.experimental import pallas as pl
from jax.experimental.pallas import tpu as pltpu
from jax.sharding import PartitionSpec as P

BF = jnp.bfloat16
F32 = jnp.float32
VMEM_LIMIT = 24 * 1024 * 1024


def ring_both(step):
    pairs = []
    for z in range(4):
        for y in range(4):
            here = (z * 4 + y) * 2
            pairs.append((here, (z * 4 + (y + step) % 4) * 2))
            pairs.append((here + 1, (((z + step) % 4) * 4 + y) * 2 + 1))
    return pairs


def ring_other(step):
    pairs = []
    for z in range(4):
        for y in range(4):
            here = (z * 4 + y) * 2
            pairs.append((here, (((z + step) % 4) * 4 + y) * 2))
            pairs.append((here + 1, (z * 4 + (y + step) % 4) * 2 + 1))
    return pairs


def pairs_x(step):
    return [(x, x ^ step) for x in range(4)]


def pairs_xy(step):
    return [
        (x * 16 + z * 4 + y, (x ^ (4 - step)) * 16 + z * 4 + (y ^ step))
        for x in range(4)
        for z in range(4)
        for y in range(4)
    ]


SWAP = [(0, 1), (1, 0)]


def place():
    row = lax.axis_index("row")
    return lax.axis_index("pole"), lax.div(row, 4), lax.rem(row, 4), lax.axis_index("col")


def index_of(x, y):
    return x ^ lax.rem(8 - y, 4)


def node_of(m):
    return 3 + 2 * lax.rem(m, 2) + lax.div(m, 2)


def vm():
    return pl.BlockSpec(memory_space=pltpu.VMEM)


def sm():
    return pl.BlockSpec(memory_space=pltpu.SMEM)


def in_hbm():
    return pl.BlockSpec(memory_space=pltpu.HBM)


def hbm():
    return pl.BlockSpec(memory_space=pl.ANY)


def call(kernel, outs, in_specs, out_specs, scratch=(), flops=0, nbytes=0, aliases={}):
    return pl.pallas_call(
        kernel,
        out_shape=outs,
        in_specs=in_specs,
        out_specs=out_specs,
        scratch_shapes=list(scratch),
        input_output_aliases=aliases,
        compiler_params=pltpu.CompilerParams(vmem_limit_bytes=VMEM_LIMIT),
        cost_estimate=pl.CostEstimate(flops=flops, bytes_accessed=nbytes, transcendentals=0),
    )


def shape(*dims, dtype=BF):
    return jax.ShapeDtypeStruct(dims, dtype)


def pack(low, up, dia, widths, pattern, outs, own):
    x, z, y, c = place()
    rows = (32 * (4 * z + y)) + lax.broadcasted_iota(jnp.int32, (32, 256), 0)
    cols = lax.broadcasted_iota(jnp.int32, (32, 256), 1)

    def mask(row_node, col_node, on, half):
        deep = jnp.where(on != 0, widths[row_node], 0)
        keep = (rows < deep) & (cols < widths[col_node] - 256 * half)
        return jnp.where(keep, 1.0, 0.0).astype(BF)[None]

    @pl.when(c == 0)
    def _():
        h = 0 if own else 1
        for d, out in enumerate(outs):
            k = node_of(index_of(x, lax.rem(y + d, 4)))
            p = lax.div(k - 1, 2)
            at = 2 * (k - 3) + 2
            out[0, h] = dia[p] * mask(p, p, jnp.int32(1), h)
            out[1, h] = low[at] * mask(p, k, pattern[at], h)
            out[2, h] = low[at + 1] * mask(0, k, pattern[at + 1], h)
            out[3, h] = up[at] * mask(k, p, pattern[at], h)
            out[4, h] = up[at + 1] * mask(k, 0, pattern[at + 1], h)

    @pl.when(c == 1)
    def _():
        h = 1 if own else 0
        tiles = [dia[0] * mask(0, 0, jnp.int32(1), h)]
        for i in range(2):
            tiles.append(up[i] * mask(1 + i, 0, pattern[i], h))
            tiles.append(low[i] * mask(0, 1 + i, pattern[i], h))
        for out in outs:
            for t in range(5):
                out[t, h] = tiles[t]


def pack_own_kernel(low_in, up_in, dia_in, widths_in, pattern_in, res_in, *refs):
    outs, parts, (widths, pattern, res, low, up, dia, sems) = refs[:4], refs[4:8], refs[8:]
    run_copies(
        [
            (low_in, low),
            (up_in, up),
            (dia_in, dia),
            (widths_in, widths),
            (pattern_in, pattern),
            (res_in, res),
        ],
        sems,
    )
    pack(low, up, dia, widths, pattern, outs, True)
    x, z, y, c = place()
    rows = (32 * (4 * z + y)) + lax.broadcasted_iota(jnp.int32, (32, 256), 0)
    cols = (256 * c) + lax.broadcasted_iota(jnp.int32, (32, 256), 1)
    for d, part in enumerate(parts):
        k = node_of(index_of(x ^ d, y))
        dens = res[0, 0] * dia[k, 0].astype(F32) - res[0, 1] * dia[k, 1].astype(F32)
        part[...] = jnp.where((rows < widths[k]) & (cols < widths[k]), dens, 0.0).astype(BF)


def pack_other_kernel(low, up, dia, widths, pattern, *refs):
    given, outs = refs[:4], refs[4:]
    for half in range(2):

        @pl.when(lax.axis_index("col") == half)
        def _():
            for before, out in zip(given, outs):
                out[:, half] = before[:, half]

    pack(low, up, dia, widths, pattern, outs, False)


def run_copies(copies, sems):
    made = [pltpu.make_async_copy(s, t, sems.at[i]) for i, (s, t) in enumerate(copies)]
    for m in made:
        m.start()
    for m in made:
        m.wait()


def merge_kernel(b0, b2, b3, b1, near, far, uk, sems):
    x, z, y, c = place()
    p = lax.rem(index_of(x, y), 2)

    @pl.when(c == 0)
    def _():
        copies = []
        for d, buf in enumerate((b0, b1, b2, b3)):
            at = lax.rem(y + 4 - d, 4)
            copies.append((buf.at[pl.ds(0, 3)], near.at[:, :, :, at]))
            copies.append((buf.at[pl.ds(0, 3)], far.at[:, :, :, at]))
            copies.append((buf.at[pl.ds(3, 2)], uk.at[:, :, :, at]))
        run_copies(copies, sems)

    @pl.when(c == 1)
    def _():
        copies = []
        for d, buf in enumerate((b0, b1, b2, b3)):
            at = lax.rem(z + 4 - d, 4)
            copies.append((buf.at[0], near.at[0, :, :, at]))
            copies.append((buf.at[0], far.at[0, :, :, at]))
            copies.append((buf.at[pl.ds(1 + 2 * p, 2)], far.at[pl.ds(1, 2), :, :, at]))
            copies.append((buf.at[pl.ds(3 - 2 * p, 2)], near.at[pl.ds(1, 2), :, :, at]))
        run_copies(copies, sems)


def left_of(pairs):
    real = [jnp.concatenate([r, -i], axis=1) for r, i in pairs]
    imag = [jnp.concatenate([i, r], axis=1) for r, i in pairs]
    return jnp.concatenate(real + imag, axis=0)


def dot(a, b):
    return jnp.dot(a, b, preferred_element_type=F32)


def pairs_of(res, count):
    half = 128 * count
    return [
        (res[128 * i : 128 * i + 128], res[half + 128 * i : half + 128 * i + 128])
        for i in range(count)
    ]


def wide_rows(get):
    return tuple(jnp.concatenate([get(0, part), get(1, part)], axis=1) for part in range(2))


def times(left, count, right):
    got = [pairs_of(dot(left, right[h].reshape(1024, 256)), count) for h in range(2)]
    return [
        tuple(jnp.concatenate([got[0][n][i], got[1][n][i]], axis=1) for i in range(2))
        for n in range(count)
    ]


def put(out, pair, sign=1):
    for i in range(2):
        out[i] = (pair[i] if sign > 0 else -pair[i]).astype(BF)


def early_kernel(r0, r2, p2, p3, p1, go, sems):
    x, z, y, c = place()
    part_of_last(((0, r0), (2, r2)), go, sems)


def part_of_last(given, go, sems):
    x, z, y, c = place()

    @pl.when(c == 0)
    def _():
        copies = []
        for d, buf in given:
            at = lax.div(lax.rem(z + 4 - d, 4), 2)
            copies.append((buf.at[pl.ds(1, 2), 1], go.at[:, :, at]))
        run_copies(copies, sems)

    @pl.when(c == 1)
    def _():
        copies = []
        for d, buf in given:
            at = lax.div(lax.rem(y + 4 - d, 4), 2)
            copies.append((buf.at[2], go.at[:, :, at]))
        run_copies(copies, sems)


def first_kernel(
    r0, r3, r2, r1, uks, before, out0, out1, out2, stay, go, lead, right, sems
):
    x, z, y, c = place()
    part_of_last(((1, r1), (3, r3)), go, sems)

    def rows_of(block):
        return wide_rows(lambda h, part: right[block, h, part, z].reshape(128, 256))

    @pl.when(c == 0)
    def _():
        copies = []
        for d, buf in enumerate((r0, r1, r2, r3)):
            at = lax.rem(z + 4 - d, 4)
            copies.append((buf.at[pl.ds(1, 2), 0], stay.at[:, :, at]))
            copies.append((buf.at[0], lead.at[:, :, at]))
        run_copies(copies, sems)

    @pl.when(c == 1)
    def _():
        copies = []
        for d, buf in enumerate((r0, r1, r2, r3)):
            at = lax.rem(y + 4 - d, 4)
            copies.append((buf.at[pl.ds(0, 2)], right.at[:, :, :, :, at]))
            copies.append((buf.at[2], stay.at[:, :, :, at]))
        run_copies(copies, sems)
        ukp = wide_rows(lambda h, part: uks[0, h, part].reshape(128, 256))
        uk0 = wide_rows(lambda h, part: uks[1, h, part].reshape(128, 256))
        (kv,) = times(left_of([ukp]), 1, right[1])
        v = tuple((uk0[i].astype(F32) - kv[i]).astype(BF) for i in range(2))
        xk0, xp0 = times(left_of([v, rows_of(1)]), 2, right[0])
        put(out0, xp0, -1)
        put(out1, rows_of(0))
        put(out2, xk0, -1)


def next_kernel(edge0, edge1, lead, uk, after, out0, out1):
    x, z, y, c = place()

    @pl.when(c == 0)
    def _():
        ukp = wide_rows(lambda h, part: uk[0, h, part].reshape(128, 256))
        (kd,) = times(left_of([ukp]), 1, lead)
        put(out0, kd)
        put(out1, wide_rows(lambda h, part: lead[h, part, z].reshape(128, 256)))

    @pl.when(c == 1)
    def _():
        out0[...] = edge0[...]
        out1[...] = edge1[...]


def inner_kernel(edge0, edge1, edge2, stay, got_a, got_b, out, early, other, sems):
    x, z, y, c = place()

    def work(last, own):
        lp = wide_rows(lambda h, part: last[h, part].reshape(512, 256))
        prod = dot(left_of([lp]), own[0].reshape(1024, 256))
        out[...] = (own[1].reshape(1024, 256).astype(F32) - prod).astype(BF)

    @pl.when(c == 0)
    def _():
        copies = []
        for buf, low in ((got_a, lax.rem(y, 2)), (got_b, 1 - lax.rem(y, 2))):
            for n in range(2):
                copies.append((buf.at[:, :, n], other.at[:, :, :, 2 * n + low]))
        run_copies(copies, sems)
        work(other, stay)
        left = left_of([(e[0], e[1]) for e in (edge0, edge1)])
        early[0:512] = dot(left, stay[0].reshape(1024, 256))

    @pl.when(c == 1)
    def _():
        copies = []
        for buf, low in ((got_a, lax.rem(z, 2)), (got_b, 1 - lax.rem(z, 2))):
            for n in range(2):
                copies.append((buf.at[:, :, n], other.at[:, :, 2 * n + low]))
        run_copies(copies, sems)
        work(stay, other)
        left = left_of([(e[0], e[1]) for e in (edge0, edge1, edge2)])
        early[...] = dot(left, stay[1].reshape(1024, 256))


def last_kernel(
    edge0, edge1, edge2, swap0, swap1, swap2, inner, early, got, res,
    slot0, slot1, slot2, slot3, parts,
):
    edge, edge_s = (edge0, edge1, edge2), (swap0, swap1, swap2)
    x, z, y, c = place()
    wr, wi = res[0, 0], res[0, 1]

    def density(re, im):
        return (wr * re.astype(F32) - wi * im.astype(F32)).astype(BF)

    def work(e0, e1, half):
        cols = slice(256 * half, 256 * half + 256)
        xp0, d0r, xk0 = [(e1[n][0], e1[n][1]) for n in range(3)]
        kd, dpr = [(e0[n][0], e0[n][1]) for n in range(2)]
        left = left_of([xp0, d0r, xk0])
        pg, og, kg = pairs_of(dot(left, inner[...]), 3)
        if half == 0:
            pe, oe, ke = pairs_of(dot(left, got[0].reshape(1024, 256)), 3)
            kl, pl_ = pairs_of(early[0:512], 2)
        else:
            pe, oe, ke = pairs_of(early[...], 3)
            kl, pl_ = pairs_of(dot(left_of([kd, dpr]), got[0].reshape(1024, 256)), 2)
        parts[0] = density(*[kl[i] - kg[i] for i in range(2)])
        parts[1] = density(*[-(pl_[i] + pg[i]) for i in range(2)])
        parts[2] = density(-og[0], -og[1])
        parts[3] = density(*[-(kd[i][:, cols].astype(F32) + ke[i]) for i in range(2)])
        parts[4] = density(xk0[0][:, cols], xk0[1][:, cols])

        @pl.when(index_of(x, y) < 2)
        def _():
            parts[5] = density(d0r[0][:, cols], d0r[1][:, cols])
            parts[6] = density(*[dpr[i][:, cols].astype(F32) - pe[i] for i in range(2)])

        @pl.when(index_of(x, y) >= 2)
        def _():
            parts[5] = density(xp0[0][:, cols], xp0[1][:, cols])
            parts[6] = density(-oe[0], -oe[1])

    @pl.when(c == 0)
    def _():
        work(edge, edge_s, 0)

    @pl.when(c == 1)
    def _():
        work(edge_s, edge, 1)

    for d, out in enumerate((slot0, slot1, slot2, slot3)):
        at = pl.multiple_of(32 * (y ^ d), 32)
        for b in range(7):
            out[b] = parts[b, pl.ds(at, 32), :]


def sum_kernel(a0, a1, a2, a3, d0, d1, d2, d3, out):
    total = a0[...].astype(F32) + a1[...].astype(F32)
    total = total + (a2[...].astype(F32) + a3[...].astype(F32))
    diag = d0[...].astype(F32) + d1[...].astype(F32) + d2[...].astype(F32) + d3[...].astype(F32)
    out[0] = (total[0] + diag).astype(BF)
    out[1:] = total[1:].astype(BF)


def final_kernel(g0, g1, g3, g2, out):
    x, z, y, c = place()
    for d, g in enumerate((g0, g1, g2, g3)):
        b = index_of(x ^ d, y)
        k = node_of(b)
        p = 1 + lax.rem(b, 2)
        pair = 2 * (k - 3) + 2
        low = b < 2
        out[k] = g[0].astype(F32)
        out[7 + pair] = g[1].astype(F32)
        out[8 + pair] = g[2].astype(F32)
        out[17 + pair] = g[3].astype(F32)
        out[18 + pair] = g[4].astype(F32)
        out[jnp.where(low, p, 6 + p)] = g[6].astype(F32)

        @pl.when(b != 1)
        def _():
            out[jnp.where(low, 0, 16 + p)] = g[5].astype(F32)


def body(lower_factor, upper_factor, diag_inverse, residues, widths, pattern):
    mine = (lower_factor[0], upper_factor[0], diag_inverse[0])
    swapped = [lax.ppermute(a, "col", SWAP) for a in mine]
    grid = ("row", "col")
    *bufs, widths, pattern, weights = call(
        pack_own_kernel,
        [shape(5, 2, 2, 32, 256)] * 4
        + [shape(32, 256)] * 4
        + [shape(7, dtype=jnp.int32), shape(10, dtype=jnp.int32), shape(1, 2, dtype=F32)],
        [in_hbm()] * 6,
        [vm()] * 8 + [sm()] * 3,
        [
            pltpu.VMEM((10, 2, 32, 256), BF),
            pltpu.VMEM((10, 2, 32, 256), BF),
            pltpu.VMEM((7, 2, 32, 256), BF),
            pltpu.SemaphoreType.DMA((6,)),
        ],
        nbytes=4 << 20,
    )(*[pltpu.with_memory_space_constraint(a, pltpu.HBM) for a in (*mine, widths, pattern, residues)])
    bufs, parts = bufs[:4], bufs[4:]
    bufs = call(
        pack_other_kernel,
        [shape(5, 2, 2, 32, 256)] * 4,
        [vm()] * 3 + [sm()] * 2 + [vm()] * 4,
        [vm()] * 4,
        nbytes=4 << 20,
        aliases={5: 0, 6: 1, 7: 2, 8: 3},
    )(*swapped, widths, pattern, *bufs)
    came = {d: lax.ppermute(bufs[d], grid, ring_both(d)) for d in (1, 3, 2)}
    parts = [parts[0]] + [lax.ppermute(parts[d], "pole", pairs_x(d)) for d in (2, 3, 1)]
    near, far, uk = call(
        merge_kernel,
        [shape(3, 2, 2, 4, 32, 256)] * 2 + [shape(2, 2, 2, 4, 32, 256)],
        [hbm()] * 4,
        [hbm()] * 3,
        [pltpu.SemaphoreType.DMA((16,))],
        nbytes=4 << 20,
    )(bufs[0], came[2], came[3], came[1])
    came = {d: lax.ppermute(near, grid, ring_other(d)) for d in (1, 3)}
    came[2] = lax.ppermute(far, grid, ring_other(2))
    uks = lax.ppermute(uk, "col", SWAP)
    blocks = (far, came[3], came[2], came[1])
    half = shape(2, 2, 2, 4, 32, 256)
    go = call(
        early_kernel,
        [half],
        [hbm()] * 5,
        [hbm()],
        [pltpu.SemaphoreType.DMA((2,))],
        nbytes=1 << 20,
    )(far, came[2], *parts[1:])[0]
    got_early = lax.ppermute(go, "col", SWAP)
    whole = shape(2, 2, 4, 4, 32, 256)
    slab = shape(2, 128, 512)
    *edge, stay, go, lead = call(
        first_kernel,
        [slab] * 3 + [whole, half, whole],
        [hbm()] * 4 + [vm()] + [hbm()],
        [vm()] * 3 + [hbm()] * 3,
        [pltpu.VMEM((2, 2, 2, 4, 4, 32, 256), BF), pltpu.SemaphoreType.DMA((8,))],
        flops=805306368,
        nbytes=4 << 20,
    )(*blocks, uks, got_early)
    got = lax.ppermute(go, "col", SWAP)
    edge[:2] = call(
        next_kernel,
        [slab] * 2,
        [vm()] * 4 + [hbm()],
        [vm()] * 2,
        flops=268435456,
        nbytes=2 << 20,
        aliases={0: 0, 1: 1},
    )(*edge[:2], lead, uk, stay)
    edge_s = [lax.ppermute(e, "col", SWAP) for e in edge]
    inner, early, other = call(
        inner_kernel,
        [shape(1024, 256), shape(768, 256, dtype=F32), whole],
        [vm()] * 4 + [hbm()] * 2,
        [vm()] * 3,
        [pltpu.SemaphoreType.DMA((4,))],
        flops=939524096,
        nbytes=4 << 20,
    )(*edge, stay, got_early, got)
    slots = call(
        last_kernel,
        [shape(7, 32, 256)] * 4,
        [vm()] * 9 + [sm()],
        [vm()] * 4,
        [pltpu.VMEM((7, 128, 256), BF)],
        flops=805306368,
        nbytes=4 << 20,
    )(*edge, *edge_s, inner, early, other, weights)
    at_x = [slots[0]] + [lax.ppermute(slots[d], ("pole", "row"), pairs_xy(d)) for d in (2, 3, 1)]
    total = call(sum_kernel, [shape(7, 32, 256)], [vm()] * 8, [vm()], nbytes=1 << 20)(
        *at_x, *parts
    )[0]
    full = [total] + [lax.ppermute(total, "pole", pairs_x(d)) for d in (1, 3, 2)]
    return call(
        final_kernel, [shape(27, 32, 256, dtype=F32)], [vm()] * 4, [vm()], nbytes=2 << 20
    )(*full)[0]


def solution(mesh):
    return jax.shard_map(
        body,
        mesh=mesh,
        in_specs=(
            P("pole", None, None, "row", "col"),
            P("pole", None, None, "row", "col"),
            P("pole", None, None, "row", "col"),
            P("pole", None),
            P(),
            P(),
        ),
        out_specs=P(None, "row", "col"),
        check_vma=False,
    )
```
